32 devices in a mesh: rep: 4 (over x, core), shard: 8 (over z, y).
Axes of the slice: x: 2, y: 2, z: 4, core: 2. Of those that a mesh axis runs over, the one named last changes fastest.
Arguments:
- token_ids: int32 [4096], P(('rep', 'shard')), may hold values from 0 to 49151
- target_ids: int32 [4096], P(('rep', 'shard')), may hold values from 0 to 49151
- loss_mask: int32 [4096], P(('rep', 'shard')), may hold values from 0 to 1
- table_master: float32 [49152, 960], P('shard'), may hold values from -1 to 1
- attn_in_master: float32 [1, 960, 1600], P(None, 'shard'), may hold values from -0.1875 to 0.1875
- attn_out_master: float32 [1, 960, 960], P(None, 'shard'), may hold values from -1.5 to 1.5
- mlp_in_master: float32 [1, 960, 5120], P(None, 'shard'), may hold values from -0.1875 to 0.1875
- mlp_out_master: float32 [1, 2560, 960], P(None, 'shard'), may hold values from -0.125 to 0.125
- gain_master: float32 [3, 960], P(None, 'shard'), may hold values from 0.5 to 2.1
- table_first: float32 [49152, 960], P('shard'), may hold values from -1 to 1
- attn_in_first: float32 [1, 960, 1600], P(None, 'shard'), may hold values from -1 to 1
- attn_out_first: float32 [1, 960, 960], P(None, 'shard'), may hold values from -1 to 1
- mlp_in_first: float32 [1, 960, 5120], P(None, 'shard'), may hold values from -1 to 1
- mlp_out_first: float32 [1, 2560, 960], P(None, 'shard'), may hold values from -1 to 1
- gain_first: float32 [3, 960], P(None, 'shard'), may hold values from -1 to 1
- table_second: float32 [49152, 960], P('shard'), may hold values from 0 to 1
- attn_in_second: float32 [1, 960, 1600], P(None, 'shard'), may hold values from 0 to 1
- attn_out_second: float32 [1, 960, 960], P(None, 'shard'), may hold values from 0 to 1
- mlp_in_second: float32 [1, 960, 5120], P(None, 'shard'), may hold values from 0 to 1
- mlp_out_second: float32 [1, 2560, 960], P(None, 'shard'), may hold values from 0 to 1
- gain_second: float32 [3, 960], P(None, 'shard'), may hold values from 0 to 1
Outputs:
- loss_sum: float32 [], replicated
- valid_count: float32 [], replicated
- grad_norm: float32 [], replicated
- table_new: float32 [49152, 960], P('shard')
- table_first_new: float32 [49152, 960], P('shard')
- table_second_new: float32 [49152, 960], P('shard')
- table_copy: bfloat16 [49152, 960], P('shard')
- attn_in_new: float32 [1, 960, 1600], P(None, 'shard')
- attn_in_first_new: float32 [1, 960, 1600], P(None, 'shard')
- attn_in_second_new: float32 [1, 960, 1600], P(None, 'shard')
- attn_in_copy: bfloat16 [1, 960, 1600], P(None, 'shard')
- attn_out_new: float32 [1, 960, 960], P(None, 'shard')
- attn_out_first_new: float32 [1, 960, 960], P(None, 'shard')
- attn_out_second_new: float32 [1, 960, 960], P(None, 'shard')
- attn_out_copy: bfloat16 [1, 960, 960], P(None, 'shard')
- mlp_in_new: float32 [1, 960, 5120], P(None, 'shard')
- mlp_in_first_new: float32 [1, 960, 5120], P(None, 'shard')
- mlp_in_second_new: float32 [1, 960, 5120], P(None, 'shard')
- mlp_in_copy: bfloat16 [1, 960, 5120], P(None, 'shard')
- mlp_out_new: float32 [1, 2560, 960], P(None, 'shard')
- mlp_out_first_new: float32 [1, 2560, 960], P(None, 'shard')
- mlp_out_second_new: float32 [1, 2560, 960], P(None, 'shard')
- mlp_out_copy: bfloat16 [1, 2560, 960], P(None, 'shard')
- gain_new: float32 [3, 960], P(None, 'shard')
- gain_first_new: float32 [3, 960], P(None, 'shard')
- gain_second_new: float32 [3, 960], P(None, 'shard')
- gain_copy: bfloat16 [3, 960], P(None, 'shard')
The draws below stay inside these ranges and needn't reach their ends.
All inputs are finite; a program needn't handle non-finite values.
Results may differ from the reference program's by a relative error of at most 0.01.
The reference program's roundings to bfloat16 on the way count: a program that leaves them out, or rounds other values in their place, can miss the bound.
Values may be sent and summed in bfloat16 or wider, within the bound.
No kernel may reach another device: no remote copies, remote signals or barrier semaphores. Data moves between devices by JAX's collectives and lax.ppermute only.
A program may use at most 576 MiB of HBM per device.

```python
import math
import jax
import jax.numpy as jnp
import numpy as np
from jax import lax

D = 960
HEADS = 15
KV_HEADS = 5
HEAD_DIM = 64
FF = 2560
V = 49152
LAYERS = 1
BLOCK = 256
STEP = 5
TOK_DEV = 128
SEQ = 1024
TOKENS = 4096
N_SHARD = 8


def grad_scale(factor):
    params_total = V * D + LAYERS * (D * (HEADS + 2 * KV_HEADS) * HEAD_DIM + HEADS * HEAD_DIM * D + 3 * D * FF) + (2 * LAYERS + 1) * D
    return factor * 0.01 / params_total ** 0.5


def first_moment(key, shape, factor):
    return grad_scale(factor) * jax.random.truncated_normal(key, -4.0, 4.0, shape, jnp.float32)


def second_moment(key, shape, factor):
    return grad_scale(factor) ** 2 * jnp.exp(jax.random.uniform(key, shape, jnp.float32, -0.6931472, 2.0794415))


def draw_loss_mask(key, part):
    key = jax.random.fold_in(key, 1)
    place = jnp.arange(TOKENS, dtype=jnp.int32)
    within = place % SEQ
    sequence = place // SEQ
    spread = max(1, TOKENS // SEQ - 1)
    limit = (250 + 625 * within // SEQ) * (spread + 2 * sequence) // (3 * spread)
    return (jax.random.randint(key, (TOKENS,), 0, 1000) < limit).astype(jnp.int32)


def draw_table_master(key, part):
    key = jax.random.fold_in(key, 2)
    ramp = jnp.arange(V, dtype=jnp.float32)[:, None] / V
    return (0.8 + 1.6 * ramp) * D ** (-0.5) * jax.random.truncated_normal(key, -3.0, 3.0, (V, D), jnp.float32)


def draw_gain_master(key, part):
    key = jax.random.fold_in(key, 3)
    ramp = jnp.arange(D, dtype=jnp.float32)[None, :] / D
    return (0.6 + 1.2 * ramp) * jax.random.uniform(key, (2 * LAYERS + 1, D), jnp.float32, 0.85, 1.15)


def draw_table_first(key, part):
    key = jax.random.fold_in(key, 11)
    return first_moment(key, (V, D), 0.5)


def draw_attn_in_first(key, part):
    key = jax.random.fold_in(key, 12)
    return first_moment(key, (LAYERS, D, (HEADS + 2 * KV_HEADS) * HEAD_DIM), 1.0)


def draw_attn_out_first(key, part):
    key = jax.random.fold_in(key, 13)
    return first_moment(key, (LAYERS, HEADS * HEAD_DIM, D), 1.0)


def draw_mlp_in_first(key, part):
    key = jax.random.fold_in(key, 14)
    return first_moment(key, (LAYERS, D, 2 * FF), 1.0)


def draw_mlp_out_first(key, part):
    key = jax.random.fold_in(key, 15)
    return first_moment(key, (LAYERS, FF, D), 1.0)


def draw_gain_first(key, part):
    key = jax.random.fold_in(key, 16)
    return first_moment(key, (2 * LAYERS + 1, D), 4.0)


def draw_table_second(key, part):
    key = jax.random.fold_in(key, 21)
    return second_moment(key, (V, D), 0.5)


def draw_attn_in_second(key, part):
    key = jax.random.fold_in(key, 22)
    return second_moment(key, (LAYERS, D, (HEADS + 2 * KV_HEADS) * HEAD_DIM), 1.0)


def draw_attn_out_second(key, part):
    key = jax.random.fold_in(key, 23)
    return second_moment(key, (LAYERS, HEADS * HEAD_DIM, D), 1.0)


def draw_mlp_in_second(key, part):
    key = jax.random.fold_in(key, 24)
    return second_moment(key, (LAYERS, D, 2 * FF), 1.0)


def draw_mlp_out_second(key, part):
    key = jax.random.fold_in(key, 25)
    return second_moment(key, (LAYERS, FF, D), 1.0)


def draw_gain_second(key, part):
    key = jax.random.fold_in(key, 26)
    return second_moment(key, (2 * LAYERS + 1, D), 4.0)


def touch_ends(result, key, smallest, high):
    spot = [jax.random.randint(jax.random.fold_in(key, axis), (), 0, length) for axis, length in enumerate(result.shape)]
    longest = result.shape.index(max(result.shape))
    neighbour = spot[:longest] + [(spot[longest] + 1) % result.shape[longest]] + spot[longest + 1:]
    return result.at[tuple(spot)].set(smallest).at[tuple(neighbour)].set(high)


def block_scale(own_key, extent, shards, smallest, largest):
    loudness = 1.0
    for position, blocks in shards:
        heights = jax.random.uniform(jax.random.fold_in(jax.random.fold_in(own_key, 6), position), (blocks,), jnp.float32, smallest / len(shards), largest / len(shards))
        loudness = loudness * jnp.repeat(jnp.exp(heights), extent[position] // blocks).reshape((-1,) + (1,) * (len(extent) - 1 - position))
    return loudness


def rank_bounds(number_of, slope):
    portions = [(1 << 20) // math.isqrt(grade ** slope) + 1 for grade in range(1, number_of + 1)]
    deviation = 1 + sum(portions) // (1 << 30)
    return np.cumsum(np.array([max(1, weight // deviation) for weight in portions]))


def ranked_ids(key, dims, count, skew):
    grid = rank_bounds(count, skew)
    lot = jax.random.randint(jax.random.fold_in(key, 1), dims, 0, int(grid[count - 1]))
    rank = jnp.searchsorted(jnp.asarray(grid, jnp.int32), lot, side="right")
    return jax.random.permutation(jax.random.fold_in(key, 2), count)[rank].astype(jnp.int32)


def normal_values(rng, shape, scale, most, split=(), held_as=jnp.bfloat16):
    factor_of = block_scale(rng, shape, split, -0.22, 0.18) if split else 1.0
    drawn = jax.random.normal(rng, shape, jnp.float32) * scale * factor_of
    return jnp.minimum(jnp.maximum(drawn, -most), most).astype(held_as)


def setup_inputs(seed: int = 0) -> dict:
    keys = jax.random.split(jax.random.key(seed), 22)
    token_ids = touch_ends(ranked_ids(keys[0], (TOKENS,), V, 2), jax.random.fold_in(keys[0], 3), 0, V - 1).astype(jnp.int32)
    target_ids = touch_ends(ranked_ids(keys[1], (TOKENS,), V, 2), jax.random.fold_in(keys[1], 3), 0, V - 1).astype(jnp.int32)
    loss_mask = draw_loss_mask(jax.random.fold_in(keys[21], 71), 0)
    table_master = draw_table_master(jax.random.fold_in(keys[21], 71), 0)
    attn_in_master = normal_values(keys[4], (LAYERS, D, (HEADS + 2 * KV_HEADS) * HEAD_DIM), D ** -0.5, 0.1875, ((1, 8),), jnp.float32)
    attn_out_master = normal_values(keys[5], (LAYERS, HEADS * HEAD_DIM, D), (max(1, HEADS * HEAD_DIM * 16 // SEQ)) ** -0.5, 1.5, ((1, 8),), jnp.float32)
    mlp_in_master = normal_values(keys[6], (LAYERS, D, 2 * FF), D ** -0.5, 0.1875, ((1, 8),), jnp.float32)
    mlp_out_master = normal_values(keys[7], (LAYERS, FF, D), FF ** -0.5, 0.125, ((1, 8),), jnp.float32)
    gain_master = draw_gain_master(jax.random.fold_in(keys[21], 71), 0)
    table_first = draw_table_first(jax.random.fold_in(keys[21], 71), 0)
    attn_in_first = draw_attn_in_first(jax.random.fold_in(keys[21], 71), 0)
    attn_out_first = draw_attn_out_first(jax.random.fold_in(keys[21], 71), 0)
    mlp_in_first = draw_mlp_in_first(jax.random.fold_in(keys[21], 71), 0)
    mlp_out_first = draw_mlp_out_first(jax.random.fold_in(keys[21], 71), 0)
    gain_first = draw_gain_first(jax.random.fold_in(keys[21], 71), 0)
    table_second = draw_table_second(jax.random.fold_in(keys[21], 71), 0)
    attn_in_second = draw_attn_in_second(jax.random.fold_in(keys[21], 71), 0)
    attn_out_second = draw_attn_out_second(jax.random.fold_in(keys[21], 71), 0)
    mlp_in_second = draw_mlp_in_second(jax.random.fold_in(keys[21], 71), 0)
    mlp_out_second = draw_mlp_out_second(jax.random.fold_in(keys[21], 71), 0)
    gain_second = draw_gain_second(jax.random.fold_in(keys[21], 71), 0)
    return dict(token_ids=token_ids, target_ids=target_ids, loss_mask=loss_mask, table_master=table_master, attn_in_master=attn_in_master, attn_out_master=attn_out_master, mlp_in_master=mlp_in_master, mlp_out_master=mlp_out_master, gain_master=gain_master, table_first=table_first, attn_in_first=attn_in_first, attn_out_first=attn_out_first, mlp_in_first=mlp_in_first, mlp_out_first=mlp_out_first, gain_first=gain_first, table_second=table_second, attn_in_second=attn_in_second, attn_out_second=attn_out_second, mlp_in_second=mlp_in_second, mlp_out_second=mlp_out_second, gain_second=gain_second)


EPS_NORM = 1e-05
ROPE_BASE = 100000.0
BETA_ONE = 0.5
BETA_TWO = 0.5
DECAY = 0.1
CLIP_AT = 0.01
ADAM_EPS = 1e-08
HIGHEST = lax.Precision.HIGHEST

@jax.custom_vjp
def low(v):
    return lax.optimization_barrier(v.astype(jnp.bfloat16)).astype(jnp.float32)

@jax.custom_vjp
def low_back(v):
    return v

def low_keep(v):
    return (low(v), None)

def low_pass(kept, grad):
    return (grad,)

def back_keep(v):
    return (v, None)

def back_low(kept, grad):
    return (low(grad),)
low.defvjp(low_keep, low_pass)
low_back.defvjp(back_keep, back_low)

def rms_norm(values, gain):
    return values * lax.rsqrt(lax.optimization_barrier(jnp.mean(values * values, axis=-1, keepdims=True)) + EPS_NORM) * gain

def rotate(values, positions):
    half_dim = values.shape[-1] // 2
    freqs = ROPE_BASE ** (-2.0 * jnp.arange(half_dim).astype(jnp.float32) / values.shape[-1])
    angles = positions.astype(jnp.float32)[:, None] * freqs[None, :]
    cosine = jnp.cos(angles)[:, None, :]
    sine = jnp.sin(angles)[:, None, :]
    first_half = values[..., :half_dim]
    second_half = values[..., half_dim:]
    return jnp.concatenate([first_half * cosine - second_half * sine, second_half * cosine + first_half * sine], axis=-1)

def rates(seq_len):
    out_fan = max(1, HEADS * HEAD_DIM * 16 // seq_len)
    return (0.8 * D ** (-0.5), 0.5 * D ** (-0.5), 0.5 * out_fan ** (-0.5), 0.5 * D ** (-0.5), 0.5 * FF ** (-0.5), 0.2)

def adam_update(master, first, second, gradient, rate):
    first_new = BETA_ONE * first + (1.0 - BETA_ONE) * gradient
    second_new = BETA_TWO * second + (1.0 - BETA_TWO) * gradient * gradient
    step_size = first_new / (1.0 - BETA_ONE ** STEP) / (jnp.sqrt(second_new / (1.0 - BETA_TWO ** STEP)) + ADAM_EPS)
    master_new = master - rate * (step_size + DECAY * master)
    return (master_new, first_new, second_new, master_new.astype(jnp.bfloat16))

def attend(queries, key_heads, value_heads):
    seq_len = queries.shape[0]
    row_block = min(512, seq_len)
    group = HEADS // KV_HEADS
    scale = HEAD_DIM ** (-0.5)
    key_blocks = jnp.arange(seq_len) // BLOCK

    def one_block(start):
        row_part = lax.dynamic_slice_in_dim(queries, start, row_block, 0).reshape(row_block, KV_HEADS, group, HEAD_DIM)
        scores = low_back(jnp.einsum('tkgd,skd->kgts', row_part, key_heads, precision=HIGHEST) * scale)
        query_blocks = (start + jnp.arange(row_block)) // BLOCK
        allowed = key_blocks[None, :] <= query_blocks[:, None]
        scores = jnp.where(allowed, scores, -1e+30)
        highest = lax.optimization_barrier(jnp.max(scores, axis=-1, keepdims=True))
        weights = jnp.exp(scores - highest)
        chances = low(weights / lax.optimization_barrier(jnp.sum(weights, axis=-1, keepdims=True)))
        output = jnp.einsum('kgts,skd->tkgd', chances, value_heads, precision=HIGHEST)
        return output.reshape(row_block, HEADS * HEAD_DIM)
    starts = (jnp.arange(seq_len // row_block) * row_block).astype(jnp.int32)
    return lax.map(jax.checkpoint(one_block), starts).reshape(seq_len, HEADS * HEAD_DIM)

def layer_forward(values, attn_in, attn_out, mlp_in, mlp_out, gain_one, gain_two, positions):
    query_width = HEADS * HEAD_DIM
    key_width = KV_HEADS * HEAD_DIM
    normed = low(rms_norm(values, gain_one))
    mixed = low_back(jnp.dot(normed, attn_in, precision=HIGHEST))
    queries = low(rotate(mixed[:, :query_width].reshape(-1, HEADS, HEAD_DIM), positions))
    key_heads = low(rotate(mixed[:, query_width:query_width + key_width].reshape(-1, KV_HEADS, HEAD_DIM), positions))
    value_heads = low(mixed[:, query_width + key_width:].reshape(-1, KV_HEADS, HEAD_DIM))
    attended = low_back(low(attend(queries, key_heads, value_heads)))
    middle = values + low_back(jnp.dot(attended, attn_out, precision=HIGHEST))
    normed_two = low(rms_norm(middle, gain_two))
    gate_up = low_back(jnp.dot(normed_two, mlp_in, precision=HIGHEST))
    hidden = low(jax.nn.silu(gate_up[:, :FF]) * gate_up[:, FF:])
    return middle + low_back(jnp.dot(hidden, mlp_out, precision=HIGHEST))

def head_loss(final, table, target_row, mask_row):
    seq_len = final.shape[0]
    row_block = min(512, seq_len)

    def one_block(start):
        state_rows = lax.dynamic_slice_in_dim(final, start, row_block, 0)
        target_part = lax.dynamic_slice_in_dim(target_row, start, row_block, 0)
        mask_part = lax.dynamic_slice_in_dim(mask_row, start, row_block, 0)
        logits = low_back(jnp.dot(state_rows, table.T, precision=HIGHEST))
        highest = lax.optimization_barrier(jnp.max(logits, axis=-1, keepdims=True))
        log_total = highest[:, 0] + jnp.log(lax.optimization_barrier(jnp.sum(jnp.exp(logits - highest), axis=-1)))
        picked = jnp.take_along_axis(logits, target_part[:, None], axis=-1)[:, 0]
        return jnp.sum((log_total - picked) * mask_part)
    starts = (jnp.arange(seq_len // row_block) * row_block).astype(jnp.int32)
    return jnp.sum(lax.map(jax.checkpoint(one_block), starts))

def forward(params, token_ids, target_ids, weight_mask):
    table, attn_in, attn_out, mlp_in, mlp_out, gains = [low(param) for param in params]
    seq_len = TOK_DEV * N_SHARD
    positions = jnp.arange(seq_len)

    def one_sequence(running, inputs):
        ids_row, target_row, mask_row = inputs
        values = low_back(table[ids_row])
        for layer_index in range(LAYERS):
            values = layer_forward(values, attn_in[layer_index], attn_out[layer_index], mlp_in[layer_index], mlp_out[layer_index], gains[2 * layer_index], gains[2 * layer_index + 1], positions)
        final = low(rms_norm(values, gains[2 * LAYERS]))
        return (running + head_loss(final, table, target_row, mask_row), None)
    running, _ = lax.scan(one_sequence, jnp.zeros((), jnp.float32), (token_ids.reshape(-1, seq_len), target_ids.reshape(-1, seq_len), weight_mask.reshape(-1, seq_len)))
    return running

def reference(token_ids, target_ids, loss_mask, table_master, attn_in_master, attn_out_master, mlp_in_master, mlp_out_master, gain_master, table_first, attn_in_first, attn_out_first, mlp_in_first, mlp_out_first, gain_first, table_second, attn_in_second, attn_out_second, mlp_in_second, mlp_out_second, gain_second):
    masters = (table_master, attn_in_master, attn_out_master, mlp_in_master, mlp_out_master, gain_master)
    firsts = (table_first, attn_in_first, attn_out_first, mlp_in_first, mlp_out_first, gain_first)
    seconds = (table_second, attn_in_second, attn_out_second, mlp_in_second, mlp_out_second, gain_second)
    weight_mask = loss_mask.astype(jnp.float32)
    valid_count = jnp.sum(weight_mask)
    loss_sum, pullback = jax.vjp(lambda params: forward(params, token_ids, target_ids, weight_mask), masters)
    gradients = pullback(1.0 / valid_count)[0]
    squares = jnp.zeros((), jnp.float32)
    for gradient in gradients:
        squares = squares + jnp.sum(gradient * gradient)
    grad_norm = jnp.sqrt(squares)
    clip_scale = CLIP_AT / jnp.maximum(grad_norm, CLIP_AT)
    results = [loss_sum, valid_count, grad_norm]
    rate_list = rates(TOK_DEV * N_SHARD)
    for member in range(6):
        results.extend(adam_update(masters[member], firsts[member], seconds[member], gradients[member] * clip_scale, rate_list[member]))
    return tuple(results)
```

```python
import jax
import jax.numpy as jnp
from jax import lax
from jax.sharding import PartitionSpec as P

D = 960
HEADS = 15
KV_HEADS = 5
HEAD_DIM = 64
FF = 2560
BLOCK = 256
STEP = 5
LINE = 4

EPS_NORM = 1e-05
ROPE_BASE = 100000.0
BETA_ONE = 0.5
BETA_TWO = 0.5
DECAY = 0.1
CLIP_AT = 0.01
ADAM_EPS = 1e-08

F32 = jnp.float32
BF16 = jnp.bfloat16
QUERY = HEADS * HEAD_DIM
KEY = KV_HEADS * HEAD_DIM


def rms_norm(values, gain):
    return values * lax.rsqrt(jnp.mean(values * values, axis=-1, keepdims=True) + EPS_NORM) * gain


def rotate(values, positions):
    half_dim = values.shape[-1] // 2
    freqs = ROPE_BASE ** (-2.0 * jnp.arange(half_dim).astype(F32) / values.shape[-1])
    angles = positions.astype(F32)[:, None] * freqs[None, :]
    cosine = jnp.cos(angles)[:, None, :]
    sine = jnp.sin(angles)[:, None, :]
    first_half = values[..., :half_dim]
    second_half = values[..., half_dim:]
    return jnp.concatenate(
        [first_half * cosine - second_half * sine, second_half * cosine + first_half * sine],
        axis=-1,
    )


def swiglu(gate, up):
    return jax.nn.silu(gate) * up


def rates(seq_len):
    out_fan = max(1, HEADS * HEAD_DIM * 16 // seq_len)
    return (
        0.8 * D ** (-0.5),
        0.5 * D ** (-0.5),
        0.5 * out_fan ** (-0.5),
        0.5 * D ** (-0.5),
        0.5 * FF ** (-0.5),
        0.2,
    )


def adam_update(master, first, second, gradient, rate):
    first_new = BETA_ONE * first + (1.0 - BETA_ONE) * gradient
    second_new = BETA_TWO * second + (1.0 - BETA_TWO) * gradient * gradient
    step_size = (
        first_new
        / (1.0 - BETA_ONE**STEP)
        / (jnp.sqrt(second_new / (1.0 - BETA_TWO**STEP)) + ADAM_EPS)
    )
    master_new = master - rate * (step_size + DECAY * master)
    return (master_new, first_new, second_new, master_new.astype(BF16))


def dot(a, b, dims=((1,), (0,))):
    return lax.dot_general(a, b, (dims, ((), ())), preferred_element_type=F32)


class Links:
    def __init__(self, n_shard, n_rep):
        self.n = n_shard
        self.wide = n_shard // LINE
        self.n_rep = n_rep
        me = lax.axis_index("shard")
        self.z = me // self.wide
        self.w = me % self.wide

    def along(self, value, step, low=0, high=LINE):
        pairs = [
            (z * self.wide + w, (z + step) * self.wide + w)
            for z in range(LINE)
            for w in range(self.wide)
            if 0 <= z + step < LINE and low <= z < high
        ]
        return lax.ppermute(value, "shard", pairs)

    def across(self, value, step):
        pairs = [
            (z * self.wide + w, z * self.wide + (w + step) % self.wide)
            for z in range(LINE)
            for w in range(self.wide)
        ]
        return lax.ppermute(value, "shard", pairs)

    def gather(self, value):
        rows = value.shape[0]
        z = self.z
        blocks = [(z, value)]
        up = [None, value]
        down = [None, value]
        up[1] = self.along(value, 1)
        down[1] = self.along(value, -1)
        for k in range(2, LINE):
            up.append(self.along(up[-1], 1, low=k - 1))
            down.append(self.along(down[-1], -1, high=LINE - k + 1))
        blocks.append((jnp.where(z == 0, 1, z - 1), jnp.where(z == 0, down[1], up[1])))
        blocks.append((jnp.where(z < 2, z + 2, z - 2), jnp.where(z < 2, down[2], up[2])))
        inner = (z == 1) | (z == 2)
        blocks.append(
            (
                jnp.where(inner, z + 1, jnp.where(z == 0, 3, 0)),
                jnp.where(inner, down[1], jnp.where(z == 0, down[3], up[3])),
            )
        )
        out = jnp.zeros((self.n * rows,) + value.shape[1:], value.dtype)
        zeros = (0,) * (value.ndim - 1)
        for source, block in blocks:
            out = lax.dynamic_update_slice(
                out, block, ((source * self.wide + self.w) * rows,) + zeros
            )
            for step in range(1, self.wide):
                other = self.across(block, step)
                place = source * self.wide + (self.w - step) % self.wide
                out = lax.dynamic_update_slice(out, other, (place * rows,) + zeros)
        return out

    def scatter(self, value):
        rows = value.shape[0] // self.n
        kind = value.dtype

        def block(z, w):
            return lax.dynamic_slice_in_dim(value, (z * self.wide + w) * rows, rows, 0)

        parts = [None] * LINE
        for k in (2, 1, 3, 0):
            target = (self.z + k) % LINE
            total = block(target, self.w).astype(F32)
            for step in range(1, self.wide):
                total = total + self.across(
                    block(target, (self.w + step) % self.wide), step
                ).astype(F32)
            parts[k] = total
        up = self.along(parts[3].astype(kind), 1, high=1).astype(F32)
        down = self.along(parts[1].astype(kind), -1, low=3).astype(F32)
        up = self.along((parts[2] + up).astype(kind), 1, high=2).astype(F32)
        down = self.along((parts[2] + down).astype(kind), -1, low=2).astype(F32)
        up = self.along((parts[1] + up).astype(kind), 1).astype(F32)
        down = self.along((parts[3] + down).astype(kind), -1).astype(F32)
        return parts[0] + up + down

    def spread(self, value):
        many = jnp.broadcast_to(value[None], (self.n,) + value.shape)
        return lax.all_to_all(many, "shard", 0, 0, tiled=True)

    def core(self, value):
        return lax.ppermute(value, "rep", [(r, r ^ 1) for r in range(self.n_rep)])

    def chip(self, value):
        return lax.ppermute(value, "rep", [(r, r ^ 2) for r in range(self.n_rep)])


def build(mesh):
    n_shard = mesh.shape["shard"]
    n_rep = mesh.shape["rep"]

    def local(
        token_ids,
        target_ids,
        loss_mask,
        table_master,
        attn_in_master,
        attn_out_master,
        mlp_in_master,
        mlp_out_master,
        gain_master,
        table_first,
        attn_in_first,
        attn_out_first,
        mlp_in_first,
        mlp_out_first,
        gain_first,
        table_second,
        attn_in_second,
        attn_out_second,
        mlp_in_second,
        mlp_out_second,
        gain_second,
    ):
        links = Links(n_shard, n_rep)
        my_rep = lax.axis_index("rep")
        my_shard = lax.axis_index("shard")
        second_core = (my_rep % 2) == 1
        tok_rows = token_ids.shape[0]
        seq_len = n_shard * tok_rows
        vocab_rows = table_master.shape[0]
        vocab_start = my_shard * vocab_rows
        positions = my_shard * tok_rows + jnp.arange(tok_rows, dtype=jnp.int32)

        def in_order(mine, other, axis=-1):
            return jnp.where(
                second_core,
                jnp.concatenate([other, mine], axis),
                jnp.concatenate([mine, other], axis),
            )

        def my_half(value, axis=-1):
            first, second = jnp.split(value, 2, axis)
            return jnp.where(second_core, second, first), jnp.where(second_core, first, second)

        packed = jnp.stack([token_ids, target_ids, loss_mask])
        reps = lax.all_gather(packed, "rep")
        everyone = links.spread(reps)
        all_ids = everyone[:, :, 0].transpose(1, 0, 2).reshape(-1)
        all_mask = everyone[:, :, 2].astype(F32)
        valid_count = jnp.sum(all_mask)
        group = lax.dynamic_index_in_dim(everyone, my_rep, 1, False)
        group_ids = group[:, 0].reshape(-1)
        group_targets = group[:, 1].reshape(-1)
        group_weights = group[:, 2].reshape(-1).astype(F32) / valid_count

        def halves(master):
            return my_half(master[0].astype(BF16))[0]

        attn_mine = links.gather(
            jnp.concatenate([halves(attn_in_master), halves(attn_out_master)], 1)
        )
        in_cols = attn_in_master.shape[2] // 2
        attn_other = links.core(attn_mine)
        attn_in = (attn_mine[:, :in_cols], attn_other[:, :in_cols])
        attn_out = (attn_mine[:, in_cols:], attn_other[:, in_cols:])
        gains = links.spread(gain_master.astype(BF16)).transpose(1, 0, 2).reshape(3, D).astype(F32)

        table_t = table_master.T.astype(BF16)
        vocab_iota = jnp.arange(vocab_rows, dtype=jnp.int32)
        pick = (group_ids[:, None] - vocab_start == vocab_iota[None, :]).astype(BF16)
        looked = dot(pick, table_t, ((1,), (1,))).astype(BF16)
        values = links.scatter(looked)

        mlp_in_mine = links.gather(halves(mlp_in_master))
        mlp_out_mine = links.gather(halves(mlp_out_master))
        mlp_in = (mlp_in_mine, links.core(mlp_in_mine))
        mlp_out = (mlp_out_mine, links.core(mlp_out_mine))

        def times(value, pair):
            return dot(value, pair[0]), dot(value, pair[1])

        def times_back(mine, other, pair):
            return dot(mine, pair[0], ((1,), (1,))) + dot(other, pair[1], ((1,), (1,)))

        normed_one, norm_one_back = jax.vjp(rms_norm, values, gains[0])
        normed_one = normed_one.astype(BF16)
        mixed = in_order(*times(normed_one, attn_in))
        heads_raw = mixed[:, : QUERY + KEY].reshape(tok_rows, HEADS + KV_HEADS, HEAD_DIM)
        rotated, rope_back = jax.vjp(lambda part: rotate(part, positions), heads_raw)
        rotated = rotated.astype(BF16)
        group_size = HEADS // KV_HEADS
        queries = rotated[:, :HEADS].reshape(tok_rows, KV_HEADS, group_size, HEAD_DIM)
        queries = queries.transpose(1, 2, 0, 3).reshape(KV_HEADS, group_size * tok_rows, HEAD_DIM)
        keys_values = jnp.concatenate(
            [rotated[:, HEADS:].reshape(tok_rows, KEY), mixed[:, QUERY + KEY :].astype(BF16)], 1
        )
        keys_values = links.gather(keys_values)
        keys_values = keys_values.reshape(seq_len, 2, KV_HEADS, HEAD_DIM).transpose(1, 2, 0, 3)
        keys, vals = keys_values[0], keys_values[1]
        scale = HEAD_DIM ** (-0.5)
        key_blocks = jnp.arange(seq_len, dtype=jnp.int32) // BLOCK
        query_blocks = jnp.tile(positions // BLOCK, group_size)
        allowed = (key_blocks[None, :] <= query_blocks[:, None])[None]

        def batched(spec, a, b):
            return jnp.einsum(spec, a, b, preferred_element_type=F32)

        scores = jnp.where(allowed, batched("htd,hsd->hts", queries, keys) * scale, -1e30)
        highest = jnp.max(scores, axis=-1, keepdims=True)
        weights = jnp.exp(scores - highest)
        totals = jnp.sum(weights, axis=-1, keepdims=True)
        chances = weights / totals
        chances_low = chances.astype(BF16)
        outputs = batched("hts,hsd->htd", chances_low, vals)

        def to_rows(heads):
            return (
                heads.reshape(KV_HEADS, group_size, tok_rows, HEAD_DIM)
                .transpose(2, 0, 1, 3)
                .reshape(tok_rows, QUERY)
            )

        attended = to_rows(outputs).astype(BF16)
        middle = values + in_order(*times(attended, attn_out))
        normed_two, norm_two_back = jax.vjp(rms_norm, middle, gains[1])
        normed_two = normed_two.astype(BF16)
        part_mine, part_other = times(normed_two, mlp_in)
        gate = jnp.where(second_core, part_other, part_mine)
        up = jnp.where(second_core, part_mine, part_other)
        hidden, glu_back = jax.vjp(swiglu, gate, up)
        hidden = hidden.astype(BF16)
        result = middle + in_order(*times(hidden, mlp_out))
        final, final_back = jax.vjp(rms_norm, result, gains[2])

        states = links.gather(final.astype(BF16))
        logits = dot(states, table_t)
        local_targets = group_targets - vocab_start
        hit = local_targets[:, None] == vocab_iota[None, :]
        high = jnp.max(logits, axis=-1)
        raised = jnp.exp(logits - high[:, None])
        stats = jnp.stack(
            [high, jnp.sum(raised, axis=-1), jnp.sum(jnp.where(hit, logits, 0.0), axis=-1)]
        )
        stats = links.spread(stats)
        top = jnp.max(stats[:, 0], axis=0)
        log_totals = top + jnp.log(jnp.sum(stats[:, 1] * jnp.exp(stats[:, 0] - top), axis=0))
        picked = jnp.sum(stats[:, 2], axis=0)
        group_loss = jnp.sum((log_totals - picked) * group[:, 2].reshape(-1).astype(F32))
        grad_logits = (
            (jnp.exp(logits - log_totals[:, None]) - jnp.where(hit, 1.0, 0.0))
            * group_weights[:, None]
        ).astype(BF16)
        grad_states = dot(grad_logits, table_t, ((1,), (1,))).astype(BF16)
        grad_final = links.scatter(grad_states)

        table_grad = dot(states, grad_logits, ((0,), (0,))).astype(BF16)
        grad_mine, grad_other = my_half(table_grad)
        chip_sum = (grad_mine.astype(F32) + links.core(grad_other).astype(F32)).astype(BF16)
        half_sum = (chip_sum.astype(F32) + links.chip(chip_sum).astype(F32)).astype(BF16)
        table_sum = in_order(half_sum, links.core(half_sum)).astype(F32)

        grad_output, grad_gain_three = final_back(grad_final)

        def weight_grad(value, mine, other):
            sent = dot(value, other, ((0,), (0,))).astype(BF16)
            return (dot(value, mine, ((0,), (0,))) + links.core(sent).astype(F32)).astype(BF16)

        def owned(part):
            part = links.scatter(part).astype(BF16)
            part = part.astype(F32) + links.chip(part).astype(F32)
            return part, links.core(part)

        branch_mine, branch_other = my_half(grad_output.astype(BF16))
        grad_mlp_out = weight_grad(hidden, branch_mine, branch_other)
        grad_hidden = times_back(branch_mine, branch_other, mlp_out)
        grad_gate, grad_up = glu_back(grad_hidden)
        grad_gate = grad_gate.astype(BF16)
        grad_up = grad_up.astype(BF16)
        glu_mine = jnp.where(second_core, grad_up, grad_gate)
        glu_other = jnp.where(second_core, grad_gate, grad_up)
        grad_mlp_in = weight_grad(normed_two, glu_mine, glu_other)
        middle_part, grad_gain_two = norm_two_back(times_back(glu_mine, glu_other, mlp_in))
        grad_middle = grad_output + middle_part
        mlp_out_sum = in_order(*owned(grad_mlp_out))
        mlp_in_sum = in_order(*owned(grad_mlp_in))

        out_mine, out_other = my_half(grad_middle.astype(BF16))
        grad_attn_out = weight_grad(attended, out_mine, out_other)
        grad_attended = times_back(out_mine, out_other, attn_out).astype(BF16)
        grad_heads = (
            grad_attended.reshape(tok_rows, KV_HEADS, group_size, HEAD_DIM)
            .transpose(1, 2, 0, 3)
            .reshape(KV_HEADS, group_size * tok_rows, HEAD_DIM)
        )
        deltas = jnp.sum(grad_heads.astype(F32) * outputs, axis=-1, keepdims=True)
        grad_chances = batched("htd,hsd->hts", grad_heads, vals)
        grad_scores = (chances * (grad_chances - deltas)).astype(BF16)
        grad_queries = batched("hts,hsd->htd", grad_scores, keys) * scale
        grad_keys = batched("hts,htd->hsd", grad_scores, queries) * scale
        grad_vals = batched("hts,htd->hsd", chances_low, grad_heads)
        grad_kv = jnp.stack([grad_keys, grad_vals]).transpose(2, 0, 1, 3).reshape(seq_len, 2 * KEY)
        grad_kv = links.scatter(grad_kv.astype(BF16))
        grad_rotated = jnp.concatenate(
            [
                to_rows(grad_queries).reshape(tok_rows, HEADS, HEAD_DIM),
                grad_kv[:, :KEY].reshape(tok_rows, KV_HEADS, HEAD_DIM),
            ],
            1,
        )
        grad_raw = rope_back(grad_rotated)[0].reshape(tok_rows, QUERY + KEY)
        grad_mixed = jnp.concatenate([grad_raw, grad_kv[:, KEY:]], 1).astype(BF16)
        mixed_mine, mixed_other = my_half(grad_mixed)
        values_part, grad_gain_one = norm_one_back(times_back(mixed_mine, mixed_other, attn_in))
        grad_values = (grad_middle + values_part).astype(BF16)
        grad_attn_in = weight_grad(normed_one, mixed_mine, mixed_other)
        grad_gains = jnp.stack([grad_gain_one, grad_gain_two, grad_gain_three], 1)
        grad_gains = grad_gains + links.core(grad_gains)
        small = jnp.concatenate([grad_attn_in, grad_attn_out, grad_gains.astype(BF16)], 1)
        small_mine, small_other = owned(small)
        attn_in_sum = in_order(small_mine[:, :in_cols], small_other[:, :in_cols])
        out_end = in_cols + D // 2
        attn_out_sum = in_order(small_mine[:, in_cols:out_end], small_other[:, in_cols:out_end])
        gain_sum = small_mine[:, out_end:].T

        embedded = lax.all_gather(grad_values, "rep").transpose(1, 0, 2).reshape(tok_rows, -1)
        embedded = links.gather(embedded).reshape(seq_len, n_rep, D).transpose(1, 0, 2)
        embedded = embedded.reshape(n_rep * seq_len, D)
        place = (all_ids[:, None] - vocab_start == vocab_iota[None, :]).astype(BF16)
        table_sum = table_sum + dot(embedded, place, ((0,), (0,)))

        sums = (
            table_sum,
            attn_in_sum[None],
            attn_out_sum[None],
            mlp_in_sum[None],
            mlp_out_sum[None],
            gain_sum,
        )
        squares = jnp.zeros((), F32)
        for gradient in sums:
            squares = squares + jnp.sum(gradient * gradient)
        loss = group_loss + links.core(group_loss)
        loss_sum = loss + links.chip(loss)
        squares = jnp.sum(links.spread(jnp.full((8, 128), squares))[:, 0, 0])
        grad_norm = jnp.sqrt(squares)
        clip_scale = CLIP_AT / jnp.maximum(grad_norm, CLIP_AT)
        results = [loss_sum, valid_count, grad_norm]
        masters = (
            table_master.T,
            attn_in_master,
            attn_out_master,
            mlp_in_master,
            mlp_out_master,
            gain_master,
        )
        firsts = (
            table_first.T,
            attn_in_first,
            attn_out_first,
            mlp_in_first,
            mlp_out_first,
            gain_first,
        )
        seconds = (
            table_second.T,
            attn_in_second,
            attn_out_second,
            mlp_in_second,
            mlp_out_second,
            gain_second,
        )
        rate_list = rates(seq_len)
        for member in range(6):
            new = adam_update(
                masters[member],
                firsts[member],
                seconds[member],
                sums[member] * clip_scale,
                rate_list[member],
            )
            if member == 0:
                new = tuple(part.T for part in new)
            results.extend(new)
        return tuple(results)

    return local


def solution(mesh):
    token = P(("rep", "shard"))
    weight = P(None, "shard", None)
    state = (P("shard", None), weight, weight, weight, weight, P(None, "shard"))
    outs = [P(), P(), P()]
    for spec in state:
        outs.extend([spec] * 4)
    return jax.shard_map(
        build(mesh),
        mesh=mesh,
        in_specs=(token, token, token) + state * 3,
        out_specs=tuple(outs),
        check_vma=False,
    )
```

```python
import functools

import jax
import jax.numpy as jnp
from jax import lax
from jax.experimental import pallas as pl
from jax.experimental.pallas import tpu as pltpu
from jax.sharding import PartitionSpec as P

D = 960
HEADS = 15
KV_HEADS = 5
HEAD_DIM = 64
FF = 2560
BLOCK = 256
STEP = 5
LINE = 4

EPS_NORM = 1e-05
ROPE_BASE = 100000.0
BETA_ONE = 0.5
BETA_TWO = 0.5
DECAY = 0.1
CLIP_AT = 0.01
ADAM_EPS = 1e-08

F32 = jnp.float32
BF16 = jnp.bfloat16
QUERY = HEADS * HEAD_DIM
KEY = KV_HEADS * HEAD_DIM
VMEM = 56 * 1024 * 1024


def rms_norm(values, gain):
    return values * lax.rsqrt(jnp.mean(values * values, axis=-1, keepdims=True) + EPS_NORM) * gain


def rotate(values, positions):
    half_dim = values.shape[-1] // 2
    freqs = ROPE_BASE ** (-2.0 * jnp.arange(half_dim).astype(F32) / values.shape[-1])
    angles = positions.astype(F32)[:, None] * freqs[None, :]
    cosine = jnp.cos(angles)[:, None, :]
    sine = jnp.sin(angles)[:, None, :]
    first_half = values[..., :half_dim]
    second_half = values[..., half_dim:]
    return jnp.concatenate(
        [first_half * cosine - second_half * sine, second_half * cosine + first_half * sine],
        axis=-1,
    )


def swiglu(gate, up):
    return jax.nn.silu(gate) * up


def rates(seq_len):
    out_fan = max(1, HEADS * HEAD_DIM * 16 // seq_len)
    return (
        0.8 * D ** (-0.5),
        0.5 * D ** (-0.5),
        0.5 * out_fan ** (-0.5),
        0.5 * D ** (-0.5),
        0.5 * FF ** (-0.5),
        0.2,
    )


def adam_update(master, first, second, gradient, rate):
    first_new = BETA_ONE * first + (1.0 - BETA_ONE) * gradient
    second_new = BETA_TWO * second + (1.0 - BETA_TWO) * gradient * gradient
    step_size = (
        first_new
        / (1.0 - BETA_ONE**STEP)
        / (jnp.sqrt(second_new / (1.0 - BETA_TWO**STEP)) + ADAM_EPS)
    )
    master_new = master - rate * (step_size + DECAY * master)
    return (master_new, first_new, second_new, master_new.astype(BF16))


def dot(a, b, dims=((1,), (0,))):
    return lax.dot_general(a, b, (dims, ((), ())), preferred_element_type=F32)


def params():
    return pltpu.CompilerParams(vmem_limit_bytes=VMEM)


def whole(shape):
    return pl.BlockSpec(shape, lambda *_: (0,) * len(shape), pipeline_mode=pl.Buffered(1))


def lookup_kernel(ids_ref, table_ref, low_ref, rows_ref, total):
    tile = table_ref.shape[1]
    step = pl.program_id(0)
    low = table_ref[...].astype(BF16)
    low_ref[...] = low
    columns = lax.broadcasted_iota(jnp.int32, (1, tile), 1) + step * tile
    block = min(512, rows_ref.shape[0])
    for start in range(0, rows_ref.shape[0], block):
        rows = pl.ds(start, block)
        pick = jnp.where(ids_ref[rows, :] == columns, 1.0, 0.0).astype(BF16)
        found = dot(pick, low, ((1,), (1,)))

        @pl.when(step == 0)
        def _():
            total[rows, :] = found

        @pl.when(step > 0)
        def _():
            total[rows, :] += found

    @pl.when(step == pl.num_programs(0) - 1)
    def _():
        rows_ref[...] = total[...].astype(BF16)


def lookup(table_t, local_ids, tile=512):
    width, vocab = table_t.shape
    count = local_ids.shape[0]
    return pl.pallas_call(
        lookup_kernel,
        grid=(vocab // tile,),
        in_specs=[
            whole((count, 1)),
            pl.BlockSpec((width, tile), lambda i: (0, i)),
        ],
        out_specs=[
            pl.BlockSpec((width, tile), lambda i: (0, i)),
            whole((count, width)),
        ],
        out_shape=[
            jax.ShapeDtypeStruct((width, vocab), BF16),
            jax.ShapeDtypeStruct((count, width), BF16),
        ],
        scratch_shapes=[pltpu.VMEM((count, width), F32)],
        compiler_params=params(),
        cost_estimate=pl.CostEstimate(
            flops=2 * count * width * vocab, bytes_accessed=6 * width * vocab, transcendentals=0
        ),
    )(local_ids[:, None], table_t)


def logits_kernel(states_ref, targets_ref, table_ref, raised_ref, stats_ref, logits, *, tile):
    vocab = table_ref.shape[1]
    rows = states_ref.shape[0]
    states = states_ref[...]
    high = jnp.full((rows, 1), -jnp.inf, F32)
    for start in range(0, vocab, tile):
        part = dot(states, table_ref[:, start : start + tile])
        logits[:, start : start + tile] = part
        high = jnp.maximum(high, jnp.max(part, axis=-1, keepdims=True))
    total = jnp.zeros((rows, 128), F32)
    picked = jnp.zeros((rows, 128), F32)
    targets = targets_ref[...]
    lanes = lax.broadcasted_iota(jnp.int32, (1, 128), 1)
    for start in range(0, vocab, 128):
        part = logits[:, start : start + 128]
        raised = jnp.exp(part - high)
        raised_ref[:, start : start + 128] = raised.astype(BF16)
        total += raised
        picked += jnp.where(targets == lanes + start, part, 0.0)
    total = jnp.sum(total, axis=-1, keepdims=True)
    picked = jnp.sum(picked, axis=-1, keepdims=True)
    stats_ref[...] = jnp.where(lanes == 0, high, jnp.where(lanes == 1, total, picked))


def head_logits(states, targets, table_low, rows=256, tile=512):
    count, width = states.shape
    vocab = table_low.shape[1]
    return pl.pallas_call(
        functools.partial(logits_kernel, tile=tile),
        grid=(count // rows,),
        in_specs=[
            pl.BlockSpec((rows, width), lambda i: (i, 0)),
            pl.BlockSpec((rows, 1), lambda i: (i, 0)),
            whole((width, vocab)),
        ],
        out_specs=[
            pl.BlockSpec((rows, vocab), lambda i: (i, 0)),
            pl.BlockSpec((rows, 128), lambda i: (i, 0)),
        ],
        out_shape=[
            jax.ShapeDtypeStruct((count, vocab), BF16),
            jax.ShapeDtypeStruct((count, 128), F32),
        ],
        scratch_shapes=[pltpu.VMEM((rows, vocab), F32)],
        compiler_params=params(),
        cost_estimate=pl.CostEstimate(
            flops=2 * count * width * vocab,
            bytes_accessed=2 * vocab * (width + count),
            transcendentals=count * vocab,
        ),
    )(states, targets[:, None], table_low)


def states_kernel(raised_ref, scales_ref, targets_ref, table_ref, grads_ref, out_ref, *, tile):
    vocab = table_ref.shape[1]
    weight = scales_ref[:, 1:2]
    factor = scales_ref[:, 0:1]
    targets = targets_ref[...]
    total = None
    for start in range(0, vocab, tile):
        lanes = lax.broadcasted_iota(jnp.int32, (1, tile), 1) + start
        chances = raised_ref[:, start : start + tile].astype(F32) * factor
        part = (jnp.where(targets == lanes, chances - weight, chances)).astype(BF16)
        grads_ref[:, start : start + tile] = part
        found = dot(part, table_ref[:, start : start + tile], ((1,), (1,)))
        total = found if total is None else total + found
    out_ref[...] = total.astype(BF16)


def head_states(raised, factors, weights, targets, table_low, rows=256, tile=512):
    count, vocab = raised.shape
    width = table_low.shape[0]
    scales = jnp.stack([factors * weights, weights], axis=1)
    return pl.pallas_call(
        functools.partial(states_kernel, tile=tile),
        grid=(count // rows,),
        in_specs=[
            pl.BlockSpec((rows, vocab), lambda i: (i, 0)),
            pl.BlockSpec((rows, 2), lambda i: (i, 0)),
            pl.BlockSpec((rows, 1), lambda i: (i, 0)),
            whole((width, vocab)),
        ],
        out_specs=[
            pl.BlockSpec((rows, vocab), lambda i: (i, 0)),
            pl.BlockSpec((rows, width), lambda i: (i, 0)),
        ],
        out_shape=[
            jax.ShapeDtypeStruct((count, vocab), BF16),
            jax.ShapeDtypeStruct((count, width), BF16),
        ],
        compiler_params=params(),
        cost_estimate=pl.CostEstimate(
            flops=2 * count * width * vocab,
            bytes_accessed=2 * vocab * (width + 2 * count),
            transcendentals=0,
        ),
    )(raised, scales, targets[:, None], table_low)


def table_kernel(half_ref, states_ref, grads_ref, out_ref):
    out_ref[...] = dot(states_ref[...], grads_ref[...]).astype(BF16)


def head_table(states_t, grads, half, tile=512):
    width, count = states_t.shape
    vocab = grads.shape[1] // 2
    tile = min(tile, vocab)
    steps = vocab // tile
    return pl.pallas_call(
        table_kernel,
        grid_spec=pltpu.PrefetchScalarGridSpec(
            num_scalar_prefetch=1,
            grid=(steps,),
            in_specs=[
                whole((width, count)),
                pl.BlockSpec((count, tile), lambda i, half: (0, half[0] * steps + i)),
            ],
            out_specs=pl.BlockSpec((width, tile), lambda i, half: (0, i)),
        ),
        out_shape=jax.ShapeDtypeStruct((width, vocab), BF16),
        compiler_params=params(),
        cost_estimate=pl.CostEstimate(
            flops=2 * count * width * vocab,
            bytes_accessed=2 * (vocab * (width + count) + width * count),
            transcendentals=0,
        ),
    )(jnp.reshape(half, (1,)).astype(jnp.int32), states_t, grads)


def place_kernel(
    starts_ref,
    half_ref,
    ranks_ref,
    ids_ref,
    rows_ref,
    mine_ref,
    other_ref,
    out_ref,
    square_ref,
    sorted_rows,
    *,
    chunk,
    block,
):
    step = pl.program_id(0)
    steps = pl.num_programs(0)
    tile = out_ref.shape[1]
    pieces, _, lanes = rows_ref.shape

    @pl.when(step == 0)
    def _():
        def sort(k, carry):
            columns = pl.ds(pl.multiple_of(k * block, block), block)
            wanted = lax.broadcasted_iota(jnp.int32, (1, block), 1) + k * block
            total = None
            for piece in range(0, min(pieces, 32), 2):
                total = sort_pair(piece, wanted, total)
            if pieces > 32:
                total = lax.fori_loop(
                    16, pieces // 2, lambda p, t: sort_pair(2 * p, wanted, t), total
                )
            sorted_rows[:, columns] = total.astype(BF16)
            return carry

        def sort_pair(piece, wanted, total):
            start = piece * lanes
            if not isinstance(piece, int):
                start = pl.multiple_of(start, 2 * lanes)
            pick = jnp.where(ranks_ref[pl.ds(start, 2 * lanes), :] == wanted, 1.0, 0.0)
            pair = jnp.concatenate([rows_ref[piece], rows_ref[piece + 1]], axis=1)
            found = dot(pair, pick.astype(BF16))
            return found if total is None else total + found

        lax.fori_loop(0, (starts_ref[steps] + block - 1) // block, sort, 0)

    first = starts_ref[step]
    last = starts_ref[step + 1]
    is_mine = (step * 2 >= steps) == (half_ref[0] == 1)

    @pl.when(is_mine)
    def _():
        out_ref[...] = mine_ref[...].astype(F32)

    @pl.when(jnp.logical_not(is_mine))
    def _():
        out_ref[...] = other_ref[...].astype(F32)

    columns = lax.broadcasted_iota(jnp.int32, (1, tile), 1) + step * tile

    def add(k, carry):
        rows = pl.ds(pl.multiple_of(k * chunk, chunk), chunk)
        place = lax.broadcasted_iota(jnp.int32, (chunk, 1), 0) + k * chunk
        ids = ids_ref[rows, :]
        inside = jnp.logical_and(place >= first, place < last)
        pick = jnp.where(jnp.logical_and(ids == columns, inside), 1.0, 0.0).astype(BF16)
        out_ref[...] += dot(sorted_rows[:, rows], pick)
        return carry

    lax.fori_loop(first // chunk, (last + chunk - 1) // chunk, add, 0)
    value = out_ref[...]
    squares = jnp.sum(value * value, axis=0, keepdims=True)
    part = jnp.zeros((1, 128), F32)
    for start in range(0, tile, 128):
        part += squares[:, start : start + 128]

    @pl.when(step == 0)
    def _():
        square_ref[...] = part

    @pl.when(step > 0)
    def _():
        square_ref[...] += part


def place_rows(mine, other, half, rows, ranks, ids, starts, tile, chunk=128, block=512):
    width, half_vocab = mine.shape
    pieces, _, lanes = rows.shape
    total = pieces * lanes
    steps = 2 * half_vocab // tile
    halves = steps // 2

    def half_map(wanted):
        def index(i, starts, half):
            low = jnp.where(half[0] == wanted, 0, halves)
            return (0, jnp.clip(i - low, 0, halves - 1))

        return index

    return pl.pallas_call(
        functools.partial(place_kernel, chunk=chunk, block=block),
        grid_spec=pltpu.PrefetchScalarGridSpec(
            num_scalar_prefetch=2,
            grid=(steps,),
            in_specs=[
                whole((total, 1)),
                whole((total, 1)),
                whole((pieces, width, lanes)),
                pl.BlockSpec((width, tile), half_map(0)),
                pl.BlockSpec((width, tile), half_map(1)),
            ],
            out_specs=[
                pl.BlockSpec((width, tile), lambda i, starts, half: (0, i)),
                whole((1, 128)),
            ],
            scratch_shapes=[pltpu.VMEM((width, total), BF16)],
        ),
        out_shape=[
            jax.ShapeDtypeStruct((width, 2 * half_vocab), F32),
            jax.ShapeDtypeStruct((1, 128), F32),
        ],
        compiler_params=params(),
        cost_estimate=pl.CostEstimate(
            flops=2 * 16 * chunk * tile * width,
            bytes_accessed=12 * width * half_vocab + 2 * total * width,
            transcendentals=0,
        ),
    )(
        starts,
        jnp.reshape(half, (1,)).astype(jnp.int32),
        ranks[:, None],
        ids[:, None],
        rows,
        mine,
        other,
    )


def adam_kernel(scale_ref, w_ref, m_ref, v_ref, g_ref, wn_ref, mn_ref, vn_ref, low_ref, *, rate):
    new = adam_update(
        w_ref[...], m_ref[...], v_ref[...], g_ref[...] * scale_ref[0], rate
    )
    wn_ref[...], mn_ref[...], vn_ref[...], low_ref[...] = new


def adam(master, first, second, gradient, scale, rate, tile):
    rows, columns = master.shape
    spec = pl.BlockSpec((rows, tile), lambda i: (0, i))
    shape = jax.ShapeDtypeStruct((rows, columns), F32)
    return pl.pallas_call(
        functools.partial(adam_kernel, rate=rate),
        grid=(columns // tile,),
        in_specs=[pl.BlockSpec(memory_space=pltpu.SMEM)] + [spec] * 4,
        out_specs=[spec] * 4,
        out_shape=[shape] * 3 + [jax.ShapeDtypeStruct((rows, columns), BF16)],
        compiler_params=params(),
        cost_estimate=pl.CostEstimate(
            flops=20 * rows * columns, bytes_accessed=30 * rows * columns, transcendentals=0
        ),
    )(jnp.reshape(scale, (1,)), master, first, second, gradient)


def place_tokens(mine, other, half, rows, ranks, ids, starts, tile):
    pieces, width, lanes = rows.shape
    if pieces * lanes <= 4096:
        return place_rows(mine, other, half, rows, ranks, ids, starts, tile)
    total = jnp.where(
        half == 1, jnp.concatenate([other, mine], 1), jnp.concatenate([mine, other], 1)
    ).astype(F32)
    tokens_ids = jnp.take(ids, ranks).reshape(pieces, lanes)
    columns = jnp.arange(total.shape[1], dtype=jnp.int32)

    def add(total, operands):
        part, part_ids = operands
        pick = (part_ids[:, None] == columns[None, :]).astype(BF16)
        return total + dot(part, pick), None

    total, _ = lax.scan(add, total, (rows, tokens_ids))
    return total, jnp.sum(total * total)


class Links:
    def __init__(self, n_shard, n_rep):
        self.n = n_shard
        self.wide = n_shard // LINE
        self.n_rep = n_rep
        me = lax.axis_index("shard")
        self.z = me // self.wide
        self.w = me % self.wide

    def along(self, value, step, low=0, high=LINE):
        pairs = [
            (z * self.wide + w, (z + step) * self.wide + w)
            for z in range(LINE)
            for w in range(self.wide)
            if 0 <= z + step < LINE and low <= z < high
        ]
        return lax.ppermute(value, "shard", pairs)

    def across(self, value, step):
        pairs = [
            (z * self.wide + w, z * self.wide + (w + step) % self.wide)
            for z in range(LINE)
            for w in range(self.wide)
        ]
        return lax.ppermute(value, "shard", pairs)

    def gather(self, value):
        rows = value.shape[0]
        z = self.z
        blocks = [(z, value)]
        up = [None, value]
        down = [None, value]
        up[1] = self.along(value, 1)
        down[1] = self.along(value, -1)
        for k in range(2, LINE):
            up.append(self.along(up[-1], 1, low=k - 1))
            down.append(self.along(down[-1], -1, high=LINE - k + 1))
        blocks.append((jnp.where(z == 0, 1, z - 1), jnp.where(z == 0, down[1], up[1])))
        blocks.append((jnp.where(z < 2, z + 2, z - 2), jnp.where(z < 2, down[2], up[2])))
        inner = (z == 1) | (z == 2)
        blocks.append(
            (
                jnp.where(inner, z + 1, jnp.where(z == 0, 3, 0)),
                jnp.where(inner, down[1], jnp.where(z == 0, down[3], up[3])),
            )
        )
        out = jnp.zeros((self.n,) + value.shape, value.dtype)
        for source, block in blocks:
            out = lax.dynamic_update_index_in_dim(out, block, source * self.wide + self.w, 0)
            for step in range(1, self.wide):
                other = self.across(block, step)
                place = source * self.wide + (self.w - step) % self.wide
                out = lax.dynamic_update_index_in_dim(out, other, place, 0)
        return out.reshape((self.n * rows,) + value.shape[1:])

    def scatter(self, value):
        rows = value.shape[0] // self.n
        kind = value.dtype

        blocks = value.reshape((self.n, rows) + value.shape[1:])

        def block(z, w):
            return lax.dynamic_index_in_dim(blocks, z * self.wide + w, 0, False)

        parts = [None] * LINE
        for k in (2, 1, 3, 0):
            target = (self.z + k) % LINE
            total = block(target, self.w).astype(F32)
            for step in range(1, self.wide):
                total = total + self.across(
                    block(target, (self.w + step) % self.wide), step
                ).astype(F32)
            parts[k] = total
        up = self.along(parts[3].astype(kind), 1, high=1).astype(F32)
        down = self.along(parts[1].astype(kind), -1, low=3).astype(F32)
        up = self.along((parts[2] + up).astype(kind), 1, high=2).astype(F32)
        down = self.along((parts[2] + down).astype(kind), -1, low=2).astype(F32)
        up = self.along((parts[1] + up).astype(kind), 1).astype(F32)
        down = self.along((parts[3] + down).astype(kind), -1).astype(F32)
        return parts[0] + up + down

    def spread(self, value):
        many = jnp.broadcast_to(value[None], (self.n,) + value.shape)
        return lax.all_to_all(many, "shard", 0, 0, tiled=True)

    def core(self, value):
        return lax.ppermute(value, "rep", [(r, r ^ 1) for r in range(self.n_rep)])

    def rep_sum(self, value):
        rep = lax.axis_index("rep")
        core, chip = rep % 2, rep // 2
        value = value.astype(BF16).reshape((2, 2, -1) + value.shape[1:])
        mine = lax.dynamic_index_in_dim(value, core, 1, False).astype(F32)
        mine = mine + self.core(lax.dynamic_index_in_dim(value, 1 - core, 1, False)).astype(F32)
        sent = lax.dynamic_index_in_dim(mine, 1 - chip, 0, False).astype(BF16)
        return lax.dynamic_index_in_dim(mine, chip, 0, False) + self.chip(sent).astype(F32)

    def chip(self, value):
        return lax.ppermute(value, "rep", [(r, r ^ 2) for r in range(self.n_rep)])


def build(mesh):
    n_shard = mesh.shape["shard"]
    n_rep = mesh.shape["rep"]

    def local(
        token_ids,
        target_ids,
        loss_mask,
        table_master,
        attn_in_master,
        attn_out_master,
        mlp_in_master,
        mlp_out_master,
        gain_master,
        table_first,
        attn_in_first,
        attn_out_first,
        mlp_in_first,
        mlp_out_first,
        gain_first,
        table_second,
        attn_in_second,
        attn_out_second,
        mlp_in_second,
        mlp_out_second,
        gain_second,
    ):
        links = Links(n_shard, n_rep)
        my_rep = lax.axis_index("rep")
        my_shard = lax.axis_index("shard")
        second_core = (my_rep % 2) == 1
        tok_rows = token_ids.shape[0]
        seq_len = n_shard * tok_rows
        vocab_rows = table_master.shape[0]
        vocab_start = my_shard * vocab_rows
        positions = my_shard * tok_rows + jnp.arange(tok_rows, dtype=jnp.int32)

        def in_order(mine, other, axis=-1):
            return jnp.where(
                second_core,
                jnp.concatenate([other, mine], axis),
                jnp.concatenate([mine, other], axis),
            )

        def my_half(value, axis=-1):
            first, second = jnp.split(value, 2, axis)
            return jnp.where(second_core, second, first), jnp.where(second_core, first, second)

        packed = jnp.stack([token_ids, target_ids, loss_mask])
        reps = lax.all_gather(packed, "rep")
        everyone = links.spread(reps)
        all_ids = everyone[:, :, 0].reshape(-1) - vocab_start
        all_mask = everyone[:, :, 2].astype(F32)
        valid_count = jnp.sum(all_mask)
        group = lax.dynamic_index_in_dim(everyone, my_rep, 1, False)
        group_ids = group[:, 0].reshape(-1)
        group_targets = group[:, 1].reshape(-1)
        group_weights = group[:, 2].reshape(-1).astype(F32) / valid_count

        def halves(master):
            return my_half(master[0].astype(BF16))[0]

        unit_rows = FF // n_shard
        unit_part = unit_rows // n_rep
        units = n_shard * unit_part
        mlp_in_part = mlp_in_master[0].astype(BF16)
        mlp_in_part = mlp_in_part.reshape(-1, 2, n_shard, n_rep, unit_part)
        mlp_in_part = lax.dynamic_index_in_dim(mlp_in_part, my_rep, 3, False).reshape(-1, 2 * units)
        mlp_out_part = mlp_out_master[0].astype(BF16).reshape(n_rep, unit_part, D)
        mlp_out_part = lax.dynamic_index_in_dim(mlp_out_part, my_rep, 0, False)
        attn_mine = links.gather(
            jnp.concatenate([halves(attn_in_master), halves(attn_out_master)], 1)
        )
        mlp_in = lax.all_gather(mlp_in_part, "shard", tiled=True)
        mlp_out = lax.all_gather(mlp_out_part, "shard", tiled=True)
        in_cols = attn_in_master.shape[2] // 2
        attn_other = links.core(attn_mine)
        attn_in = (attn_mine[:, :in_cols], attn_other[:, :in_cols])
        attn_out = (attn_mine[:, in_cols:], attn_other[:, in_cols:])
        gains = links.spread(gain_master.astype(BF16)).transpose(1, 0, 2).reshape(3, D).astype(F32)

        vocab_tile = min(512, vocab_rows)
        table_low, looked = lookup(table_master.T, group_ids - vocab_start, vocab_tile)
        values = links.scatter(looked)

        owned_here = (all_ids >= 0) & (all_ids < vocab_rows)
        sort_ids = jnp.where(owned_here, all_ids, vocab_rows)
        tokens = jnp.arange(sort_ids.shape[0], dtype=jnp.int32)
        before = (sort_ids[None, :] < sort_ids[:, None]) | (
            (sort_ids[None, :] == sort_ids[:, None]) & (tokens[None, :] < tokens[:, None])
        )
        ranks = jnp.sum(before.astype(jnp.int32), axis=1)
        sorted_ids = jnp.sort(sort_ids)
        edges = jnp.arange(0, vocab_rows + 1, vocab_tile, dtype=jnp.int32)
        starts = jnp.sum((sort_ids[None, :] < edges[:, None]).astype(jnp.int32), axis=1)

        def times(value, pair):
            return dot(value, pair[0]), dot(value, pair[1])

        def times_back(mine, other, pair):
            return dot(mine, pair[0], ((1,), (1,))) + dot(other, pair[1], ((1,), (1,)))

        normed_one, norm_one_back = jax.vjp(rms_norm, values, gains[0])
        normed_one = normed_one.astype(BF16)
        mixed = in_order(*times(normed_one, attn_in))
        heads_raw = mixed[:, : QUERY + KEY].reshape(tok_rows, HEADS + KV_HEADS, HEAD_DIM)
        rotated, rope_back = jax.vjp(lambda part: rotate(part, positions), heads_raw)
        rotated = rotated.astype(BF16)
        group_size = HEADS // KV_HEADS
        queries = rotated[:, :HEADS].reshape(tok_rows, KV_HEADS, group_size, HEAD_DIM)
        queries = queries.transpose(1, 2, 0, 3).reshape(KV_HEADS, group_size * tok_rows, HEAD_DIM)
        keys_values = jnp.concatenate(
            [rotated[:, HEADS:].reshape(tok_rows, KEY), mixed[:, QUERY + KEY :].astype(BF16)], 1
        )
        keys_values = links.gather(keys_values)
        keys_values = keys_values.reshape(seq_len, 2, KV_HEADS, HEAD_DIM).transpose(1, 2, 0, 3)
        keys, vals = keys_values[0], keys_values[1]
        scale = HEAD_DIM ** (-0.5)
        key_blocks = jnp.arange(seq_len, dtype=jnp.int32) // BLOCK
        query_blocks = jnp.tile(positions // BLOCK, group_size)
        allowed = (key_blocks[None, :] <= query_blocks[:, None])[None]

        def batched(spec, a, b):
            return jnp.einsum(spec, a, b, preferred_element_type=F32)

        scores = jnp.where(allowed, batched("htd,hsd->hts", queries, keys) * scale, -1e30)
        highest = jnp.max(scores, axis=-1, keepdims=True)
        weights = jnp.exp(scores - highest)
        totals = jnp.sum(weights, axis=-1, keepdims=True)
        chances = weights / totals
        chances_low = chances.astype(BF16)
        outputs = batched("hts,hsd->htd", chances_low, vals)

        def to_rows(heads):
            return (
                heads.reshape(KV_HEADS, group_size, tok_rows, HEAD_DIM)
                .transpose(2, 0, 1, 3)
                .reshape(tok_rows, QUERY)
            )

        attended = to_rows(outputs).astype(BF16)
        middle = values + in_order(*times(attended, attn_out))
        normed_two, norm_two_back = jax.vjp(rms_norm, middle, gains[1])
        normed_two = normed_two.astype(BF16)
        normed_all = lax.all_gather(normed_two, "rep", tiled=True)
        gate_up = dot(normed_all, mlp_in)
        hidden, glu_back = jax.vjp(swiglu, gate_up[:, :units], gate_up[:, units:])
        hidden = hidden.astype(BF16)
        result = middle + links.rep_sum(dot(hidden, mlp_out))
        final, final_back = jax.vjp(rms_norm, result, gains[2])

        states = links.gather(final.astype(BF16))
        local_targets = group_targets - vocab_start
        raised, stats = head_logits(states, local_targets, table_low)
        high = stats[:, 0]
        stats = links.spread(stats[:, :3].T)
        top = jnp.max(stats[:, 0], axis=0)
        log_totals = top + jnp.log(jnp.sum(stats[:, 1] * jnp.exp(stats[:, 0] - top), axis=0))
        picked = jnp.sum(stats[:, 2], axis=0)
        group_loss = jnp.sum((log_totals - picked) * group[:, 2].reshape(-1).astype(F32))
        grad_logits, grad_states = head_states(
            raised, jnp.exp(high - log_totals), group_weights, local_targets, table_low
        )
        grad_final = links.scatter(grad_states)

        my_core = my_rep % 2
        states_t = states.T
        grad_other = links.core(head_table(states_t, grad_logits, 1 - my_core))
        grad_mine = head_table(states_t, grad_logits, my_core)
        chip_sum = (grad_mine.astype(F32) + grad_other.astype(F32)).astype(BF16)
        chip_sum, grad_final = lax.optimization_barrier((chip_sum, grad_final))
        half_sum = (chip_sum.astype(F32) + links.chip(chip_sum).astype(F32)).astype(BF16)
        other_sum = links.core(half_sum)

        grad_output, grad_gain_three = final_back(grad_final)

        def weight_grad(value, mine, other):
            sent = dot(value, other, ((0,), (0,))).astype(BF16)
            return (dot(value, mine, ((0,), (0,))) + links.core(sent).astype(F32)).astype(BF16)

        def owned(part):
            part = links.scatter(part).astype(BF16)
            part = part.astype(F32) + links.chip(part).astype(F32)
            return part, links.core(part)

        branch = lax.all_gather(grad_output.astype(BF16), "rep", tiled=True)
        grad_mlp_out = dot(hidden, branch, ((0,), (0,))).astype(BF16)
        grad_hidden = dot(branch, mlp_out, ((1,), (1,)))
        grad_glu = jnp.concatenate(glu_back(grad_hidden), 1).astype(BF16)
        grad_mlp_in = dot(normed_all, grad_glu, ((0,), (0,))).astype(BF16)
        grad_normed_two = links.rep_sum(dot(grad_glu, mlp_in, ((1,), (1,))))
        middle_part, grad_gain_two = norm_two_back(grad_normed_two)
        grad_middle = grad_output + middle_part

        in_size = D // n_shard * 2 * units
        both = jnp.concatenate(
            [grad_mlp_in.reshape(n_shard, -1), grad_mlp_out.reshape(n_shard, -1)], 1
        ).reshape(-1, 128)
        both = lax.psum_scatter(both, "shard", tiled=True).reshape(-1)
        mlp_in_sum = lax.all_gather(both[:in_size].reshape(-1, 2, n_shard, unit_part), "rep")
        mlp_in_sum = mlp_in_sum.transpose(1, 2, 3, 0, 4).reshape(-1, 2 * FF).astype(F32)
        mlp_out_sum = lax.all_gather(both[in_size:].reshape(unit_part, D), "rep", tiled=True)
        mlp_out_sum = mlp_out_sum.astype(F32)

        out_mine, out_other = my_half(grad_middle.astype(BF16))
        grad_attn_out = weight_grad(attended, out_mine, out_other)
        grad_attn_out = lax.psum_scatter(grad_attn_out, "shard", tiled=True)
        grad_attn_out = grad_attn_out.astype(F32) + links.chip(grad_attn_out).astype(F32)
        attn_out_sum = in_order(grad_attn_out, links.core(grad_attn_out))
        grad_attended = times_back(out_mine, out_other, attn_out).astype(BF16)
        grad_heads = (
            grad_attended.reshape(tok_rows, KV_HEADS, group_size, HEAD_DIM)
            .transpose(1, 2, 0, 3)
            .reshape(KV_HEADS, group_size * tok_rows, HEAD_DIM)
        )
        deltas = jnp.sum(grad_heads.astype(F32) * outputs, axis=-1, keepdims=True)
        grad_chances = batched("htd,hsd->hts", grad_heads, vals)
        grad_scores = (chances * (grad_chances - deltas)).astype(BF16)
        grad_queries = batched("hts,hsd->htd", grad_scores, keys) * scale
        grad_keys = batched("hts,htd->hsd", grad_scores, queries) * scale
        grad_vals = batched("hts,htd->hsd", chances_low, grad_heads)
        grad_kv = jnp.stack([grad_keys, grad_vals]).transpose(2, 0, 1, 3).reshape(seq_len, 2 * KEY)
        grad_kv = links.scatter(grad_kv.astype(BF16))
        grad_rotated = jnp.concatenate(
            [
                to_rows(grad_queries).reshape(tok_rows, HEADS, HEAD_DIM),
                grad_kv[:, :KEY].reshape(tok_rows, KV_HEADS, HEAD_DIM),
            ],
            1,
        )
        grad_raw = rope_back(grad_rotated)[0].reshape(tok_rows, QUERY + KEY)
        grad_mixed = jnp.concatenate([grad_raw, grad_kv[:, KEY:]], 1).astype(BF16)
        mixed_mine, mixed_other = my_half(grad_mixed)
        values_part, grad_gain_one = norm_one_back(times_back(mixed_mine, mixed_other, attn_in))
        grad_values = (grad_middle + values_part).astype(BF16)
        grad_attn_in = weight_grad(normed_one, mixed_mine, mixed_other)
        grad_gains = jnp.stack([grad_gain_one, grad_gain_two, grad_gain_three], 1)
        grad_gains = grad_gains + links.core(grad_gains)
        small = jnp.concatenate([grad_attn_in, grad_gains.astype(BF16)], 1)
        small_mine, small_other = owned(small)
        attn_in_sum = in_order(small_mine[:, :in_cols], small_other[:, :in_cols])
        gain_sum = small_mine[:, in_cols:].T

        embedded = links.gather(lax.all_gather(grad_values.T, "rep"))
        table_sum, table_squares = place_tokens(
            half_sum, other_sum, my_core, embedded, ranks, sorted_ids, starts, vocab_tile
        )
        sums = (
            table_sum,
            attn_in_sum[None],
            attn_out_sum[None],
            mlp_in_sum[None],
            mlp_out_sum[None],
            gain_sum,
        )
        squares = jnp.sum(table_squares)
        for gradient in sums[1:]:
            squares = squares + jnp.sum(gradient * gradient)
        loss = group_loss + links.core(group_loss)
        loss_sum = loss + links.chip(loss)
        squares = jnp.sum(links.spread(jnp.full((8, 128), squares))[:, 0, 0])
        grad_norm = jnp.sqrt(squares)
        clip_scale = CLIP_AT / jnp.maximum(grad_norm, CLIP_AT)
        results = [loss_sum, valid_count, grad_norm]
        masters = (
            table_master.T,
            attn_in_master,
            attn_out_master,
            mlp_in_master,
            mlp_out_master,
            gain_master,
        )
        firsts = (
            table_first.T,
            attn_in_first,
            attn_out_first,
            mlp_in_first,
            mlp_out_first,
            gain_first,
        )
        seconds = (
            table_second.T,
            attn_in_second,
            attn_out_second,
            mlp_in_second,
            mlp_out_second,
            gain_second,
        )
        rate_list = rates(seq_len)
        new = adam(
            masters[0], firsts[0], seconds[0], sums[0], clip_scale, rate_list[0], vocab_tile
        )
        results.extend(part.T for part in new)
        for member in range(1, 6):
            results.extend(
                adam_update(
                    masters[member],
                    firsts[member],
                    seconds[member],
                    sums[member] * clip_scale,
                    rate_list[member],
                )
            )
        return tuple(results)

    return local


def solution(mesh):
    token = P(("rep", "shard"))
    weight = P(None, "shard", None)
    state = (P("shard", None), weight, weight, weight, weight, P(None, "shard"))
    outs = [P(), P(), P()]
    for spec in state:
        outs.extend([spec] * 4)
    return jax.shard_map(
        build(mesh),
        mesh=mesh,
        in_specs=(token, token, token) + state * 3,
        out_specs=tuple(outs),
        check_vma=False,
    )
```

```python
import functools

import jax
import jax.numpy as jnp
from jax import lax
from jax.experimental import pallas as pl
from jax.experimental.pallas import tpu as pltpu
from jax.sharding import PartitionSpec as P

D = 960
HEADS = 15
KV_HEADS = 5
HEAD_DIM = 64
FF = 2560
BLOCK = 256
STEP = 5
LINE = 4

EPS_NORM = 1e-05
ROPE_BASE = 100000.0
BETA_ONE = 0.5
BETA_TWO = 0.5
DECAY = 0.1
CLIP_AT = 0.01
ADAM_EPS = 1e-08

F32 = jnp.float32
BF16 = jnp.bfloat16
QUERY = HEADS * HEAD_DIM
KEY = KV_HEADS * HEAD_DIM
VMEM = 56 * 1024 * 1024


def rms_norm(values, gain):
    return values * lax.rsqrt(jnp.mean(values * values, axis=-1, keepdims=True) + EPS_NORM) * gain


def rotate(values, positions):
    half_dim = values.shape[-1] // 2
    freqs = ROPE_BASE ** (-2.0 * jnp.arange(half_dim).astype(F32) / values.shape[-1])
    angles = positions.astype(F32)[:, None] * freqs[None, :]
    cosine = jnp.cos(angles)[:, None, :]
    sine = jnp.sin(angles)[:, None, :]
    first_half = values[..., :half_dim]
    second_half = values[..., half_dim:]
    return jnp.concatenate(
        [first_half * cosine - second_half * sine, second_half * cosine + first_half * sine],
        axis=-1,
    )


def swiglu(gate, up):
    return jax.nn.silu(gate) * up


def rates(seq_len):
    out_fan = max(1, HEADS * HEAD_DIM * 16 // seq_len)
    return (
        0.8 * D ** (-0.5),
        0.5 * D ** (-0.5),
        0.5 * out_fan ** (-0.5),
        0.5 * D ** (-0.5),
        0.5 * FF ** (-0.5),
        0.2,
    )


def adam_update(master, first, second, gradient, rate):
    first_new = BETA_ONE * first + (1.0 - BETA_ONE) * gradient
    second_new = BETA_TWO * second + (1.0 - BETA_TWO) * gradient * gradient
    step_size = (
        first_new
        / (1.0 - BETA_ONE**STEP)
        / (jnp.sqrt(second_new / (1.0 - BETA_TWO**STEP)) + ADAM_EPS)
    )
    master_new = master - rate * (step_size + DECAY * master)
    return (master_new, first_new, second_new, master_new.astype(BF16))


def dot(a, b, dims=((1,), (0,))):
    return lax.dot_general(a, b, (dims, ((), ())), preferred_element_type=F32)


def params():
    return pltpu.CompilerParams(vmem_limit_bytes=VMEM)


def whole(shape):
    return pl.BlockSpec(shape, lambda *_: (0,) * len(shape), pipeline_mode=pl.Buffered(1))


def lookup_kernel(ids_ref, table_ref, low_ref, rows_ref, total):
    tile = table_ref.shape[1]
    step = pl.program_id(0)
    low = table_ref[...].astype(BF16)
    low_ref[...] = low
    columns = lax.broadcasted_iota(jnp.int32, (1, tile), 1) + step * tile
    block = min(512, rows_ref.shape[0])
    for start in range(0, rows_ref.shape[0], block):
        rows = pl.ds(start, block)
        pick = jnp.where(ids_ref[rows, :] == columns, 1.0, 0.0).astype(BF16)
        found = dot(pick, low, ((1,), (1,)))

        @pl.when(step == 0)
        def _():
            total[rows, :] = found

        @pl.when(step > 0)
        def _():
            total[rows, :] += found

    @pl.when(step == pl.num_programs(0) - 1)
    def _():
        rows_ref[...] = total[...].astype(BF16)


def lookup(table_t, local_ids, tile=512):
    width, vocab = table_t.shape
    count = local_ids.shape[0]
    return pl.pallas_call(
        lookup_kernel,
        grid=(vocab // tile,),
        in_specs=[
            whole((count, 1)),
            pl.BlockSpec((width, tile), lambda i: (0, i)),
        ],
        out_specs=[
            pl.BlockSpec((width, tile), lambda i: (0, i)),
            whole((count, width)),
        ],
        out_shape=[
            jax.ShapeDtypeStruct((width, vocab), BF16),
            jax.ShapeDtypeStruct((count, width), BF16),
        ],
        scratch_shapes=[pltpu.VMEM((count, width), F32)],
        compiler_params=params(),
        cost_estimate=pl.CostEstimate(
            flops=2 * count * width * vocab, bytes_accessed=6 * width * vocab, transcendentals=0
        ),
    )(local_ids[:, None], table_t)


def logits_kernel(states_ref, targets_ref, table_ref, raised_ref, stats_ref, logits, *, tile):
    vocab = table_ref.shape[1]
    rows = states_ref.shape[0]
    states = states_ref[...]
    high = jnp.full((rows, 1), -jnp.inf, F32)
    for start in range(0, vocab, tile):
        part = dot(states, table_ref[:, start : start + tile])
        logits[:, start : start + tile] = part
        high = jnp.maximum(high, jnp.max(part, axis=-1, keepdims=True))
    total = jnp.zeros((rows, 128), F32)
    picked = jnp.zeros((rows, 128), F32)
    targets = targets_ref[...]
    lanes = lax.broadcasted_iota(jnp.int32, (1, 128), 1)
    for start in range(0, vocab, 128):
        part = logits[:, start : start + 128]
        raised = jnp.exp(part - high)
        raised_ref[:, start : start + 128] = raised.astype(BF16)
        total += raised
        picked += jnp.where(targets == lanes + start, part, 0.0)
    total = jnp.sum(total, axis=-1, keepdims=True)
    picked = jnp.sum(picked, axis=-1, keepdims=True)
    stats_ref[...] = jnp.where(lanes == 0, high, jnp.where(lanes == 1, total, picked))


def head_logits(states, targets, table_low, rows=256, tile=512):
    count, width = states.shape
    vocab = table_low.shape[1]
    return pl.pallas_call(
        functools.partial(logits_kernel, tile=tile),
        grid=(count // rows,),
        in_specs=[
            pl.BlockSpec((rows, width), lambda i: (i, 0)),
            pl.BlockSpec((rows, 1), lambda i: (i, 0)),
            whole((width, vocab)),
        ],
        out_specs=[
            pl.BlockSpec((rows, vocab), lambda i: (i, 0)),
            pl.BlockSpec((rows, 128), lambda i: (i, 0)),
        ],
        out_shape=[
            jax.ShapeDtypeStruct((count, vocab), BF16),
            jax.ShapeDtypeStruct((count, 128), F32),
        ],
        scratch_shapes=[pltpu.VMEM((rows, vocab), F32)],
        compiler_params=params(),
        cost_estimate=pl.CostEstimate(
            flops=2 * count * width * vocab,
            bytes_accessed=2 * vocab * (width + count),
            transcendentals=count * vocab,
        ),
    )(states, targets[:, None], table_low)


def states_kernel(raised_ref, scales_ref, targets_ref, table_ref, grads_ref, out_ref, *, tile):
    vocab = table_ref.shape[1]
    weight = scales_ref[:, 1:2]
    factor = scales_ref[:, 0:1]
    targets = targets_ref[...]
    total = None
    for start in range(0, vocab, tile):
        lanes = lax.broadcasted_iota(jnp.int32, (1, tile), 1) + start
        chances = raised_ref[:, start : start + tile].astype(F32) * factor
        part = (jnp.where(targets == lanes, chances - weight, chances)).astype(BF16)
        grads_ref[:, start : start + tile] = part
        found = dot(part, table_ref[:, start : start + tile], ((1,), (1,)))
        total = found if total is None else total + found
    out_ref[...] = total.astype(BF16)


def head_states(raised, factors, weights, targets, table_low, rows=256, tile=512):
    count, vocab = raised.shape
    width = table_low.shape[0]
    scales = jnp.stack([factors * weights, weights], axis=1)
    return pl.pallas_call(
        functools.partial(states_kernel, tile=tile),
        grid=(count // rows,),
        in_specs=[
            pl.BlockSpec((rows, vocab), lambda i: (i, 0)),
            pl.BlockSpec((rows, 2), lambda i: (i, 0)),
            pl.BlockSpec((rows, 1), lambda i: (i, 0)),
            whole((width, vocab)),
        ],
        out_specs=[
            pl.BlockSpec((rows, vocab), lambda i: (i, 0)),
            pl.BlockSpec((rows, width), lambda i: (i, 0)),
        ],
        out_shape=[
            jax.ShapeDtypeStruct((count, vocab), BF16),
            jax.ShapeDtypeStruct((count, width), BF16),
        ],
        compiler_params=params(),
        cost_estimate=pl.CostEstimate(
            flops=2 * count * width * vocab,
            bytes_accessed=2 * vocab * (width + 2 * count),
            transcendentals=0,
        ),
    )(raised, scales, targets[:, None], table_low)


def table_kernel(
    part_ref,
    near_t,
    far_t,
    near_pair_t,
    far_pair_t,
    near_grads,
    far_grads,
    near_pair,
    far_pair,
    scales,
    targets,
    table_ref,
    out_ref,
):
    tile = out_ref.shape[1]
    step = part_ref[0] * pl.num_programs(0) + pl.program_id(0)
    columns = lax.broadcasted_iota(jnp.int32, (1, tile), 1) + step * tile
    total = dot(near_t[...], near_grads[...]) + dot(far_t[...], far_grads[...])
    offset = 0
    for pair, pair_t in ((near_pair, near_pair_t), (far_pair, far_pair_t)):
        block = min(512, pair.shape[0])
        for start in range(0, pair.shape[0], block):
            rows = slice(offset + start, offset + start + block)
            weight = scales[rows, 1:2]
            logits = dot(pair[start : start + block, :], table_ref[...])
            chances = jnp.exp(logits - scales[rows, 0:1]) * weight
            grads = jnp.where(targets[rows, :] == columns, chances - weight, chances)
            total += dot(pair_t[:, start : start + block], grads.astype(BF16))
        offset += pair.shape[0]
    out_ref[...] = total.astype(BF16)


def head_table(
    near_t,
    far_t,
    near_grads,
    far_grads,
    near_pair,
    far_pair,
    scales,
    targets,
    table_low,
    part,
    tile,
):
    width, near = near_t.shape
    far = far_t.shape[1]
    both = near + far
    vocab = near_grads.shape[1] // 4
    steps = vocab // tile

    def column(i, part):
        return (0, part[0] * steps + i)

    return pl.pallas_call(
        table_kernel,
        grid_spec=pltpu.PrefetchScalarGridSpec(
            num_scalar_prefetch=1,
            grid=(steps,),
            in_specs=[
                whole((width, near)),
                whole((width, far)),
                whole((width, near)),
                whole((width, far)),
                pl.BlockSpec((near, tile), column),
                pl.BlockSpec((far, tile), column),
                whole((near, width)),
                whole((far, width)),
                whole((both, 2)),
                whole((both, 1)),
                pl.BlockSpec((width, tile), column),
            ],
            out_specs=pl.BlockSpec((width, tile), lambda i, part: (0, i)),
        ),
        out_shape=jax.ShapeDtypeStruct((width, vocab), BF16),
        compiler_params=params(),
        cost_estimate=pl.CostEstimate(
            flops=6 * both * width * vocab,
            bytes_accessed=2 * (2 * vocab + 3 * both) * width + 2 * vocab * both,
            transcendentals=both * vocab,
        ),
    )(
        jnp.reshape(part, (1,)).astype(jnp.int32),
        near_t,
        far_t,
        near_pair.T,
        far_pair.T,
        near_grads,
        far_grads,
        near_pair,
        far_pair,
        scales,
        targets[:, None],
        table_low,
    )


def place_kernel(
    starts_ref,
    ranks_ref,
    ids_ref,
    rows_ref,
    kept_ref,
    received_ref,
    out_ref,
    square_ref,
    sorted_rows,
    total,
    *,
    chunk,
    block,
):
    step = pl.program_id(0)
    tile = out_ref.shape[1]
    sources, lanes, _ = rows_ref.shape

    @pl.when(step == 0)
    def _():
        def sort(k, carry):
            columns = pl.ds(pl.multiple_of(k * block, block), block)
            wanted = lax.broadcasted_iota(jnp.int32, (1, block), 1) + k * block
            found = None
            for source in range(sources):
                pick = ranks_ref[source * lanes : (source + 1) * lanes, :] == wanted
                pick = jnp.where(pick, 1.0, 0.0).astype(BF16)
                part = dot(rows_ref[source], pick, ((0,), (0,)))
                found = part if found is None else found + part
            sorted_rows[:, columns] = found.astype(BF16)
            return carry

        lax.fori_loop(0, (starts_ref[pl.num_programs(0)] + block - 1) // block, sort, 0)

    first = starts_ref[step]
    last = starts_ref[step + 1]
    total[...] = kept_ref[...].astype(F32) + received_ref[...].astype(F32)
    columns = lax.broadcasted_iota(jnp.int32, (1, tile), 1) + step * tile

    def add(k, carry):
        rows = pl.ds(pl.multiple_of(k * chunk, chunk), chunk)
        place = lax.broadcasted_iota(jnp.int32, (chunk, 1), 0) + k * chunk
        ids = ids_ref[rows, :]
        inside = jnp.logical_and(place >= first, place < last)
        pick = jnp.where(jnp.logical_and(ids == columns, inside), 1.0, 0.0).astype(BF16)
        total[...] += dot(sorted_rows[:, rows], pick)
        return carry

    lax.fori_loop(first // chunk, (last + chunk - 1) // chunk, add, 0)
    low = total[...].astype(BF16)
    out_ref[...] = low
    value = low.astype(F32)
    squares = jnp.sum(value * value, axis=0, keepdims=True)
    part = jnp.zeros((1, 128), F32)
    for start in range(0, tile, 128):
        part += squares[:, start : start + 128]

    @pl.when(step == 0)
    def _():
        square_ref[...] = part

    @pl.when(step > 0)
    def _():
        square_ref[...] += part


def place_rows(kept, received, rows, ranks, ids, starts, tile, chunk=128, block=256):
    width, columns = kept.shape
    sources, lanes, _ = rows.shape
    total = sources * lanes
    block = min(block, total)
    spec = pl.BlockSpec((width, tile), lambda i, starts: (0, i))
    return pl.pallas_call(
        functools.partial(place_kernel, chunk=chunk, block=block),
        grid_spec=pltpu.PrefetchScalarGridSpec(
            num_scalar_prefetch=1,
            grid=(columns // tile,),
            in_specs=[whole((total, 1)), whole((total, 1)), whole((sources, lanes, width))]
            + [spec] * 2,
            out_specs=[spec, whole((1, 128))],
            scratch_shapes=[pltpu.VMEM((width, total), BF16), pltpu.VMEM((width, tile), F32)],
        ),
        out_shape=[
            jax.ShapeDtypeStruct((width, columns), BF16),
            jax.ShapeDtypeStruct((1, 128), F32),
        ],
        compiler_params=params(),
        cost_estimate=pl.CostEstimate(
            flops=2 * 4 * chunk * tile * width,
            bytes_accessed=6 * width * columns + 2 * total * width,
            transcendentals=0,
        ),
    )(starts, ranks[:, None], ids[:, None], rows, kept, received)


def adam_kernel(quarters_ref, scale_ref, w_ref, m_ref, v_ref, one_ref, two_ref, *refs, rate):
    step = pl.program_id(0)
    half = pl.num_programs(0) // 2
    outs = refs[-4:]

    def update(gradient):
        new = adam_update(w_ref[...], m_ref[...], v_ref[...], gradient * scale_ref[0], rate)
        for ref, value in zip(outs, new):
            ref[...] = value

    @pl.when(step < half)
    def _():
        update(one_ref[...].astype(F32))

    @pl.when(step >= half)
    def _():
        update(two_ref[...].astype(F32))


def adam(master, first, second, one, two, quarters, scale, rate, tile, before=None):
    rows, columns = master.shape
    steps = one.shape[1] // tile

    def column(i, quarters):
        return (0, quarters[i // steps] * steps + i % steps)

    spec = pl.BlockSpec((rows, tile), column)
    shape = jax.ShapeDtypeStruct((rows, columns), F32)
    before = list(before or [])
    return pl.pallas_call(
        functools.partial(adam_kernel, rate=rate),
        grid_spec=pltpu.PrefetchScalarGridSpec(
            num_scalar_prefetch=1,
            grid=(2 * steps,),
            in_specs=[pl.BlockSpec(memory_space=pltpu.SMEM)]
            + [spec] * 3
            + [
                pl.BlockSpec((rows, tile), lambda i, q: (0, jnp.minimum(i, steps - 1))),
                pl.BlockSpec((rows, tile), lambda i, q: (0, jnp.maximum(i - steps, 0))),
            ]
            + [pl.BlockSpec(memory_space=pl.ANY)] * len(before),
            out_specs=[spec] * 4,
        ),
        out_shape=[shape] * 3 + [jax.ShapeDtypeStruct((rows, columns), BF16)],
        input_output_aliases={7 + k: k for k in range(len(before))},
        compiler_params=params(),
        cost_estimate=pl.CostEstimate(flops=0, bytes_accessed=0, transcendentals=0),
    )(
        quarters.astype(jnp.int32),
        jnp.reshape(scale, (1,)),
        master,
        first,
        second,
        one,
        two,
        *before,
    )


def adam_many_kernel(scale_ref, *refs, rates):
    count = len(rates)
    inputs, outputs = refs[: 4 * count], refs[4 * count :]
    scale = scale_ref[0]
    for member, rate in enumerate(rates):
        olds = inputs[4 * member : 4 * member + 4]
        news = outputs[4 * member : 4 * member + 4]
        rows = olds[0].shape[0]
        block = 8 if rows % 8 == 0 else rows

        def update(k, carry, olds=olds, news=news, block=block, rate=rate):
            place = pl.ds(pl.multiple_of(k * block, block), block)
            w, m, v, g = (ref[place, :] for ref in olds)
            for ref, value in zip(news, adam_update(w, m, v, g * scale, rate)):
                ref[place, :] = value
            return carry

        lax.fori_loop(0, rows // block, update, 0)


def adam_many(olds, scale, rates):
    shapes = []
    for master, *_ in olds:
        shapes += [jax.ShapeDtypeStruct(master.shape, F32)] * 3
        shapes += [jax.ShapeDtypeStruct(master.shape, BF16)]
    inside = pl.BlockSpec(memory_space=pltpu.VMEM)
    return pl.pallas_call(
        functools.partial(adam_many_kernel, rates=rates),
        in_specs=[pl.BlockSpec(memory_space=pltpu.SMEM)] + [inside] * (4 * len(olds)),
        out_specs=[inside] * (4 * len(olds)),
        out_shape=shapes,
        compiler_params=params(),
        cost_estimate=pl.CostEstimate(flops=0, bytes_accessed=0, transcendentals=0),
    )(jnp.reshape(scale, (1,)), *[part for member in olds for part in member])


def place_slowly(kept, received, rows, ids):
    columns = jnp.arange(kept.shape[1], dtype=jnp.int32)

    def add(total, operands):
        part, part_ids = operands
        pick = (part_ids[:, None] == columns[None, :]).astype(BF16)
        return total + dot(part, pick, ((0,), (0,))), None

    total, _ = lax.scan(add, kept.astype(F32) + received.astype(F32), (rows, ids))
    total = total.astype(BF16)
    squares = jnp.sum(jnp.square(total.astype(F32)))
    return total, jnp.full((1, 128), squares / 128)


class Links:
    def __init__(self, n_shard, n_rep):
        self.n = n_shard
        self.wide = n_shard // LINE
        self.n_rep = n_rep
        me = lax.axis_index("shard")
        self.z = me // self.wide
        self.w = me % self.wide
        self.lines = [[z * self.wide + w for z in range(LINE)] for w in range(self.wide)]

    def across(self, value, step):
        pairs = [
            (z * self.wide + w, z * self.wide + (w + step) % self.wide)
            for z in range(LINE)
            for w in range(self.wide)
        ]
        return lax.ppermute(value, "shard", pairs)

    def all_across(self, value):
        return jnp.stack([self.across(value, step) for step in range(1, self.wide)])

    def sum_across(self, near, far):
        rows = near.shape[0]
        total = near.astype(F32)
        for step in range(1, self.wide):
            part = far[(step - 1) * rows : step * rows] if self.wide > 2 else far
            total = total + self.across(part, -step).astype(F32)
        return total

    def line_gather(self, value):
        return lax.all_gather(value, "shard", axis_index_groups=self.lines, tiled=True)

    def line_sum(self, value):
        parts = lax.all_to_all(
            value.astype(BF16), "shard", 0, 0, axis_index_groups=self.lines, tiled=True
        )
        return jnp.sum(parts.astype(F32), axis=0)

    def scatter(self, value):
        value = value.reshape((self.n, -1) + value.shape[1:])
        parts = lax.all_to_all(value, "shard", 0, 0, tiled=True)
        return jnp.sum(parts.astype(F32), axis=0)

    def spread(self, value):
        many = jnp.broadcast_to(value[None], (self.n,) + value.shape)
        return lax.all_to_all(many, "shard", 0, 0, tiled=True)

    def core(self, value):
        return lax.ppermute(value, "rep", [(r, r ^ 1) for r in range(self.n_rep)])

    def rep_gather(self, value):
        value = value[None]
        value = jnp.concatenate([value, self.chip(value)])
        return jnp.concatenate([value, self.core(value)])

    def rep_gather_now(self, value):
        rep = lax.axis_index("rep")
        value = lax.all_gather(value, "rep")
        return jnp.concatenate(
            [lax.dynamic_index_in_dim(value, rep ^ other, 0) for other in (0, 2, 1, 3)]
        )

    def rep_sum(self, value):
        value = value.astype(BF16)
        mine = value[:2].astype(F32) + self.core(value[2:]).astype(F32)
        return mine[0] + self.chip(mine[1].astype(BF16)).astype(F32)

    def chip(self, value):
        return lax.ppermute(value, "rep", [(r, r ^ 2) for r in range(self.n_rep)])


def build(mesh):
    n_shard = mesh.shape["shard"]
    n_rep = mesh.shape["rep"]

    def local(
        token_ids,
        target_ids,
        loss_mask,
        table_master,
        attn_in_master,
        attn_out_master,
        mlp_in_master,
        mlp_out_master,
        gain_master,
        table_first,
        attn_in_first,
        attn_out_first,
        mlp_in_first,
        mlp_out_first,
        gain_first,
        table_second,
        attn_in_second,
        attn_out_second,
        mlp_in_second,
        mlp_out_second,
        gain_second,
    ):
        links = Links(n_shard, n_rep)
        my_rep = lax.axis_index("rep")
        my_shard = lax.axis_index("shard")
        second_core = (my_rep % 2) == 1
        second_chip = (my_rep // 2) == 1
        tok_rows = token_ids.shape[0]
        seq_len = n_shard * tok_rows
        vocab_rows = table_master.shape[0]
        vocab_start = my_shard * vocab_rows
        wide = n_shard // LINE
        line_rows = LINE * tok_rows

        def in_order(mine, other, axis=-1):
            return jnp.where(
                second_core,
                jnp.concatenate([other, mine], axis),
                jnp.concatenate([mine, other], axis),
            )

        def my_half(value, axis=-1):
            first, second = jnp.split(value, 2, axis)
            return jnp.where(second_core, second, first), jnp.where(second_core, first, second)

        packed = jnp.stack([token_ids, target_ids, loss_mask])
        everyone = links.spread(lax.all_gather(packed, "rep")).transpose(1, 0, 2, 3)
        everyone = everyone.reshape(LINE, n_rep, wide, 3, tok_rows).transpose(1, 0, 2, 3, 4)
        valid_count = jnp.sum(everyone[:, :, :, 2].astype(F32))
        turn = [(links.w - step) % wide for step in range(wide)]

        def group_of(rep):
            group = lax.dynamic_index_in_dim(everyone, rep, 0, False)
            group = jnp.stack(
                [lax.dynamic_index_in_dim(group, turn[step], 1, False) for step in range(wide)]
            )
            targets = group[:, :, 1].reshape(-1) - vocab_start
            return targets, group[:, :, 2].reshape(-1).astype(F32)

        group_targets, group_mask = group_of(my_rep)
        pair_targets, pair_mask = group_of(my_rep ^ 2)
        group_weights = group_mask / valid_count
        pair_weights = pair_mask / valid_count
        place_block = my_rep * wide + links.w
        positions = place_block * tok_rows + jnp.arange(tok_rows, dtype=jnp.int32)

        def halves(master):
            return my_half(master[0].astype(BF16))[0]

        unit_rows = FF // n_shard
        unit_part = unit_rows // n_rep
        units = n_shard * unit_part
        mlp_in_part = mlp_in_master[0].astype(BF16)
        mlp_in_part = mlp_in_part.reshape(-1, 2, n_shard, n_rep, unit_part)
        mlp_in_part = lax.dynamic_index_in_dim(mlp_in_part, my_rep, 3, False).reshape(-1, 2 * units)
        mlp_out_part = mlp_out_master[0].astype(BF16).reshape(n_rep, unit_part, D)
        mlp_out_part = lax.dynamic_index_in_dim(mlp_out_part, my_rep, 0, False)
        in_rows = D // n_shard
        in_cols = attn_in_master.shape[2] // 2
        attn_part = jnp.concatenate([halves(attn_in_master), halves(attn_out_master)], 1)
        mlp_part = jnp.concatenate([mlp_in_part, mlp_out_part.reshape(in_rows, -1)], 1)
        attn_mine = lax.all_gather(attn_part, "shard", tiled=True)

        room = min(64, tok_rows)
        vocab_tile = min(512, vocab_rows // 4)
        all_ids = everyone[:, :, :, 0].reshape(n_rep, n_shard, tok_rows)
        earlier = jnp.tril(jnp.ones((tok_rows, tok_rows), BF16), -1)

        def places(inside):
            found = jnp.einsum(
                "...j,ij->...i", inside.astype(BF16), earlier, preferred_element_type=F32
            )
            return jnp.where(inside, found.astype(jnp.int32), -1)

        owners = jnp.arange(n_shard, dtype=jnp.int32)
        owned = (all_ids // vocab_rows)[:, :, None, :] == owners[:, None]
        enough = jnp.max(jnp.sum(owned.astype(jnp.int32), -1)) <= room
        local_ids = all_ids - vocab_start
        inside = (local_ids >= 0) & (local_ids < vocab_rows)
        room_iota = jnp.arange(room, dtype=jnp.int32)
        slots = places(inside)
        slot_ids = jnp.max(
            jnp.where(slots[:, :, None, :] == room_iota[:, None], local_ids[:, :, None, :], -1), -1
        )
        slot_ids = jnp.where(slot_ids < 0, vocab_rows, slot_ids)
        own_ids = lax.dynamic_index_in_dim(
            lax.dynamic_index_in_dim(all_ids, my_rep, 0, False), my_shard, 0, False
        )
        own_slots = places((own_ids // vocab_rows)[None, :] == owners[:, None])
        packing = (own_slots[:, None, :] == room_iota[:, None]).astype(BF16).reshape(-1, tok_rows)

        my_slots = lax.dynamic_index_in_dim(slot_ids, my_rep, 0, False).reshape(-1)
        table_low, looked = lookup(table_master.T, my_slots, min(512, vocab_rows))

        looked, mlp_part = lax.optimization_barrier((looked, mlp_part))
        mlp_all = lax.all_gather(mlp_part, "shard", tiled=True)
        packed = lax.all_to_all(looked.reshape(n_shard, room, D), "shard", 0, 0, tiled=True)
        packed = dot(packing, packed.reshape(-1, D), ((0,), (0,)))

        def read_whole(packed, table_low):
            ids = lax.dynamic_index_in_dim(local_ids, my_rep, 0, False).reshape(-1)
            columns = jnp.arange(vocab_rows, dtype=jnp.int32)
            pick = (ids[:, None] == columns[None, :]).astype(BF16)
            rows = dot(pick, table_low, ((1,), (1,))).astype(BF16)
            rows = lax.all_to_all(rows.reshape(n_shard, tok_rows, D), "shard", 0, 0, tiled=True)
            return jnp.sum(rows.astype(F32), axis=0)

        values = lax.cond(enough, lambda packed, _: packed, read_whole, packed, table_low)
        values, gain_low = lax.optimization_barrier((values, gain_master.astype(BF16)))
        gains = links.spread(gain_low).transpose(1, 0, 2).reshape(3, D).astype(F32)

        rank_ids = jnp.concatenate(
            [lax.dynamic_index_in_dim(slot_ids, my_rep ^ r, 0, False) for r in (0, 2, 1, 3)]
        ).reshape(-1)
        quarter_rows = vocab_rows // n_rep
        quarter_start = my_rep * quarter_rows
        rank_ids = rank_ids - quarter_start
        rank_ids = jnp.where((rank_ids >= 0) & (rank_ids < quarter_rows), rank_ids, quarter_rows)
        slot_iota = jnp.arange(rank_ids.shape[0], dtype=jnp.int32)
        before = (rank_ids[None, :] < rank_ids[:, None]) | (
            (rank_ids[None, :] == rank_ids[:, None]) & (slot_iota[None, :] < slot_iota[:, None])
        )
        ranks = jnp.sum(before.astype(jnp.int32), axis=1)
        sorted_ids = jnp.sort(rank_ids)
        edges = jnp.arange(0, quarter_rows + 1, vocab_tile, dtype=jnp.int32)
        starts = jnp.sum((rank_ids[None, :] < edges[:, None]).astype(jnp.int32), axis=1)
        attn_mine, ranks, sorted_ids, starts, gains = lax.optimization_barrier(
            (attn_mine, ranks, sorted_ids, starts, gains)
        )
        attn_other = links.core(attn_mine)
        attn_in = (attn_mine[:, :in_cols], attn_other[:, :in_cols])
        attn_out = (attn_mine[:, in_cols:], attn_other[:, in_cols:])
        mlp_in = mlp_all[:, : 2 * units]
        mlp_out = mlp_all[:, 2 * units :].reshape(n_shard * unit_part, D)

        def times(value, pair):
            return dot(value, pair[0]), dot(value, pair[1])

        def times_back(mine, other, pair):
            return dot(mine, pair[0], ((1,), (1,))) + dot(other, pair[1], ((1,), (1,)))

        normed_one, norm_one_back = jax.vjp(rms_norm, values, gains[0])
        normed_one = normed_one.astype(BF16)
        mixed = in_order(*times(normed_one, attn_in))
        heads_raw = mixed[:, : QUERY + KEY].reshape(tok_rows, HEADS + KV_HEADS, HEAD_DIM)
        rotated, rope_back = jax.vjp(lambda part: rotate(part, positions), heads_raw)
        rotated = rotated.astype(BF16)
        group_size = HEADS // KV_HEADS
        queries = rotated[:, :HEADS].reshape(tok_rows, KV_HEADS, group_size, HEAD_DIM)
        queries = queries.transpose(1, 2, 0, 3).reshape(KV_HEADS, group_size * tok_rows, HEAD_DIM)
        queries = jnp.pad(queries, ((0, 0), (0, 0), (0, HEAD_DIM)))
        vals = mixed[:, QUERY + KEY :].astype(BF16).reshape(tok_rows, KV_HEADS, HEAD_DIM)
        kv = jnp.concatenate([rotated[:, HEADS:], vals], 2).transpose(1, 0, 2)
        kv = links.rep_gather(jnp.concatenate([kv[None], links.all_across(kv)]))
        kv = kv.transpose(2, 0, 1, 3, 4).reshape(KV_HEADS, seq_len, 2 * HEAD_DIM)
        scale = HEAD_DIM ** (-0.5)
        key_places = (
            (jnp.stack([my_rep ^ other for other in (0, 2, 1, 3)]) * wide)[:, None, None]
            + ((links.w - jnp.arange(wide, dtype=jnp.int32)) % wide)[None, :, None]
        ) * tok_rows + jnp.arange(tok_rows, dtype=jnp.int32)
        key_blocks = key_places.reshape(-1) // BLOCK
        query_blocks = jnp.tile(positions // BLOCK, group_size)
        allowed = (key_blocks[None, :] <= query_blocks[:, None])[None]

        def batched(spec, a, b):
            return jnp.einsum(spec, a, b, preferred_element_type=F32)

        scores = jnp.where(allowed, batched("htd,hsd->hts", queries, kv) * scale, -1e30)
        highest = jnp.max(scores, axis=-1, keepdims=True)
        weights = jnp.exp(scores - highest)
        totals = jnp.sum(weights, axis=-1, keepdims=True)
        chances = weights / totals
        chances_low = chances.astype(BF16)
        outputs = batched("hts,hsd->htd", chances_low, kv)[:, :, HEAD_DIM:]

        def to_rows(heads):
            return (
                heads.reshape(KV_HEADS, group_size, tok_rows, HEAD_DIM)
                .transpose(2, 0, 1, 3)
                .reshape(tok_rows, QUERY)
            )

        attended = to_rows(outputs).astype(BF16)
        middle = values + in_order(*times(attended, attn_out))
        normed_two, norm_two_back = jax.vjp(rms_norm, middle, gains[1])
        normed_two = normed_two.astype(BF16)
        normed_all = links.rep_gather_now(normed_two).reshape(-1, D)
        gate_up = dot(normed_all, mlp_in)
        hidden, glu_back = jax.vjp(swiglu, gate_up[:, :units], gate_up[:, units:])
        hidden = hidden.astype(BF16)
        result = middle + links.rep_sum(dot(hidden, mlp_out).reshape(n_rep, tok_rows, D))
        final, final_back = jax.vjp(rms_norm, result, gains[2])

        near = links.line_gather(final.astype(BF16))
        far = links.all_across(near).reshape(-1, D)
        near_targets, far_targets = group_targets[:line_rows], group_targets[line_rows:]
        pair_near = links.chip(near)
        pair_far = links.chip(far)
        near_raised, near_stats = head_logits(near, near_targets, table_low)
        far, near_stats = lax.optimization_barrier((far, near_stats))
        far_raised, far_stats = head_logits(far, far_targets, table_low)
        stats = jnp.concatenate([near_stats, far_stats])[:, :3].T
        high = stats[0]
        stats = stats.reshape(3, wide, LINE, tok_rows)
        ordered = jnp.stack(
            [lax.dynamic_index_in_dim(stats, turn[step], 1, False) for step in range(wide)], 1
        )
        stats = links.spread(ordered)
        top = jnp.max(stats[:, 0], axis=0)
        log_totals = top + jnp.log(jnp.sum(stats[:, 1] * jnp.exp(stats[:, 0] - top), axis=0))
        picked = jnp.sum(stats[:, 2], axis=0)
        losses = log_totals - picked

        def turned(part):
            return jnp.stack(
                [lax.dynamic_index_in_dim(part, turn[step], 0, False) for step in range(wide)]
            ).reshape(-1)

        log_totals = turned(log_totals)
        group_loss = jnp.sum(turned(losses) * group_mask)
        pair_logs = links.chip(log_totals)
        factors = jnp.exp(high - log_totals)
        far_grads, far_part = head_states(
            far_raised, factors[line_rows:], group_weights[line_rows:], far_targets, table_low
        )
        far_sent = far_part
        near_raised, far_part = lax.optimization_barrier((near_raised, far_part))
        near_grads, near_part = head_states(
            near_raised, factors[:line_rows], group_weights[:line_rows], near_targets, table_low
        )

        table_operands = (
            near.T,
            far.T,
            near_grads,
            far_grads,
            pair_near,
            pair_far,
            jnp.stack([pair_logs, pair_weights], axis=1),
            pair_targets,
            table_low,
        )
        sent = head_table(*table_operands, my_rep ^ 1, vocab_tile)
        received = links.core(sent)
        sent, near_part = lax.optimization_barrier((sent, near_part))
        grad_states = links.sum_across(near_part, far_sent)
        grad_final = links.line_sum(grad_states.reshape(LINE, tok_rows, D))
        kept = head_table(*table_operands, my_rep, vocab_tile)
        kept, grad_final = lax.optimization_barrier((kept, grad_final))

        grad_output, grad_gain_three = final_back(grad_final)

        def weight_grad(value, mine, other):
            sent = dot(value, other, ((0,), (0,))).astype(BF16)
            half = dot(value, mine, ((0,), (0,))) + links.core(sent).astype(F32)
            first, second = jnp.split(half, 2, 1)
            sent = links.chip(jnp.where(second_chip, first, second).astype(BF16))
            return (jnp.where(second_chip, second, first) + sent.astype(F32)).astype(BF16)

        pad_rows = -in_rows % 16

        def pad_blocks(value):
            value = value.reshape(-1, n_shard, in_rows)
            value = jnp.pad(value, ((0, 0), (0, 0), (0, pad_rows)))
            return value.reshape(-1, n_shard * (in_rows + pad_rows))

        branch = links.rep_gather_now(grad_output.astype(BF16)).reshape(-1, D)
        grad_mlp_out = dot(hidden, branch, ((0,), (0,))).astype(BF16)
        grad_hidden = dot(branch, mlp_out, ((1,), (1,)))
        grad_glu = jnp.concatenate(glu_back(grad_hidden), 1).astype(BF16)
        grad_mlp_in = dot(pad_blocks(normed_all), grad_glu, ((0,), (0,))).astype(BF16)
        grad_normed_two = dot(grad_glu, mlp_in, ((1,), (1,))).reshape(n_rep, tok_rows, D)
        grad_normed_two = links.rep_sum(grad_normed_two)
        middle_part, grad_gain_two = norm_two_back(grad_normed_two)
        grad_middle = grad_output + middle_part

        grad_mlp = [
            links.scatter(grad_mlp_in)[:in_rows].astype(BF16),
            grad_mlp_out,
        ]

        out_mine, out_other = my_half(grad_middle.astype(BF16))
        grad_attn_out = weight_grad(pad_blocks(attended), out_mine, out_other)
        grad_attended = times_back(out_mine, out_other, attn_out).astype(BF16)
        grad_heads = (
            grad_attended.reshape(tok_rows, KV_HEADS, group_size, HEAD_DIM)
            .transpose(1, 2, 0, 3)
            .reshape(KV_HEADS, group_size * tok_rows, HEAD_DIM)
        )
        deltas = jnp.sum(grad_heads.astype(F32) * outputs, axis=-1, keepdims=True)
        grad_heads = jnp.pad(grad_heads, ((0, 0), (0, 0), (HEAD_DIM, 0)))
        grad_chances = batched("htd,hsd->hts", grad_heads, kv)
        grad_scores = (chances * (grad_chances - deltas)).astype(BF16)
        grad_kv = batched("hts,htd->hsd", grad_scores, queries) * scale
        grad_kv = grad_kv + batched("hts,htd->hsd", chances_low, grad_heads)
        grad_kv = grad_kv.astype(BF16).reshape(KV_HEADS, n_rep, wide, tok_rows, 2 * HEAD_DIM)
        grad_kv = links.rep_sum(grad_kv.transpose(1, 2, 0, 3, 4))
        far_kv = grad_kv[1:].astype(BF16).reshape(-1, tok_rows, 2 * HEAD_DIM)
        grad_kv = links.sum_across(grad_kv[0], far_kv).transpose(1, 0, 2)
        grad_queries = batched("hts,hsd->htd", grad_scores, kv)[:, :, :HEAD_DIM] * scale
        grad_rotated = jnp.concatenate(
            [
                to_rows(grad_queries).reshape(tok_rows, HEADS, HEAD_DIM),
                grad_kv[:, :, :HEAD_DIM],
            ],
            1,
        )
        grad_raw = rope_back(grad_rotated)[0].reshape(tok_rows, QUERY + KEY)
        grad_mixed = jnp.concatenate([grad_raw, grad_kv[:, :, HEAD_DIM:].reshape(tok_rows, KEY)], 1).astype(BF16)
        mixed_mine, mixed_other = my_half(grad_mixed)
        values_part, grad_gain_one = norm_one_back(times_back(mixed_mine, mixed_other, attn_in))
        grad_values = (grad_middle + values_part).astype(BF16)
        grad_gains = jnp.stack([grad_gain_one, grad_gain_two, grad_gain_three], 1)
        grad_gains = grad_gains + links.core(grad_gains)
        grad_gains = pad_blocks((grad_gains + links.chip(grad_gains)).T).T
        grad_values, grad_mlp[0] = lax.optimization_barrier((grad_values, grad_mlp[0]))
        packed = dot(packing, grad_values).astype(BF16).reshape(n_shard, room, D)
        packed = lax.all_to_all(packed, "shard", 0, 0, tiled=True)
        packed, grad_mlp[1] = lax.optimization_barrier((packed, grad_mlp[1]))
        grad_mlp[1] = links.scatter(grad_mlp[1]).astype(BF16).reshape(in_rows, -1)
        rows = packed.reshape(1, n_shard * room, D)
        rows = jnp.concatenate([rows, links.chip(rows)])
        rows, grad_mlp[1], normed_one, grad_attn_out = lax.optimization_barrier(
            (rows, grad_mlp[1], normed_one, grad_attn_out)
        )
        grad_attn_in = weight_grad(pad_blocks(normed_one), mixed_mine, mixed_other)
        grad_small = jnp.concatenate([grad_attn_in, grad_gains.astype(BF16)], 1)
        grad_attn_out = links.scatter(grad_attn_out)[:in_rows].astype(BF16)
        rows = jnp.concatenate([rows, links.core(rows)])
        grad_small = links.scatter(grad_small)[:in_rows].astype(BF16)
        placed = place_rows(kept, received, rows, ranks, sorted_ids, starts, vocab_tile)

        def place_whole(placed, grad_values, kept, received):
            rows = lax.all_gather(lax.all_gather(grad_values, "rep"), "shard")
            ids = local_ids.transpose(1, 0, 2).reshape(-1, tok_rows) - quarter_start
            return place_slowly(kept, received, rows.reshape(-1, tok_rows, D), ids)

        table_sum, table_squares = lax.cond(
            enough, lambda placed, *_: tuple(placed), place_whole, placed, grad_values, kept, received
        )

        parts = [*grad_mlp, grad_attn_out, grad_small[:, :-3]]
        gain_sum = grad_small[:, -3:].astype(F32).T
        squares = jnp.sum(table_squares) + jnp.sum(gain_sum * gain_sum) / n_rep
        for part in parts:
            squares = squares + jnp.sum(jnp.square(part.astype(F32)))
        squares = jnp.sum(lax.all_gather(squares, "rep"))
        squares = jnp.sum(links.spread(jnp.full((8, 128), squares))[:, 0, 0])
        grad_norm = jnp.sqrt(squares)
        clip_scale = CLIP_AT / jnp.maximum(grad_norm, CLIP_AT)

        table_core = links.core(table_sum)
        table_chip = links.chip(table_sum)
        mlp = lax.all_gather(jnp.concatenate(grad_mlp, 1), "rep")
        mlp_in_sum = mlp[:, :, : 2 * units].reshape(n_rep, in_rows, 2, n_shard, unit_part)
        mlp_in_sum = mlp_in_sum.transpose(1, 2, 3, 0, 4).reshape(in_rows, 2 * FF).astype(F32)
        mlp_out_sum = mlp[:, :, 2 * units :].reshape(n_rep * unit_part, D).astype(F32)
        attn = lax.all_gather(jnp.concatenate(parts[2:], 1), "rep")[jnp.array([0, 2, 1, 3])]
        attn = attn.transpose(1, 0, 2).astype(F32)
        out_cols = D // n_rep
        attn_out_sum = attn[:, :, :out_cols].reshape(in_rows, D)
        attn_in_sum = attn[:, :, out_cols:].reshape(in_rows, 2 * in_cols)
        weight_sum = (attn_in_sum, attn_out_sum, mlp_in_sum, mlp_out_sum, gain_sum)
        loss = group_loss + links.core(group_loss)
        loss_sum = loss + links.chip(loss)
        results = [loss_sum, valid_count, grad_norm]
        masters = (
            table_master.T,
            attn_in_master,
            attn_out_master,
            mlp_in_master,
            mlp_out_master,
            gain_master,
        )
        firsts = (
            table_first.T,
            attn_in_first,
            attn_out_first,
            mlp_in_first,
            mlp_out_first,
            gain_first,
        )
        seconds = (
            table_second.T,
            attn_in_second,
            attn_out_second,
            mlp_in_second,
            mlp_out_second,
            gain_second,
        )
        rate_list = rates(seq_len)
        table = (masters[0], firsts[0], seconds[0])
        half = jnp.stack([my_rep, my_rep ^ 1])
        settings = (clip_scale, rate_list[0], vocab_tile)
        new = list(adam(*table, table_sum, table_core, half, *settings))
        olds = [
            tuple(part.reshape(-1, part.shape[-1]) for part in member)
            for member in zip(masters[1:], firsts[1:], seconds[1:], weight_sum)
        ]
        new[0], table_chip = lax.optimization_barrier((new[0], table_chip))
        table_both = links.core(table_chip)
        news = adam_many(olds, clip_scale, rate_list[1:])
        new = adam(*table, table_chip, table_both, half ^ 2, *settings, new)
        results.extend(part.T for part in new)
        for index, new in enumerate(news):
            results.append(new.reshape(masters[1 + index // 4].shape))
        return tuple(results)

    return local


def solution(mesh):
    token = P(("rep", "shard"))
    weight = P(None, "shard", None)
    state = (P("shard", None), weight, weight, weight, weight, P(None, "shard"))
    outs = [P(), P(), P()]
    for spec in state:
        outs.extend([spec] * 4)
    return jax.shard_map(
        build(mesh),
        mesh=mesh,
        in_specs=(token, token, token) + state * 3,
        out_specs=tuple(outs),
        check_vma=False,
    )
```

```python
import functools

import jax
import jax.numpy as jnp
from jax import lax
from jax.experimental import pallas as pl
from jax.experimental.pallas import tpu as pltpu
from jax.sharding import PartitionSpec as P

D = 960
HEADS = 15
KV_HEADS = 5
HEAD_DIM = 64
FF = 2560
BLOCK = 256
STEP = 5
LINE = 4

EPS_NORM = 1e-05
ROPE_BASE = 100000.0
BETA_ONE = 0.5
BETA_TWO = 0.5
DECAY = 0.1
CLIP_AT = 0.01
ADAM_EPS = 1e-08

F32 = jnp.float32
BF16 = jnp.bfloat16
QUERY = HEADS * HEAD_DIM
KEY = KV_HEADS * HEAD_DIM
VMEM = 56 * 1024 * 1024


def rms_norm(values, gain):
    return values * lax.rsqrt(jnp.mean(values * values, axis=-1, keepdims=True) + EPS_NORM) * gain


def rotate(values, positions):
    half_dim = values.shape[-1] // 2
    freqs = ROPE_BASE ** (-2.0 * jnp.arange(half_dim).astype(F32) / values.shape[-1])
    angles = positions.astype(F32)[:, None] * freqs[None, :]
    cosine = jnp.cos(angles)[:, None, :]
    sine = jnp.sin(angles)[:, None, :]
    first_half = values[..., :half_dim]
    second_half = values[..., half_dim:]
    return jnp.concatenate(
        [first_half * cosine - second_half * sine, second_half * cosine + first_half * sine],
        axis=-1,
    )


def swiglu(gate, up):
    return jax.nn.silu(gate) * up


def rates(seq_len):
    out_fan = max(1, HEADS * HEAD_DIM * 16 // seq_len)
    return (
        0.8 * D ** (-0.5),
        0.5 * D ** (-0.5),
        0.5 * out_fan ** (-0.5),
        0.5 * D ** (-0.5),
        0.5 * FF ** (-0.5),
        0.2,
    )


def adam_update(master, first, second, gradient, rate):
    first_new = BETA_ONE * first + (1.0 - BETA_ONE) * gradient
    second_new = BETA_TWO * second + (1.0 - BETA_TWO) * gradient * gradient
    step_size = (
        first_new
        / (1.0 - BETA_ONE**STEP)
        / (jnp.sqrt(second_new / (1.0 - BETA_TWO**STEP)) + ADAM_EPS)
    )
    master_new = master - rate * (step_size + DECAY * master)
    return (master_new, first_new, second_new, master_new.astype(BF16))


def dot(a, b, dims=((1,), (0,))):
    return lax.dot_general(a, b, (dims, ((), ())), preferred_element_type=F32)


def params():
    return pltpu.CompilerParams(vmem_limit_bytes=VMEM)


def whole(shape):
    return pl.BlockSpec(shape, lambda *_: (0,) * len(shape), pipeline_mode=pl.Buffered(1))


def lookup_kernel(ids_ref, table_ref, low_ref, rows_ref, total):
    tile = table_ref.shape[1]
    step = pl.program_id(0)
    low = table_ref[...].astype(BF16)
    low_ref[...] = low
    columns = lax.broadcasted_iota(jnp.int32, (1, tile), 1) + step * tile
    block = min(512, rows_ref.shape[0])
    for start in range(0, rows_ref.shape[0], block):
        rows = pl.ds(start, block)
        pick = jnp.where(ids_ref[rows, :] == columns, 1.0, 0.0).astype(BF16)
        found = dot(pick, low, ((1,), (1,)))

        @pl.when(step == 0)
        def _():
            total[rows, :] = found

        @pl.when(step > 0)
        def _():
            total[rows, :] += found

    @pl.when(step == pl.num_programs(0) - 1)
    def _():
        rows_ref[...] = total[...].astype(BF16)


def lookup(table_t, local_ids, tile=512):
    width, vocab = table_t.shape
    count = local_ids.shape[0]
    return pl.pallas_call(
        lookup_kernel,
        grid=(vocab // tile,),
        in_specs=[
            whole((count, 1)),
            pl.BlockSpec((width, tile), lambda i: (0, i)),
        ],
        out_specs=[
            pl.BlockSpec((width, tile), lambda i: (0, i)),
            whole((count, width)),
        ],
        out_shape=[
            jax.ShapeDtypeStruct((width, vocab), BF16),
            jax.ShapeDtypeStruct((count, width), BF16),
        ],
        scratch_shapes=[pltpu.VMEM((count, width), F32)],
        compiler_params=params(),
        cost_estimate=pl.CostEstimate(
            flops=2 * count * width * vocab, bytes_accessed=6 * width * vocab, transcendentals=0
        ),
    )(local_ids[:, None], table_t)


def logits_kernel(states_ref, targets_ref, table_ref, raised_ref, stats_ref, logits, *, tile):
    vocab = table_ref.shape[1]
    rows = states_ref.shape[0]
    states = states_ref[...]
    high = jnp.full((rows, 1), -jnp.inf, F32)
    for start in range(0, vocab, tile):
        part = dot(states, table_ref[:, start : start + tile])
        logits[:, start : start + tile] = part
        high = jnp.maximum(high, jnp.max(part, axis=-1, keepdims=True))
    total = jnp.zeros((rows, 128), F32)
    picked = jnp.zeros((rows, 128), F32)
    targets = targets_ref[...]
    lanes = lax.broadcasted_iota(jnp.int32, (1, 128), 1)
    for start in range(0, vocab, 128):
        part = logits[:, start : start + 128]
        raised = jnp.exp(part - high)
        raised_ref[:, start : start + 128] = raised.astype(BF16)
        total += raised
        picked += jnp.where(targets == lanes + start, part, 0.0)
    total = jnp.sum(total, axis=-1, keepdims=True)
    picked = jnp.sum(picked, axis=-1, keepdims=True)
    stats_ref[...] = jnp.where(lanes == 0, high, jnp.where(lanes == 1, total, picked))


def head_logits(states, targets, table_low, rows=256, tile=512):
    count, width = states.shape
    vocab = table_low.shape[1]
    return pl.pallas_call(
        functools.partial(logits_kernel, tile=tile),
        grid=(count // rows,),
        in_specs=[
            pl.BlockSpec((rows, width), lambda i: (i, 0)),
            pl.BlockSpec((rows, 1), lambda i: (i, 0)),
            whole((width, vocab)),
        ],
        out_specs=[
            pl.BlockSpec((rows, vocab), lambda i: (i, 0)),
            pl.BlockSpec((rows, 128), lambda i: (i, 0)),
        ],
        out_shape=[
            jax.ShapeDtypeStruct((count, vocab), BF16),
            jax.ShapeDtypeStruct((count, 128), F32),
        ],
        scratch_shapes=[pltpu.VMEM((rows, vocab), F32)],
        compiler_params=params(),
        cost_estimate=pl.CostEstimate(
            flops=2 * count * width * vocab,
            bytes_accessed=2 * vocab * (width + count),
            transcendentals=count * vocab,
        ),
    )(states, targets[:, None], table_low)


def states_kernel(raised_ref, scales_ref, targets_ref, table_ref, grads_ref, out_ref, *, tile):
    vocab = table_ref.shape[1]
    weight = scales_ref[:, 1:2]
    factor = scales_ref[:, 0:1]
    targets = targets_ref[...]
    total = None
    for start in range(0, vocab, tile):
        lanes = lax.broadcasted_iota(jnp.int32, (1, tile), 1) + start
        chances = raised_ref[:, start : start + tile].astype(F32) * factor
        part = (jnp.where(targets == lanes, chances - weight, chances)).astype(BF16)
        grads_ref[:, start : start + tile] = part
        found = dot(part, table_ref[:, start : start + tile], ((1,), (1,)))
        total = found if total is None else total + found
    out_ref[...] = total.astype(BF16)


def head_states(raised, factors, weights, targets, table_low, rows=256, tile=512):
    count, vocab = raised.shape
    width = table_low.shape[0]
    scales = jnp.stack([factors * weights, weights], axis=1)
    return pl.pallas_call(
        functools.partial(states_kernel, tile=tile),
        grid=(count // rows,),
        in_specs=[
            pl.BlockSpec((rows, vocab), lambda i: (i, 0)),
            pl.BlockSpec((rows, 2), lambda i: (i, 0)),
            pl.BlockSpec((rows, 1), lambda i: (i, 0)),
            whole((width, vocab)),
        ],
        out_specs=[
            pl.BlockSpec((rows, vocab), lambda i: (i, 0)),
            pl.BlockSpec((rows, width), lambda i: (i, 0)),
        ],
        out_shape=[
            jax.ShapeDtypeStruct((count, vocab), BF16),
            jax.ShapeDtypeStruct((count, width), BF16),
        ],
        compiler_params=params(),
        cost_estimate=pl.CostEstimate(
            flops=2 * count * width * vocab,
            bytes_accessed=2 * vocab * (width + 2 * count),
            transcendentals=0,
        ),
    )(raised, scales, targets[:, None], table_low)


def table_kernel(
    part_ref,
    near_t,
    far_t,
    near_pair_t,
    far_pair_t,
    near_grads,
    far_grads,
    near_pair,
    far_pair,
    scales,
    targets,
    table_ref,
    out_ref,
):
    tile = out_ref.shape[1]
    step = part_ref[0] * pl.num_programs(0) + pl.program_id(0)
    columns = lax.broadcasted_iota(jnp.int32, (1, tile), 1) + step * tile
    total = dot(near_t[...], near_grads[...]) + dot(far_t[...], far_grads[...])
    offset = 0
    for pair, pair_t in ((near_pair, near_pair_t), (far_pair, far_pair_t)):
        block = min(512, pair.shape[0])
        for start in range(0, pair.shape[0], block):
            rows = slice(offset + start, offset + start + block)
            weight = scales[rows, 1:2]
            logits = dot(pair[start : start + block, :], table_ref[...])
            chances = jnp.exp(logits - scales[rows, 0:1]) * weight
            grads = jnp.where(targets[rows, :] == columns, chances - weight, chances)
            total += dot(pair_t[:, start : start + block], grads.astype(BF16))
        offset += pair.shape[0]
    out_ref[...] = total.astype(BF16)


def head_table(
    near_t,
    far_t,
    near_grads,
    far_grads,
    near_pair,
    far_pair,
    scales,
    targets,
    table_low,
    part,
    tile,
):
    width, near = near_t.shape
    far = far_t.shape[1]
    both = near + far
    vocab = near_grads.shape[1] // 4
    steps = vocab // tile

    def column(i, part):
        return (0, part[0] * steps + i)

    return pl.pallas_call(
        table_kernel,
        grid_spec=pltpu.PrefetchScalarGridSpec(
            num_scalar_prefetch=1,
            grid=(steps,),
            in_specs=[
                whole((width, near)),
                whole((width, far)),
                whole((width, near)),
                whole((width, far)),
                pl.BlockSpec((near, tile), column),
                pl.BlockSpec((far, tile), column),
                whole((near, width)),
                whole((far, width)),
                whole((both, 2)),
                whole((both, 1)),
                pl.BlockSpec((width, tile), column),
            ],
            out_specs=pl.BlockSpec((width, tile), lambda i, part: (0, i)),
        ),
        out_shape=jax.ShapeDtypeStruct((width, vocab), BF16),
        compiler_params=params(),
        cost_estimate=pl.CostEstimate(
            flops=6 * both * width * vocab,
            bytes_accessed=2 * (2 * vocab + 3 * both) * width + 2 * vocab * both,
            transcendentals=both * vocab,
        ),
    )(
        jnp.reshape(part, (1,)).astype(jnp.int32),
        near_t,
        far_t,
        near_pair.T,
        far_pair.T,
        near_grads,
        far_grads,
        near_pair,
        far_pair,
        scales,
        targets[:, None],
        table_low,
    )


def place_kernel(
    starts_ref,
    ranks_ref,
    ids_ref,
    *refs,
    chunk,
    block,
):
    rows_refs = refs[:-6]
    kept_ref, received_ref, out_ref, square_ref, sorted_rows, total = refs[-6:]
    step = pl.program_id(0)
    tile = out_ref.shape[1]
    lanes = rows_refs[0].shape[0]

    @pl.when(step == 0)
    def _():
        def sort(k, carry):
            columns = pl.ds(pl.multiple_of(k * block, block), block)
            wanted = lax.broadcasted_iota(jnp.int32, (1, block), 1) + k * block
            found = None
            for source, rows_ref in enumerate(rows_refs):
                pick = ranks_ref[source * lanes : (source + 1) * lanes, :] == wanted
                pick = jnp.where(pick, 1.0, 0.0).astype(BF16)
                part = dot(rows_ref[...], pick, ((0,), (0,)))
                found = part if found is None else found + part
            sorted_rows[:, columns] = found.astype(BF16)
            return carry

        lax.fori_loop(0, (starts_ref[pl.num_programs(0)] + block - 1) // block, sort, 0)

    first = starts_ref[step]
    last = starts_ref[step + 1]
    total[...] = kept_ref[...].astype(F32) + received_ref[...].astype(F32)
    columns = lax.broadcasted_iota(jnp.int32, (1, tile), 1) + step * tile

    def add(k, carry):
        rows = pl.ds(pl.multiple_of(k * chunk, chunk), chunk)
        place = lax.broadcasted_iota(jnp.int32, (chunk, 1), 0) + k * chunk
        ids = ids_ref[rows, :]
        inside = jnp.logical_and(place >= first, place < last)
        pick = jnp.where(jnp.logical_and(ids == columns, inside), 1.0, 0.0).astype(BF16)
        total[...] += dot(sorted_rows[:, rows], pick)
        return carry

    lax.fori_loop(first // chunk, (last + chunk - 1) // chunk, add, 0)
    low = total[...].astype(BF16)
    out_ref[...] = low
    value = low.astype(F32)
    squares = jnp.sum(value * value, axis=0, keepdims=True)
    part = jnp.zeros((1, 128), F32)
    for start in range(0, tile, 128):
        part += squares[:, start : start + 128]

    @pl.when(step == 0)
    def _():
        square_ref[...] = part

    @pl.when(step > 0)
    def _():
        square_ref[...] += part


def place_rows(kept, received, rows, ranks, ids, starts, tile, chunk=128, block=256):
    width, columns = kept.shape
    lanes = rows[0].shape[0]
    total = len(rows) * lanes
    block = min(block, total)
    spec = pl.BlockSpec((width, tile), lambda i, starts: (0, i))
    return pl.pallas_call(
        functools.partial(place_kernel, chunk=chunk, block=block),
        grid_spec=pltpu.PrefetchScalarGridSpec(
            num_scalar_prefetch=1,
            grid=(columns // tile,),
            in_specs=[whole((total, 1)), whole((total, 1))]
            + [whole((lanes, width))] * len(rows)
            + [spec] * 2,
            out_specs=[spec, whole((1, 128))],
            scratch_shapes=[pltpu.VMEM((width, total), BF16), pltpu.VMEM((width, tile), F32)],
        ),
        out_shape=[
            jax.ShapeDtypeStruct((width, columns), BF16),
            jax.ShapeDtypeStruct((1, 128), F32),
        ],
        compiler_params=params(),
        cost_estimate=pl.CostEstimate(
            flops=2 * 4 * chunk * tile * width,
            bytes_accessed=6 * width * columns + 2 * total * width,
            transcendentals=0,
        ),
    )(starts, ranks[:, None], ids[:, None], *rows, kept, received)


def adam_kernel(quarters_ref, scale_ref, w_ref, m_ref, v_ref, *refs, rate, count):
    grads, outs = refs[:count], refs[-4:]
    part = pl.program_id(0) // (pl.num_programs(0) // count)
    for index, ref in enumerate(grads):

        @pl.when(part == index)
        def _(ref=ref):
            gradient = ref[...].astype(F32) * scale_ref[0]
            new = adam_update(w_ref[...], m_ref[...], v_ref[...], gradient, rate)
            for out, value in zip(outs, new):
                out[...] = value


def adam(master, first, second, grads, quarters, scale, rate, tile, before=()):
    rows, columns = master.shape
    count = len(grads)
    steps = grads[0].shape[1] // tile

    def column(i, quarters):
        return (0, quarters[i // steps] * steps + i % steps)

    def own(index):
        return lambda i, quarters: (0, jnp.clip(i - index * steps, 0, steps - 1))

    spec = pl.BlockSpec((rows, tile), column)
    shape = jax.ShapeDtypeStruct((rows, columns), F32)
    return pl.pallas_call(
        functools.partial(adam_kernel, rate=rate, count=count),
        grid_spec=pltpu.PrefetchScalarGridSpec(
            num_scalar_prefetch=1,
            grid=(count * steps,),
            in_specs=[pl.BlockSpec(memory_space=pltpu.SMEM)]
            + [spec] * 3
            + [pl.BlockSpec((rows, tile), own(index)) for index in range(count)]
            + [pl.BlockSpec(memory_space=pl.ANY)] * len(before),
            out_specs=[spec] * 4,
        ),
        out_shape=[shape] * 3 + [jax.ShapeDtypeStruct((rows, columns), BF16)],
        input_output_aliases={5 + count + k: k for k in range(len(before))},
        compiler_params=params(),
        cost_estimate=pl.CostEstimate(flops=0, bytes_accessed=0, transcendentals=0),
    )(
        jnp.stack(quarters).astype(jnp.int32),
        jnp.reshape(scale, (1,)),
        master,
        first,
        second,
        *grads,
        *before,
    )


def adam_many_kernel(scale_ref, *refs, rates):
    count = len(rates)
    inputs, outputs = refs[: 4 * count], refs[4 * count :]
    scale = scale_ref[0]
    for member, rate in enumerate(rates):
        olds = inputs[4 * member : 4 * member + 4]
        news = outputs[4 * member : 4 * member + 4]
        rows = olds[0].shape[0]
        block = 8 if rows % 8 == 0 else rows

        def update(k, carry, olds=olds, news=news, block=block, rate=rate):
            place = pl.ds(pl.multiple_of(k * block, block), block)
            w, m, v, g = (ref[place, :] for ref in olds)
            for ref, value in zip(news, adam_update(w, m, v, g.astype(F32) * scale, rate)):
                ref[place, :] = value
            return carry

        lax.fori_loop(0, rows // block, update, 0)


def adam_many(olds, scale, rates, steps=5):
    if any(master.shape[0] % (8 * steps) for master, *_ in olds[:-1]):
        steps = 1
    shapes, specs = [], []
    for index, (master, *_) in enumerate(olds):
        rows, columns = master.shape
        shapes += [jax.ShapeDtypeStruct(master.shape, F32)] * 3
        shapes += [jax.ShapeDtypeStruct(master.shape, BF16)]
        if index < len(olds) - 1:
            specs += [pl.BlockSpec((rows // steps, columns), lambda i: (i, 0))] * 4
        else:
            specs += [pl.BlockSpec((rows, columns), lambda i: (0, 0))] * 4
    return pl.pallas_call(
        functools.partial(adam_many_kernel, rates=rates),
        grid=(steps,),
        in_specs=[pl.BlockSpec(memory_space=pltpu.SMEM)] + specs,
        out_specs=specs,
        out_shape=shapes,
        compiler_params=params(),
        cost_estimate=pl.CostEstimate(flops=0, bytes_accessed=0, transcendentals=0),
    )(jnp.reshape(scale, (1,)), *[part for member in olds for part in member])


def place_slowly(kept, received, rows, ids):
    columns = jnp.arange(kept.shape[1], dtype=jnp.int32)

    def add(total, operands):
        part, part_ids = operands
        pick = (part_ids[:, None] == columns[None, :]).astype(BF16)
        return total + dot(part, pick, ((0,), (0,))), None

    total, _ = lax.scan(add, kept.astype(F32) + received.astype(F32), (rows, ids))
    total = total.astype(BF16)
    squares = jnp.sum(jnp.square(total.astype(F32)))
    return total, jnp.full((1, 128), squares / 128)


class Links:
    def __init__(self, n_shard, n_rep):
        self.n = n_shard
        self.wide = n_shard // LINE
        self.n_rep = n_rep
        me = lax.axis_index("shard")
        self.z = me // self.wide
        self.w = me % self.wide
        self.lines = [[z * self.wide + w for z in range(LINE)] for w in range(self.wide)]

    def across(self, value, step):
        pairs = [
            (z * self.wide + w, z * self.wide + (w + step) % self.wide)
            for z in range(LINE)
            for w in range(self.wide)
        ]
        return lax.ppermute(value, "shard", pairs)

    def all_across(self, value):
        return jnp.stack([self.across(value, step) for step in range(1, self.wide)])

    def sum_across(self, near, far):
        rows = near.shape[0]
        total = near.astype(F32)
        for step in range(1, self.wide):
            part = far[(step - 1) * rows : step * rows] if self.wide > 2 else far
            total = total + self.across(part, -step).astype(F32)
        return total

    def line_gather(self, value):
        return lax.all_gather(value, "shard", axis_index_groups=self.lines, tiled=True)

    def line_sum(self, value):
        parts = lax.all_to_all(
            value.astype(BF16), "shard", 0, 0, axis_index_groups=self.lines, tiled=True
        )
        return jnp.sum(parts.astype(F32), axis=0)

    def scatter(self, value):
        value = value.reshape((self.n, -1) + value.shape[1:])
        parts = lax.all_to_all(value, "shard", 0, 0, tiled=True)
        return jnp.sum(parts.astype(F32), axis=0)

    def spread(self, value):
        many = jnp.broadcast_to(value[None], (self.n,) + value.shape)
        return lax.all_to_all(many, "shard", 0, 0, tiled=True)

    def core(self, value):
        return lax.ppermute(value, "rep", [(r, r ^ 1) for r in range(self.n_rep)])

    def rep_gather(self, value):
        value = value[None]
        value = jnp.concatenate([value, self.chip(value)])
        return jnp.concatenate([value, self.core(value)])

    def in_turn(self, value, back=False):
        rep = lax.axis_index("rep")
        places = [rep ^ k for k in (0, 2, 1, 3)]
        if back:
            places = [(rep ^ k) % 2 * 2 + (rep ^ k) // 2 for k in range(4)]
        return [lax.dynamic_index_in_dim(value, place, 0, False) for place in places]

    def rep_scatter(self, value):
        parts = lax.all_to_all(value.astype(BF16), "rep", 0, 0, tiled=True)
        return jnp.sum(parts.astype(F32), axis=0)

    def rep_sum(self, value):
        value = value.astype(BF16)
        mine = value[:2].astype(F32) + self.core(value[2:]).astype(F32)
        return mine[0] + self.chip(mine[1].astype(BF16)).astype(F32)

    def chip(self, value):
        return lax.ppermute(value, "rep", [(r, r ^ 2) for r in range(self.n_rep)])


def build(mesh):
    n_shard = mesh.shape["shard"]
    n_rep = mesh.shape["rep"]

    def local(
        token_ids,
        target_ids,
        loss_mask,
        table_master,
        attn_in_master,
        attn_out_master,
        mlp_in_master,
        mlp_out_master,
        gain_master,
        table_first,
        attn_in_first,
        attn_out_first,
        mlp_in_first,
        mlp_out_first,
        gain_first,
        table_second,
        attn_in_second,
        attn_out_second,
        mlp_in_second,
        mlp_out_second,
        gain_second,
    ):
        links = Links(n_shard, n_rep)
        my_rep = lax.axis_index("rep")
        my_shard = lax.axis_index("shard")
        second_core = (my_rep % 2) == 1
        second_chip = (my_rep // 2) == 1
        tok_rows = token_ids.shape[0]
        seq_len = n_shard * tok_rows
        vocab_rows = table_master.shape[0]
        vocab_start = my_shard * vocab_rows
        wide = n_shard // LINE
        line_rows = LINE * tok_rows

        def in_order(mine, other, axis=-1):
            return jnp.where(
                second_core,
                jnp.concatenate([other, mine], axis),
                jnp.concatenate([mine, other], axis),
            )

        def my_half(value, axis=-1):
            first, second = jnp.split(value, 2, axis)
            return jnp.where(second_core, second, first), jnp.where(second_core, first, second)

        def halves(master):
            return my_half(master[0].astype(BF16))[0]

        in_rows = D // n_shard
        in_cols = attn_in_master.shape[2] // 2
        attn_part = jnp.concatenate([halves(attn_in_master), halves(attn_out_master)], 1)

        packed = jnp.stack([token_ids, target_ids, loss_mask])
        packed, attn_part = lax.optimization_barrier((packed, attn_part))
        everyone = links.spread(lax.all_gather(packed, "rep")).transpose(1, 0, 2, 3)
        everyone = everyone.reshape(LINE, n_rep, wide, 3, tok_rows).transpose(1, 0, 2, 3, 4)
        valid_count = jnp.sum(everyone[:, :, :, 2].astype(F32))
        turn = [(links.w - step) % wide for step in range(wide)]

        def group_of(rep):
            group = lax.dynamic_index_in_dim(everyone, rep, 0, False)
            group = jnp.stack(
                [lax.dynamic_index_in_dim(group, turn[step], 1, False) for step in range(wide)]
            )
            targets = group[:, :, 1].reshape(-1) - vocab_start
            return targets, group[:, :, 2].reshape(-1).astype(F32)

        group_targets, group_mask = group_of(my_rep)
        pair_targets, pair_mask = group_of(my_rep ^ 2)
        group_weights = group_mask / valid_count
        pair_weights = pair_mask / valid_count
        place_block = my_rep * wide + links.w
        positions = place_block * tok_rows + jnp.arange(tok_rows, dtype=jnp.int32)

        unit_rows = FF // n_shard
        unit_part = unit_rows // n_rep
        units = n_shard * unit_part
        mlp_in_part = mlp_in_master[0].astype(BF16)
        mlp_in_part = mlp_in_part.reshape(-1, 2, n_shard, n_rep, unit_part)
        mlp_in_part = lax.dynamic_index_in_dim(mlp_in_part, my_rep, 3, False).reshape(-1, 2 * units)
        mlp_out_part = mlp_out_master[0].astype(BF16).reshape(n_rep, unit_part, D)
        mlp_out_part = lax.dynamic_index_in_dim(mlp_out_part, my_rep, 0, False)
        mlp_part = jnp.concatenate([mlp_in_part, mlp_out_part.reshape(in_rows, -1)], 1)
        attn_mine = lax.all_gather(attn_part, "shard", tiled=True)

        room = min(64, tok_rows)
        vocab_tile = min(512, vocab_rows // 4)
        all_ids = everyone[:, :, :, 0].reshape(n_rep, n_shard, tok_rows)
        earlier = jnp.tril(jnp.ones((tok_rows, tok_rows), BF16), -1)

        def places(inside):
            found = jnp.einsum(
                "...j,ij->...i", inside.astype(BF16), earlier, preferred_element_type=F32
            )
            return jnp.where(inside, found.astype(jnp.int32), -1)

        owners = jnp.arange(n_shard, dtype=jnp.int32)
        owned = (all_ids // vocab_rows)[:, :, None, :] == owners[:, None]
        enough = jnp.max(jnp.sum(owned.astype(jnp.int32), -1)) <= room
        local_ids = all_ids - vocab_start
        inside = (local_ids >= 0) & (local_ids < vocab_rows)
        room_iota = jnp.arange(room, dtype=jnp.int32)
        slots = places(inside)
        slot_ids = jnp.max(
            jnp.where(slots[:, :, None, :] == room_iota[:, None], local_ids[:, :, None, :], -1), -1
        )
        slot_ids = jnp.where(slot_ids < 0, vocab_rows, slot_ids)
        own_ids = lax.dynamic_index_in_dim(
            lax.dynamic_index_in_dim(all_ids, my_rep, 0, False), my_shard, 0, False
        )
        own_slots = places((own_ids // vocab_rows)[None, :] == owners[:, None])
        packing = (own_slots[:, None, :] == room_iota[:, None]).astype(BF16).reshape(-1, tok_rows)

        my_slots = lax.dynamic_index_in_dim(slot_ids, my_rep, 0, False).reshape(-1)
        table_low, looked = lookup(table_master.T, my_slots, min(512, vocab_rows))

        looked, mlp_part = lax.optimization_barrier((looked, mlp_part))
        mlp_all = lax.all_gather(mlp_part, "shard", tiled=True)
        packed = lax.all_to_all(looked.reshape(n_shard, room, D), "shard", 0, 0, tiled=True)
        packed = dot(packing, packed.reshape(-1, D), ((0,), (0,)))

        def read_whole(packed, table_low):
            ids = lax.dynamic_index_in_dim(local_ids, my_rep, 0, False).reshape(-1)
            columns = jnp.arange(vocab_rows, dtype=jnp.int32)
            pick = (ids[:, None] == columns[None, :]).astype(BF16)
            rows = dot(pick, table_low, ((1,), (1,))).astype(BF16)
            rows = lax.all_to_all(rows.reshape(n_shard, tok_rows, D), "shard", 0, 0, tiled=True)
            return jnp.sum(rows.astype(F32), axis=0)

        values = lax.cond(enough, lambda packed, _: packed, read_whole, packed, table_low)
        values, gain_low = lax.optimization_barrier((values, gain_master.astype(BF16)))
        gains = links.spread(gain_low).transpose(1, 0, 2).reshape(3, D).astype(F32)

        rank_ids = jnp.concatenate(
            [lax.dynamic_index_in_dim(slot_ids, my_rep ^ r, 0, False) for r in (0, 2, 1, 3)]
        ).reshape(-1)
        quarter_rows = vocab_rows // n_rep
        quarter_start = my_rep * quarter_rows
        rank_ids = rank_ids - quarter_start
        rank_ids = jnp.where((rank_ids >= 0) & (rank_ids < quarter_rows), rank_ids, quarter_rows)
        slot_iota = jnp.arange(rank_ids.shape[0], dtype=jnp.int32)
        before = (rank_ids[None, :] < rank_ids[:, None]) | (
            (rank_ids[None, :] == rank_ids[:, None]) & (slot_iota[None, :] < slot_iota[:, None])
        )
        ranks = jnp.sum(before.astype(jnp.int32), axis=1)
        sorted_ids = jnp.sort(rank_ids)
        edges = jnp.arange(0, quarter_rows + 1, vocab_tile, dtype=jnp.int32)
        starts = jnp.sum((rank_ids[None, :] < edges[:, None]).astype(jnp.int32), axis=1)
        attn_mine, ranks, sorted_ids, starts, gains = lax.optimization_barrier(
            (attn_mine, ranks, sorted_ids, starts, gains)
        )
        attn_other = links.core(attn_mine)
        attn_in = (attn_mine[:, :in_cols], attn_other[:, :in_cols])
        attn_out = (attn_mine[:, in_cols:], attn_other[:, in_cols:])
        mlp_in = mlp_all[:, : 2 * units]
        mlp_out = mlp_all[:, 2 * units :].reshape(n_shard * unit_part, D)
        def times(value, pair):
            return dot(value, pair[0]), dot(value, pair[1])

        def times_back(mine, other, pair):
            return dot(mine, pair[0], ((1,), (1,))) + dot(other, pair[1], ((1,), (1,)))

        normed_one, norm_one_back = jax.vjp(rms_norm, values, gains[0])
        normed_one = normed_one.astype(BF16)
        mixed = in_order(*times(normed_one, attn_in))
        heads_raw = mixed[:, : QUERY + KEY].reshape(tok_rows, HEADS + KV_HEADS, HEAD_DIM)
        rotated, rope_back = jax.vjp(lambda part: rotate(part, positions), heads_raw)
        rotated = rotated.astype(BF16)
        group_size = HEADS // KV_HEADS
        queries = rotated[:, :HEADS].reshape(tok_rows, KV_HEADS, group_size, HEAD_DIM)
        queries = queries.transpose(1, 2, 0, 3).reshape(KV_HEADS, group_size * tok_rows, HEAD_DIM)
        queries = jnp.pad(queries, ((0, 0), (0, 0), (0, HEAD_DIM)))
        vals = mixed[:, QUERY + KEY :].astype(BF16).reshape(tok_rows, KV_HEADS, HEAD_DIM)
        kv = jnp.concatenate([rotated[:, HEADS:], vals], 2).transpose(1, 0, 2)
        kv = links.rep_gather(jnp.concatenate([kv[None], links.all_across(kv)]))
        kv = kv.transpose(2, 0, 1, 3, 4).reshape(KV_HEADS, seq_len, 2 * HEAD_DIM)
        scale = HEAD_DIM ** (-0.5)
        key_places = (
            (jnp.stack([my_rep ^ other for other in (0, 2, 1, 3)]) * wide)[:, None, None]
            + ((links.w - jnp.arange(wide, dtype=jnp.int32)) % wide)[None, :, None]
        ) * tok_rows + jnp.arange(tok_rows, dtype=jnp.int32)
        key_blocks = key_places.reshape(-1) // BLOCK
        query_blocks = jnp.tile(positions // BLOCK, group_size)
        allowed = (key_blocks[None, :] <= query_blocks[:, None])[None]

        def batched(spec, a, b):
            return jnp.einsum(spec, a, b, preferred_element_type=F32)

        scores = jnp.where(allowed, batched("htd,hsd->hts", queries, kv) * scale, -1e30)
        highest = jnp.max(scores, axis=-1, keepdims=True)
        weights = jnp.exp(scores - highest)
        totals = jnp.sum(weights, axis=-1, keepdims=True)
        chances = weights / totals
        chances_low = chances.astype(BF16)
        outputs = batched("hts,hsd->htd", chances_low, kv)[:, :, HEAD_DIM:]

        def to_rows(heads):
            return (
                heads.reshape(KV_HEADS, group_size, tok_rows, HEAD_DIM)
                .transpose(2, 0, 1, 3)
                .reshape(tok_rows, QUERY)
            )

        attended = to_rows(outputs).astype(BF16)
        middle = values + in_order(*times(attended, attn_out))
        normed_two, norm_two_back = jax.vjp(rms_norm, middle, gains[1])
        normed_two = normed_two.astype(BF16)
        normed_all = lax.all_gather(normed_two, "rep", tiled=True)
        gate_up = dot(normed_all, mlp_in)
        hidden, glu_back = jax.vjp(swiglu, gate_up[:, :units], gate_up[:, units:])
        hidden = hidden.astype(BF16)
        result = middle + links.rep_scatter(dot(hidden, mlp_out).reshape(n_rep, tok_rows, D))
        final, final_back = jax.vjp(rms_norm, result, gains[2])

        near = links.line_gather(final.astype(BF16))
        far = links.all_across(near).reshape(-1, D)
        near_targets, far_targets = group_targets[:line_rows], group_targets[line_rows:]
        pair_near = links.chip(near)
        pair_far = links.chip(far)
        near_raised, near_stats = head_logits(near, near_targets, table_low)
        far, near_stats = lax.optimization_barrier((far, near_stats))
        far_raised, far_stats = head_logits(far, far_targets, table_low)
        stats = jnp.concatenate([near_stats, far_stats])[:, :3].T
        high = stats[0]
        stats = stats.reshape(3, wide, LINE, tok_rows)
        ordered = jnp.stack(
            [lax.dynamic_index_in_dim(stats, turn[step], 1, False) for step in range(wide)], 1
        )
        stats = links.spread(ordered)
        top = jnp.max(stats[:, 0], axis=0)
        log_totals = top + jnp.log(jnp.sum(stats[:, 1] * jnp.exp(stats[:, 0] - top), axis=0))
        picked = jnp.sum(stats[:, 2], axis=0)
        losses = log_totals - picked

        def turned(part):
            return jnp.stack(
                [lax.dynamic_index_in_dim(part, turn[step], 0, False) for step in range(wide)]
            ).reshape(-1)

        log_totals = turned(log_totals)
        group_loss = jnp.sum(turned(losses) * group_mask)
        pair_logs = links.chip(log_totals)
        factors = jnp.exp(high - log_totals)
        far_grads, far_part = head_states(
            far_raised, factors[line_rows:], group_weights[line_rows:], far_targets, table_low
        )
        far_sent = far_part
        near_raised, far_part = lax.optimization_barrier((near_raised, far_part))
        near_grads, near_part = head_states(
            near_raised, factors[:line_rows], group_weights[:line_rows], near_targets, table_low
        )

        table_operands = (
            near.T,
            far.T,
            near_grads,
            far_grads,
            pair_near,
            pair_far,
            jnp.stack([pair_logs, pair_weights], axis=1),
            pair_targets,
            table_low,
        )
        sent = head_table(*table_operands, my_rep ^ 1, vocab_tile)
        received = links.core(sent)
        sent, near_part = lax.optimization_barrier((sent, near_part))
        grad_states = links.sum_across(near_part, far_sent)
        grad_final = links.line_sum(grad_states.reshape(LINE, tok_rows, D))
        kept = head_table(*table_operands, my_rep, vocab_tile)
        kept, grad_final = lax.optimization_barrier((kept, grad_final))

        grad_output, grad_gain_three = final_back(grad_final)

        def weight_grad(value, mine, other):
            sent = dot(value, other, ((0,), (0,))).astype(BF16)
            half = dot(value, mine, ((0,), (0,))) + links.core(sent).astype(F32)
            first, second = jnp.split(half, 2, 1)
            sent = links.chip(jnp.where(second_chip, first, second).astype(BF16))
            return (jnp.where(second_chip, second, first) + sent.astype(F32)).astype(BF16)

        pad_rows = -in_rows % 16

        def pad_blocks(value):
            value = value.reshape(-1, n_shard, in_rows)
            value = jnp.pad(value, ((0, 0), (0, 0), (0, pad_rows)))
            return value.reshape(-1, n_shard * (in_rows + pad_rows))

        branch = lax.all_gather(grad_output.astype(BF16), "rep", tiled=True)
        grad_mlp_out = dot(hidden, branch, ((0,), (0,))).astype(BF16)
        grad_hidden = dot(branch, mlp_out, ((1,), (1,)))
        grad_glu = jnp.concatenate(glu_back(grad_hidden), 1).astype(BF16)
        grad_mlp_in = dot(pad_blocks(normed_all), grad_glu, ((0,), (0,))).astype(BF16)
        grad_normed_two = dot(grad_glu, mlp_in, ((1,), (1,))).reshape(n_rep, tok_rows, D)
        turns = links.in_turn(grad_normed_two)
        sent = links.core(jnp.stack(turns[2:]).astype(BF16)).astype(F32)
        passed = links.chip((turns[1] + sent[1]).astype(BF16))
        grad_normed_two = turns[0] + sent[0] + passed.astype(F32)
        middle_part, grad_gain_two = norm_two_back(grad_normed_two)
        grad_middle = grad_output + middle_part

        grad_mlp = [grad_mlp_in, grad_mlp_out.reshape(grad_mlp_in.shape[0], -1)]
        grad_mlp = lax.psum_scatter(jnp.concatenate(grad_mlp, 1), "shard", tiled=True)

        out_mine, out_other = my_half(grad_middle.astype(BF16))
        grad_attn_out = weight_grad(pad_blocks(attended), out_mine, out_other)
        grad_attended = times_back(out_mine, out_other, attn_out).astype(BF16)
        grad_heads = (
            grad_attended.reshape(tok_rows, KV_HEADS, group_size, HEAD_DIM)
            .transpose(1, 2, 0, 3)
            .reshape(KV_HEADS, group_size * tok_rows, HEAD_DIM)
        )
        deltas = jnp.sum(grad_heads.astype(F32) * outputs, axis=-1, keepdims=True)
        grad_heads = jnp.pad(grad_heads, ((0, 0), (0, 0), (HEAD_DIM, 0)))
        grad_chances = batched("htd,hsd->hts", grad_heads, kv)
        grad_scores = (chances * (grad_chances - deltas)).astype(BF16)
        grad_kv = batched("hts,htd->hsd", grad_scores, queries) * scale
        grad_kv = grad_kv + batched("hts,htd->hsd", chances_low, grad_heads)
        grad_kv = grad_kv.astype(BF16).reshape(KV_HEADS, n_rep, wide, tok_rows, 2 * HEAD_DIM)
        grad_kv = links.rep_sum(grad_kv.transpose(1, 2, 0, 3, 4))
        far_kv = grad_kv[1:].astype(BF16).reshape(-1, tok_rows, 2 * HEAD_DIM)
        grad_kv = links.sum_across(grad_kv[0], far_kv).transpose(1, 0, 2)
        grad_queries = batched("hts,hsd->htd", grad_scores, kv)[:, :, :HEAD_DIM] * scale
        grad_rotated = jnp.concatenate(
            [
                to_rows(grad_queries).reshape(tok_rows, HEADS, HEAD_DIM),
                grad_kv[:, :, :HEAD_DIM],
            ],
            1,
        )
        grad_raw = rope_back(grad_rotated)[0].reshape(tok_rows, QUERY + KEY)
        grad_mixed = jnp.concatenate([grad_raw, grad_kv[:, :, HEAD_DIM:].reshape(tok_rows, KEY)], 1).astype(BF16)
        mixed_mine, mixed_other = my_half(grad_mixed)
        values_part, grad_gain_one = norm_one_back(times_back(mixed_mine, mixed_other, attn_in))
        grad_values = (grad_middle + values_part).astype(BF16)
        grad_gains = jnp.stack([grad_gain_one, grad_gain_two, grad_gain_three], 1)
        grad_gains = grad_gains + links.core(grad_gains)
        grad_gains = pad_blocks((grad_gains + links.chip(grad_gains)).T).T
        packed = dot(packing, grad_values).astype(BF16).reshape(n_shard, room, D)
        packed = lax.all_to_all(packed, "shard", 0, 0, tiled=True)
        grad_attn_in = weight_grad(pad_blocks(normed_one), mixed_mine, mixed_other)
        grad_attn = jnp.concatenate([grad_attn_out, grad_attn_in, grad_gains.astype(BF16)], 1)
        packed, grad_attn = lax.optimization_barrier((packed, grad_attn))
        packed = packed.reshape(n_shard * room, D)
        across = links.chip(packed)
        grad_attn = links.scatter(grad_attn)[:in_rows].astype(BF16)
        across, grad_mlp = lax.optimization_barrier((across, grad_mlp))
        grad_mlp_in = grad_mlp[:in_rows, : 2 * units]
        grad_mlp_out = grad_mlp[:, 2 * units :].reshape(unit_part, D)
        mlp_in_sum = lax.all_gather(grad_mlp_in, "rep")
        rows = (packed, across, links.core(packed), links.core(across))
        rows, mlp_in_sum = lax.optimization_barrier((rows, mlp_in_sum))
        placed = place_rows(kept, received, rows, ranks, sorted_ids, starts, vocab_tile)

        def place_whole(placed, grad_values, kept, received):
            rows = lax.all_gather(lax.all_gather(grad_values, "rep"), "shard")
            ids = local_ids.transpose(1, 0, 2).reshape(-1, tok_rows) - quarter_start
            return place_slowly(kept, received, rows.reshape(-1, tok_rows, D), ids)

        table_sum, table_squares = lax.cond(
            enough, lambda placed, *_: tuple(placed), place_whole, placed, grad_values, kept, received
        )

        table_squares, grad_attn = lax.optimization_barrier((table_squares, grad_attn))
        gain_sum = grad_attn[:, -3:].astype(F32).T
        grad_attn = grad_attn[:, :-3]
        table_core = links.core(table_sum)
        squares = jnp.sum(table_squares) + jnp.sum(gain_sum * gain_sum) / n_rep
        for part in (grad_mlp_in, grad_mlp_out, grad_attn):
            squares = squares + jnp.sum(jnp.square(part.astype(F32)))
        totals = jnp.stack([squares, group_loss])
        totals = totals + links.core(totals)
        shared = jnp.concatenate([grad_attn, grad_mlp_out.reshape(in_rows, -1)], 1)[None]
        totals, shared = lax.optimization_barrier((totals, shared))
        totals = totals + links.chip(totals)
        shared = jnp.concatenate([shared, links.chip(shared)])
        totals, table_sum, shared = lax.optimization_barrier((totals, table_sum, shared))
        table_chip = links.chip(table_sum)
        shared = jnp.concatenate([shared, links.core(shared)])
        shared = jnp.stack(links.in_turn(shared, True))
        loss_sum = totals[1]
        squares = links.spread(jnp.broadcast_to(totals[0], (8, 128)))
        out_cols = D // n_rep
        mlp_in_sum = mlp_in_sum.reshape(n_rep, in_rows, 2, n_shard, unit_part)
        mlp_in_sum = mlp_in_sum.transpose(1, 2, 3, 0, 4).reshape(in_rows, 2 * FF)
        attn_cols = out_cols + 2 * in_cols // n_rep
        attn = jnp.stack([shared[r, :, :attn_cols] for r in (0, 2, 1, 3)], 1)
        mlp_out_sum = shared[:, :, attn_cols:].reshape(n_rep * unit_part, D)
        attn_out_sum = attn[:, :, :out_cols].reshape(in_rows, D)
        attn_in_sum = attn[:, :, out_cols:].reshape(in_rows, 2 * in_cols)
        squares, attn_in_sum, attn_out_sum, mlp_in_sum, mlp_out_sum = lax.optimization_barrier(
            (squares, attn_in_sum, attn_out_sum, mlp_in_sum, mlp_out_sum)
        )
        grad_norm = jnp.sqrt(jnp.sum(squares[:, 0, 0]))
        clip_scale = CLIP_AT / jnp.maximum(grad_norm, CLIP_AT)
        weight_sum = (attn_in_sum, attn_out_sum, mlp_in_sum, mlp_out_sum, gain_sum)
        results = [loss_sum, valid_count, grad_norm]
        masters = (
            table_master.T,
            attn_in_master,
            attn_out_master,
            mlp_in_master,
            mlp_out_master,
            gain_master,
        )
        firsts = (
            table_first.T,
            attn_in_first,
            attn_out_first,
            mlp_in_first,
            mlp_out_first,
            gain_first,
        )
        seconds = (
            table_second.T,
            attn_in_second,
            attn_out_second,
            mlp_in_second,
            mlp_out_second,
            gain_second,
        )
        rate_list = rates(seq_len)
        table = (masters[0], firsts[0], seconds[0])
        settings = (clip_scale, rate_list[0], vocab_tile)
        new = list(adam(*table, (table_sum, table_core), (my_rep, my_rep ^ 1), *settings))
        olds = [
            tuple(part.reshape(-1, part.shape[-1]) for part in member)
            for member in zip(masters[1:], firsts[1:], seconds[1:], weight_sum)
        ]
        olds[0] = (*olds[0][:3], lax.optimization_barrier((olds[0][3], new[0]))[0])
        news = list(adam_many(olds, clip_scale, rate_list[1:]))
        news[0], table_chip = lax.optimization_barrier((news[0], table_chip))
        table_both = links.core(table_chip)
        new = list(adam(*table, (table_chip,), (my_rep ^ 2,), *settings, new))
        new = adam(*table, (table_both,), (my_rep ^ 3,), *settings, new)
        results.extend(part.T for part in new)
        for index, new in enumerate(news):
            results.append(new.reshape(masters[1 + index // 4].shape))
        return tuple(results)

    return local


def solution(mesh):
    token = P(("rep", "shard"))
    weight = P(None, "shard", None)
    state = (P("shard", None), weight, weight, weight, weight, P(None, "shard"))
    outs = [P(), P(), P()]
    for spec in state:
        outs.extend([spec] * 4)
    return jax.shard_map(
        build(mesh),
        mesh=mesh,
        in_specs=(token, token, token) + state * 3,
        out_specs=tuple(outs),
        check_vma=False,
    )
```

```python
import functools

import jax
import jax.numpy as jnp
from jax import lax
from jax.experimental import pallas as pl
from jax.experimental.pallas import tpu as pltpu
from jax.sharding import PartitionSpec as P

D = 960
HEADS = 15
KV_HEADS = 5
HEAD_DIM = 64
FF = 2560
BLOCK = 256
STEP = 5
LINE = 4

EPS_NORM = 1e-05
ROPE_BASE = 100000.0
BETA_ONE = 0.5
BETA_TWO = 0.5
DECAY = 0.1
CLIP_AT = 0.01
ADAM_EPS = 1e-08

F32 = jnp.float32
BF16 = jnp.bfloat16
QUERY = HEADS * HEAD_DIM
KEY = KV_HEADS * HEAD_DIM
VMEM = 56 * 1024 * 1024


def rms_norm(values, gain):
    return values * lax.rsqrt(jnp.mean(values * values, axis=-1, keepdims=True) + EPS_NORM) * gain


def rotate(values, positions):
    half_dim = values.shape[-1] // 2
    freqs = ROPE_BASE ** (-2.0 * jnp.arange(half_dim).astype(F32) / values.shape[-1])
    angles = positions.astype(F32)[:, None] * freqs[None, :]
    cosine = jnp.cos(angles)[:, None, :]
    sine = jnp.sin(angles)[:, None, :]
    first_half = values[..., :half_dim]
    second_half = values[..., half_dim:]
    return jnp.concatenate(
        [first_half * cosine - second_half * sine, second_half * cosine + first_half * sine],
        axis=-1,
    )


def swiglu(gate, up):
    return jax.nn.silu(gate) * up


def rates(seq_len):
    out_fan = max(1, HEADS * HEAD_DIM * 16 // seq_len)
    return (
        0.8 * D ** (-0.5),
        0.5 * D ** (-0.5),
        0.5 * out_fan ** (-0.5),
        0.5 * D ** (-0.5),
        0.5 * FF ** (-0.5),
        0.2,
    )


def adam_update(master, first, second, gradient, rate):
    first_new = BETA_ONE * first + (1.0 - BETA_ONE) * gradient
    second_new = BETA_TWO * second + (1.0 - BETA_TWO) * gradient * gradient
    step_size = (
        first_new
        / (1.0 - BETA_ONE**STEP)
        / (jnp.sqrt(second_new / (1.0 - BETA_TWO**STEP)) + ADAM_EPS)
    )
    master_new = master - rate * (step_size + DECAY * master)
    return (master_new, first_new, second_new, master_new.astype(BF16))


def dot(a, b, dims=((1,), (0,))):
    return lax.dot_general(a, b, (dims, ((), ())), preferred_element_type=F32)


def params():
    return pltpu.CompilerParams(vmem_limit_bytes=VMEM)


def whole(shape):
    return pl.BlockSpec(shape, lambda *_: (0,) * len(shape), pipeline_mode=pl.Buffered(1))


def lookup_kernel(ids_ref, table_ref, low_ref, rows_ref, total):
    tile = table_ref.shape[1]
    step = pl.program_id(0)
    low = table_ref[...].astype(BF16)
    low_ref[...] = low
    columns = lax.broadcasted_iota(jnp.int32, (1, tile), 1) + step * tile
    block = min(512, rows_ref.shape[0])
    for start in range(0, rows_ref.shape[0], block):
        rows = pl.ds(start, block)
        pick = jnp.where(ids_ref[rows, :] == columns, 1.0, 0.0).astype(BF16)
        found = dot(pick, low, ((1,), (1,)))

        @pl.when(step == 0)
        def _():
            total[rows, :] = found

        @pl.when(step > 0)
        def _():
            total[rows, :] += found

    @pl.when(step == pl.num_programs(0) - 1)
    def _():
        rows_ref[...] = total[...].astype(BF16)


def lookup(table_t, local_ids, tile=512):
    width, vocab = table_t.shape
    count = local_ids.shape[0]
    return pl.pallas_call(
        lookup_kernel,
        grid=(vocab // tile,),
        in_specs=[
            whole((count, 1)),
            pl.BlockSpec((width, tile), lambda i: (0, i)),
        ],
        out_specs=[
            pl.BlockSpec((width, tile), lambda i: (0, i)),
            whole((count, width)),
        ],
        out_shape=[
            jax.ShapeDtypeStruct((width, vocab), BF16),
            jax.ShapeDtypeStruct((count, width), BF16),
        ],
        scratch_shapes=[pltpu.VMEM((count, width), F32)],
        compiler_params=params(),
        cost_estimate=pl.CostEstimate(
            flops=2 * count * width * vocab, bytes_accessed=6 * width * vocab, transcendentals=0
        ),
    )(local_ids[:, None], table_t)


def logits_kernel(
    states_ref,
    targets_ref,
    table_ref,
    raised_ref,
    highs_ref,
    stats_ref,
    high,
    total,
    picked,
    *,
    block,
):
    tile = table_ref.shape[1]
    step = pl.program_id(0)
    lanes = lax.broadcasted_iota(jnp.int32, (1, 128), 1)

    @pl.when(step == 0)
    def _():
        high[...] = jnp.full(high.shape, -jnp.inf, F32)
        total[...] = jnp.zeros(total.shape, F32)
        picked[...] = jnp.zeros(picked.shape, F32)
        highs_ref[...] = jnp.zeros(highs_ref.shape, F32)

    for start in range(0, states_ref.shape[0], block):
        rows = pl.ds(start, block)
        part = dot(states_ref[rows, :], table_ref[...])
        most = part[:, :128]
        for k in range(128, tile, 128):
            most = jnp.maximum(most, part[:, k : k + 128])
        old = high[rows, :]
        new = jnp.maximum(old, jnp.max(most, axis=-1, keepdims=True))
        high[rows, :] = new
        highs_ref[rows, :] = jnp.where(lanes == step, new, highs_ref[rows, :])
        targets = targets_ref[rows, :] - step * tile
        sums = total[rows, :] * jnp.exp(old - new)
        found = picked[rows, :]
        for k in range(0, tile, 128):
            logits = part[:, k : k + 128]
            raised = jnp.exp(logits - new)
            raised_ref[rows, k : k + 128] = raised.astype(BF16)
            sums += raised
            found += jnp.where(targets == lanes + k, logits, 0.0)
        total[rows, :] = sums
        picked[rows, :] = found

    @pl.when(step == pl.num_programs(0) - 1)
    def _():
        sums = jnp.sum(total[...], axis=-1, keepdims=True)
        found = jnp.sum(picked[...], axis=-1, keepdims=True)
        stats_ref[...] = jnp.where(lanes == 0, high[...], jnp.where(lanes == 1, sums, found))


def head_logits(states, targets, table_low, tile, block=256):
    count, width = states.shape
    vocab = table_low.shape[1]
    return pl.pallas_call(
        functools.partial(logits_kernel, block=block),
        grid=(vocab // tile,),
        in_specs=[
            whole((count, width)),
            whole((count, 1)),
            pl.BlockSpec((width, tile), lambda i: (0, i)),
        ],
        out_specs=[
            pl.BlockSpec((count, tile), lambda i: (0, i)),
            whole((count, 128)),
            whole((count, 128)),
        ],
        out_shape=[
            jax.ShapeDtypeStruct((count, vocab), BF16),
            jax.ShapeDtypeStruct((count, 128), F32),
            jax.ShapeDtypeStruct((count, 128), F32),
        ],
        scratch_shapes=[pltpu.VMEM((count, 128), F32)] * 3,
        compiler_params=params(),
        cost_estimate=pl.CostEstimate(
            flops=2 * count * width * vocab,
            bytes_accessed=2 * vocab * (width + count),
            transcendentals=count * vocab,
        ),
    )(states, targets[:, None], table_low)


def states_kernel(
    raised_ref, factors_ref, weights_ref, targets_ref, table_ref, grads_ref, out_ref, *, tile, each
):
    width, vocab = table_ref.shape
    weight = weights_ref[...]
    targets = targets_ref[...]
    total = None
    for start in range(0, vocab, tile):
        lanes = lax.broadcasted_iota(jnp.int32, (1, tile), 1) + start
        factor = factors_ref[:, start // each : start // each + 1]
        chances = raised_ref[:, start : start + tile].astype(F32) * factor
        part = (jnp.where(targets == lanes, chances - weight, chances)).astype(BF16)
        grads_ref[:, start : start + tile] = part
        found = dot(part, table_ref[:, start : start + tile], ((1,), (1,)))
        total = found if total is None else total + found
    out_ref[:, :width] = total.astype(BF16)
    out_ref[:, width:] = jnp.zeros((out_ref.shape[0], out_ref.shape[1] - width), BF16)


def head_states(raised, factors, weights, targets, table_low, each, rows=256, tile=512):
    count, vocab = raised.shape
    width = table_low.shape[0]
    padded = width + -width % 128
    return pl.pallas_call(
        functools.partial(states_kernel, tile=tile, each=each),
        grid=(count // rows,),
        in_specs=[
            pl.BlockSpec((rows, vocab), lambda i: (i, 0)),
            pl.BlockSpec((rows, 128), lambda i: (i, 0)),
            pl.BlockSpec((rows, 1), lambda i: (i, 0)),
            pl.BlockSpec((rows, 1), lambda i: (i, 0)),
            whole((width, vocab)),
        ],
        out_specs=[
            pl.BlockSpec((rows, vocab), lambda i: (i, 0)),
            pl.BlockSpec((rows, padded), lambda i: (i, 0)),
        ],
        out_shape=[
            jax.ShapeDtypeStruct((count, vocab), BF16),
            jax.ShapeDtypeStruct((count, padded), BF16),
        ],
        compiler_params=params(),
        cost_estimate=pl.CostEstimate(
            flops=2 * count * width * vocab,
            bytes_accessed=2 * vocab * (width + 2 * count),
            transcendentals=0,
        ),
    )(raised, factors, weights[:, None], targets[:, None], table_low)


def table_kernel(
    part_ref,
    near_t,
    far_t,
    near_pair_t,
    far_pair_t,
    near_grads,
    far_grads,
    near_pair,
    far_pair,
    scales,
    targets,
    table_ref,
    out_ref,
):
    tile = out_ref.shape[1]
    step = part_ref[0] * pl.num_programs(0) + pl.program_id(0)
    columns = lax.broadcasted_iota(jnp.int32, (1, tile), 1) + step * tile
    total = dot(near_t[...], near_grads[...]) + dot(far_t[...], far_grads[...])
    offset = 0
    for pair, pair_t in ((near_pair, near_pair_t), (far_pair, far_pair_t)):
        block = min(512, pair.shape[0])
        for start in range(0, pair.shape[0], block):
            rows = slice(offset + start, offset + start + block)
            weight = scales[rows, 1:2]
            logits = dot(pair[start : start + block, :], table_ref[...])
            chances = jnp.exp(logits - scales[rows, 0:1]) * weight
            grads = jnp.where(targets[rows, :] == columns, chances - weight, chances)
            total += dot(pair_t[:, start : start + block], grads.astype(BF16))
        offset += pair.shape[0]
    out_ref[...] = total.astype(BF16)


def head_table(
    near_t,
    far_t,
    near_grads,
    far_grads,
    near_pair,
    far_pair,
    scales,
    targets,
    table_low,
    part,
    tile,
):
    width, near = near_t.shape
    far = far_t.shape[1]
    both = near + far
    vocab = near_grads.shape[1] // 4
    steps = vocab // tile

    def column(i, part):
        return (0, part[0] * steps + i)

    return pl.pallas_call(
        table_kernel,
        grid_spec=pltpu.PrefetchScalarGridSpec(
            num_scalar_prefetch=1,
            grid=(steps,),
            in_specs=[
                whole((width, near)),
                whole((width, far)),
                whole((width, near)),
                whole((width, far)),
                pl.BlockSpec((near, tile), column),
                pl.BlockSpec((far, tile), column),
                whole((near, width)),
                whole((far, width)),
                whole((both, 2)),
                whole((both, 1)),
                pl.BlockSpec((width, tile), column),
            ],
            out_specs=pl.BlockSpec((width, tile), lambda i, part: (0, i)),
        ),
        out_shape=jax.ShapeDtypeStruct((width, vocab), BF16),
        compiler_params=params(),
        cost_estimate=pl.CostEstimate(
            flops=6 * both * width * vocab,
            bytes_accessed=2 * (2 * vocab + 3 * both) * width + 2 * vocab * both,
            transcendentals=both * vocab,
        ),
    )(
        jnp.reshape(part, (1,)).astype(jnp.int32),
        near_t,
        far_t,
        near_pair.T,
        far_pair.T,
        near_grads,
        far_grads,
        near_pair,
        far_pair,
        scales,
        targets[:, None],
        table_low,
    )


def attend_kernel(queries_ref, kv_ref, bias_ref, out_ref):
    queries = queries_ref[0]
    kv = kv_ref[:, 0].reshape(-1, queries.shape[1])
    scores = dot(queries, kv, ((1,), (1,))) * HEAD_DIM ** (-0.5) + bias_ref[...]
    highest = jnp.max(scores, axis=-1, keepdims=True)
    weights = jnp.exp(scores - highest)
    totals = jnp.sum(weights, axis=-1, keepdims=True)
    output = dot((weights / totals).astype(BF16), kv)
    lanes = lax.broadcasted_iota(jnp.int32, output.shape, 1)
    out_ref[0] = jnp.where(lanes < HEAD_DIM, highest + jnp.log(totals), output)


def attend_back_kernel(queries_ref, kv_ref, bias_ref, out_ref, grads_ref, grad_rows_ref, grad_kv_ref):
    queries, output, grads = queries_ref[0], out_ref[0], grads_ref[0]
    kv = kv_ref[:, 0].reshape(-1, queries.shape[1])
    scale = HEAD_DIM ** (-0.5)
    scores = dot(queries, kv, ((1,), (1,))) * scale + bias_ref[...]
    chances = jnp.exp(scores - output[:, :1])
    delta = jnp.sum(grads.astype(F32) * output, axis=-1, keepdims=True)
    grad_scores = (chances * (dot(grads, kv, ((1,), (1,))) - delta)).astype(BF16)
    grad_rows_ref[0] = dot(grad_scores, kv) * scale
    grad_kv = dot(grad_scores, queries, ((0,), (0,))) * scale
    grad_kv = grad_kv + dot(chances.astype(BF16), grads, ((0,), (0,)))
    grad_kv_ref[:, 0] = grad_kv.astype(BF16).reshape(grad_kv_ref[:, 0].shape)


def attend_specs(queries, kv):
    heads, rows, lanes = queries.shape
    blocks, _, block, _ = kv.shape
    return (
        pl.BlockSpec((1, rows, lanes), lambda h: (h, 0, 0)),
        pl.BlockSpec((blocks, 1, block, lanes), lambda h: (0, h, 0, 0)),
        whole((1, blocks * block)),
        pl.CostEstimate(
            flops=4 * heads * rows * blocks * block * lanes,
            bytes_accessed=4 * heads * blocks * block * lanes,
            transcendentals=heads * rows * blocks * block,
        ),
    )


def attend(queries, kv, bias):
    rows, pairs, one, cost = attend_specs(queries, kv)
    return pl.pallas_call(
        attend_kernel,
        grid=(queries.shape[0],),
        in_specs=[rows, pairs, one],
        out_specs=rows,
        out_shape=jax.ShapeDtypeStruct(queries.shape, F32),
        compiler_params=params(),
        cost_estimate=cost,
    )(queries, kv, bias)


def attend_back(queries, kv, bias, output, grads):
    rows, pairs, one, cost = attend_specs(queries, kv)
    return pl.pallas_call(
        attend_back_kernel,
        grid=(queries.shape[0],),
        in_specs=[rows, pairs, one, rows, rows],
        out_specs=[rows, pairs],
        out_shape=[
            jax.ShapeDtypeStruct(queries.shape, F32),
            jax.ShapeDtypeStruct(kv.shape, BF16),
        ],
        compiler_params=params(),
        cost_estimate=cost,
    )(queries, kv, bias, output, grads)


def place_kernel(
    starts_ref,
    ranks_ref,
    ids_ref,
    *refs,
    chunk,
    block,
):
    rows_refs = refs[:-6]
    kept_ref, received_ref, out_ref, square_ref, sorted_rows, total = refs[-6:]
    step = pl.program_id(0)
    tile = out_ref.shape[1]
    lanes = rows_refs[0].shape[0]

    @pl.when(step == 0)
    def _():
        def sort(k, carry):
            columns = pl.ds(pl.multiple_of(k * block, block), block)
            wanted = lax.broadcasted_iota(jnp.int32, (1, block), 1) + k * block
            found = None
            for source, rows_ref in enumerate(rows_refs):
                pick = ranks_ref[source * lanes : (source + 1) * lanes, :] == wanted
                pick = jnp.where(pick, 1.0, 0.0).astype(BF16)
                part = dot(rows_ref[...], pick, ((0,), (0,)))[: sorted_rows.shape[0]]
                found = part if found is None else found + part
            sorted_rows[:, columns] = found.astype(BF16)
            return carry

        lax.fori_loop(0, (starts_ref[pl.num_programs(0)] + block - 1) // block, sort, 0)

    first = starts_ref[step]
    last = starts_ref[step + 1]
    total[...] = kept_ref[...].astype(F32) + received_ref[...].astype(F32)
    columns = lax.broadcasted_iota(jnp.int32, (1, tile), 1) + step * tile

    def add(k, carry):
        rows = pl.ds(pl.multiple_of(k * chunk, chunk), chunk)
        place = lax.broadcasted_iota(jnp.int32, (chunk, 1), 0) + k * chunk
        ids = ids_ref[rows, :]
        inside = jnp.logical_and(place >= first, place < last)
        pick = jnp.where(jnp.logical_and(ids == columns, inside), 1.0, 0.0).astype(BF16)
        total[...] += dot(sorted_rows[:, rows], pick)
        return carry

    lax.fori_loop(first // chunk, (last + chunk - 1) // chunk, add, 0)
    low = total[...].astype(BF16)
    out_ref[...] = low
    value = low.astype(F32)
    squares = jnp.sum(value * value, axis=0, keepdims=True)
    part = jnp.zeros((1, 128), F32)
    for start in range(0, tile, 128):
        part += squares[:, start : start + 128]

    @pl.when(step == 0)
    def _():
        square_ref[...] = part

    @pl.when(step > 0)
    def _():
        square_ref[...] += part


def place_rows(kept, received, rows, ranks, ids, starts, tile, chunk=128, block=256):
    width, columns = kept.shape
    lanes, padded = rows[0].shape
    total = len(rows) * lanes
    block = min(block, total)
    spec = pl.BlockSpec((width, tile), lambda i, starts: (0, i))
    return pl.pallas_call(
        functools.partial(place_kernel, chunk=chunk, block=block),
        grid_spec=pltpu.PrefetchScalarGridSpec(
            num_scalar_prefetch=1,
            grid=(columns // tile,),
            in_specs=[whole((total, 1)), whole((total, 1))]
            + [whole((lanes, padded))] * len(rows)
            + [spec] * 2,
            out_specs=[spec, whole((1, 128))],
            scratch_shapes=[pltpu.VMEM((width, total), BF16), pltpu.VMEM((width, tile), F32)],
        ),
        out_shape=[
            jax.ShapeDtypeStruct((width, columns), BF16),
            jax.ShapeDtypeStruct((1, 128), F32),
        ],
        compiler_params=params(),
        cost_estimate=pl.CostEstimate(
            flops=2 * 4 * chunk * tile * width,
            bytes_accessed=6 * width * columns + 2 * total * width,
            transcendentals=0,
        ),
    )(starts, ranks[:, None], ids[:, None], *rows, kept, received)


def adam_kernel(quarters_ref, scale_ref, w_ref, m_ref, v_ref, *refs, rate, count):
    grads, outs = refs[:count], refs[-4:]
    part = pl.program_id(0) // (pl.num_programs(0) // count)
    for index, ref in enumerate(grads):

        @pl.when(part == index)
        def _(ref=ref):
            gradient = ref[...].astype(F32) * scale_ref[0]
            new = adam_update(w_ref[...], m_ref[...], v_ref[...], gradient, rate)
            for out, value in zip(outs, new):
                out[...] = value


def adam(master, first, second, grads, quarters, scale, rate, tile, before=()):
    rows, columns = master.shape
    count = len(grads)
    steps = grads[0].shape[1] // tile

    def column(i, quarters):
        return (0, quarters[i // steps] * steps + i % steps)

    def own(index):
        return lambda i, quarters: (0, jnp.clip(i - index * steps, 0, steps - 1))

    spec = pl.BlockSpec((rows, tile), column)
    shape = jax.ShapeDtypeStruct((rows, columns), F32)
    return pl.pallas_call(
        functools.partial(adam_kernel, rate=rate, count=count),
        grid_spec=pltpu.PrefetchScalarGridSpec(
            num_scalar_prefetch=1,
            grid=(count * steps,),
            in_specs=[pl.BlockSpec(memory_space=pltpu.SMEM)]
            + [spec] * 3
            + [pl.BlockSpec((rows, tile), own(index)) for index in range(count)]
            + [pl.BlockSpec(memory_space=pl.ANY)] * len(before),
            out_specs=[spec] * 4,
        ),
        out_shape=[shape] * 3 + [jax.ShapeDtypeStruct((rows, columns), BF16)],
        input_output_aliases={5 + count + k: k for k in range(len(before))},
        compiler_params=params(),
        cost_estimate=pl.CostEstimate(flops=0, bytes_accessed=0, transcendentals=0),
    )(
        jnp.stack(quarters).astype(jnp.int32),
        jnp.reshape(scale, (1,)),
        master,
        first,
        second,
        *grads,
        *before,
    )


def adam_many_kernel(scale_ref, *refs, rates):
    count = len(rates)
    inputs, outputs = refs[: 4 * count], refs[4 * count :]
    scale = scale_ref[0]
    for member, rate in enumerate(rates):
        olds = inputs[4 * member : 4 * member + 4]
        news = outputs[4 * member : 4 * member + 4]
        rows = olds[0].shape[0]
        block = 8 if rows % 8 == 0 else rows

        def update(k, carry, olds=olds, news=news, block=block, rate=rate):
            place = pl.ds(pl.multiple_of(k * block, block), block)
            w, m, v, g = (ref[place, :] for ref in olds)
            for ref, value in zip(news, adam_update(w, m, v, g.astype(F32) * scale, rate)):
                ref[place, :] = value
            return carry

        lax.fori_loop(0, rows // block, update, 0)


def adam_many(olds, scale, rates, steps=5):
    if any(master.shape[0] % (8 * steps) for master, *_ in olds[:-1]):
        steps = 1
    shapes, specs = [], []
    for index, (master, *_) in enumerate(olds):
        rows, columns = master.shape
        shapes += [jax.ShapeDtypeStruct(master.shape, F32)] * 3
        shapes += [jax.ShapeDtypeStruct(master.shape, BF16)]
        if index < len(olds) - 1:
            specs += [pl.BlockSpec((rows // steps, columns), lambda i: (i, 0))] * 4
        else:
            specs += [pl.BlockSpec((rows, columns), lambda i: (0, 0))] * 4
    return pl.pallas_call(
        functools.partial(adam_many_kernel, rates=rates),
        grid=(steps,),
        in_specs=[pl.BlockSpec(memory_space=pltpu.SMEM)] + specs,
        out_specs=specs,
        out_shape=shapes,
        compiler_params=params(),
        cost_estimate=pl.CostEstimate(flops=0, bytes_accessed=0, transcendentals=0),
    )(jnp.reshape(scale, (1,)), *[part for member in olds for part in member])


def place_slowly(kept, received, rows, ids):
    columns = jnp.arange(kept.shape[1], dtype=jnp.int32)

    def add(total, operands):
        part, part_ids = operands
        pick = (part_ids[:, None] == columns[None, :]).astype(BF16)
        return total + dot(part, pick, ((0,), (0,))), None

    total, _ = lax.scan(add, kept.astype(F32) + received.astype(F32), (rows, ids))
    total = total.astype(BF16)
    squares = jnp.sum(jnp.square(total.astype(F32)))
    return total, jnp.full((1, 128), squares / 128)


class Links:
    def __init__(self, n_shard, n_rep):
        self.n = n_shard
        self.wide = n_shard // LINE
        self.n_rep = n_rep
        me = lax.axis_index("shard")
        self.z = me // self.wide
        self.w = me % self.wide
        self.lines = [[z * self.wide + w for z in range(LINE)] for w in range(self.wide)]

    def across(self, value, step):
        pairs = [
            (z * self.wide + w, z * self.wide + (w + step) % self.wide)
            for z in range(LINE)
            for w in range(self.wide)
        ]
        return lax.ppermute(value, "shard", pairs)

    def all_across(self, value):
        return jnp.stack([self.across(value, step) for step in range(1, self.wide)])

    def sum_across(self, near, far):
        rows = near.shape[0]
        total = near.astype(F32)
        for step in range(1, self.wide):
            part = far[(step - 1) * rows : step * rows] if self.wide > 2 else far
            total = total + self.across(part, -step).astype(F32)
        return total

    def line_gather(self, value):
        return lax.all_gather(value, "shard", axis_index_groups=self.lines, tiled=True)

    def line_sum(self, value):
        parts = lax.all_to_all(
            value.astype(BF16), "shard", 0, 0, axis_index_groups=self.lines, tiled=True
        )
        return jnp.sum(parts.astype(F32), axis=0)

    def scatter(self, value):
        value = value.reshape((self.n, -1) + value.shape[1:])
        parts = lax.all_to_all(value, "shard", 0, 0, tiled=True)
        return jnp.sum(parts.astype(F32), axis=0)

    def spread(self, value):
        many = jnp.broadcast_to(value[None], (self.n,) + value.shape)
        return lax.all_to_all(many, "shard", 0, 0, tiled=True)

    def core(self, value):
        return lax.ppermute(value, "rep", [(r, r ^ 1) for r in range(self.n_rep)])

    def rep_gather(self, value):
        value = value[None]
        value = jnp.concatenate([value, self.chip(value)])
        return jnp.concatenate([value, self.core(value)])

    def in_turn(self, value, back=False):
        rep = lax.axis_index("rep")
        places = [rep ^ k for k in (0, 2, 1, 3)]
        if back:
            places = [(rep ^ k) % 2 * 2 + (rep ^ k) // 2 for k in range(4)]
        return [lax.dynamic_index_in_dim(value, place, 0, False) for place in places]

    def rep_scatter(self, value):
        parts = lax.all_to_all(value.astype(BF16), "rep", 0, 0, tiled=True)
        return jnp.sum(parts.astype(F32), axis=0)

    def rep_sum(self, value):
        value = value.astype(BF16)
        mine = value[:2].astype(F32) + self.core(value[2:]).astype(F32)
        return mine[0] + self.chip(mine[1].astype(BF16)).astype(F32)

    def chip(self, value):
        return lax.ppermute(value, "rep", [(r, r ^ 2) for r in range(self.n_rep)])


def build(mesh):
    n_shard = mesh.shape["shard"]
    n_rep = mesh.shape["rep"]

    def local(
        token_ids,
        target_ids,
        loss_mask,
        table_master,
        attn_in_master,
        attn_out_master,
        mlp_in_master,
        mlp_out_master,
        gain_master,
        table_first,
        attn_in_first,
        attn_out_first,
        mlp_in_first,
        mlp_out_first,
        gain_first,
        table_second,
        attn_in_second,
        attn_out_second,
        mlp_in_second,
        mlp_out_second,
        gain_second,
    ):
        links = Links(n_shard, n_rep)
        my_rep = lax.axis_index("rep")
        my_shard = lax.axis_index("shard")
        second_core = (my_rep % 2) == 1
        second_chip = (my_rep // 2) == 1
        tok_rows = token_ids.shape[0]
        seq_len = n_shard * tok_rows
        vocab_rows = table_master.shape[0]
        vocab_start = my_shard * vocab_rows
        wide = n_shard // LINE
        line_rows = LINE * tok_rows

        def in_order(mine, other, axis=-1):
            return jnp.where(
                second_core,
                jnp.concatenate([other, mine], axis),
                jnp.concatenate([mine, other], axis),
            )

        def my_half(value, axis=-1):
            first, second = jnp.split(value, 2, axis)
            return jnp.where(second_core, second, first), jnp.where(second_core, first, second)

        def halves(master):
            return my_half(master[0].astype(BF16))[0]

        in_rows = D // n_shard
        in_cols = attn_in_master.shape[2] // 2
        attn_part = jnp.concatenate([halves(attn_in_master), halves(attn_out_master)], 1)

        packed = jnp.stack([token_ids, target_ids, loss_mask])
        packed, attn_part = lax.optimization_barrier((packed, attn_part))
        everyone = links.spread(lax.all_gather(packed, "rep")).transpose(1, 0, 2, 3)
        everyone = everyone.reshape(LINE, n_rep, wide, 3, tok_rows).transpose(1, 0, 2, 3, 4)
        valid_count = jnp.sum(everyone[:, :, :, 2].astype(F32))
        turn = [(links.w - step) % wide for step in range(wide)]

        def group_of(rep):
            group = lax.dynamic_index_in_dim(everyone, rep, 0, False)
            group = jnp.stack(
                [lax.dynamic_index_in_dim(group, turn[step], 1, False) for step in range(wide)]
            )
            targets = group[:, :, 1].reshape(-1) - vocab_start
            return targets, group[:, :, 2].reshape(-1).astype(F32)

        group_targets, group_mask = group_of(my_rep)
        pair_targets, pair_mask = group_of(my_rep ^ 2)
        group_weights = group_mask / valid_count
        pair_weights = pair_mask / valid_count
        place_block = my_rep * wide + links.w
        positions = place_block * tok_rows + jnp.arange(tok_rows, dtype=jnp.int32)

        unit_rows = FF // n_shard
        unit_part = unit_rows // n_rep
        units = n_shard * unit_part
        mlp_in_part = mlp_in_master[0].astype(BF16)
        mlp_in_part = mlp_in_part.reshape(-1, 2, n_shard, n_rep, unit_part)
        mlp_in_part = lax.dynamic_index_in_dim(mlp_in_part, my_rep, 3, False).reshape(-1, 2 * units)
        mlp_out_part = mlp_out_master[0].astype(BF16).reshape(n_rep, unit_part, D)
        mlp_out_part = lax.dynamic_index_in_dim(mlp_out_part, my_rep, 0, False)
        mlp_part = jnp.concatenate([mlp_in_part, mlp_out_part.reshape(in_rows, -1)], 1)
        attn_mine = lax.all_gather(attn_part, "shard", tiled=True)

        room = min(64, tok_rows)
        vocab_tile = min(512, vocab_rows // 4)
        all_ids = everyone[:, :, :, 0].reshape(n_rep, n_shard, tok_rows)
        earlier = jnp.tril(jnp.ones((tok_rows, tok_rows), BF16), -1)

        def places(inside):
            found = jnp.einsum(
                "...j,ij->...i", inside.astype(BF16), earlier, preferred_element_type=F32
            )
            return jnp.where(inside, found.astype(jnp.int32), -1)

        owners = jnp.arange(n_shard, dtype=jnp.int32)
        owned = (all_ids // vocab_rows)[:, :, None, :] == owners[:, None]
        enough = jnp.max(jnp.sum(owned.astype(jnp.int32), -1)) <= room
        local_ids = all_ids - vocab_start
        inside = (local_ids >= 0) & (local_ids < vocab_rows)
        room_iota = jnp.arange(room, dtype=jnp.int32)
        slots = places(inside)
        slot_ids = jnp.max(
            jnp.where(slots[:, :, None, :] == room_iota[:, None], local_ids[:, :, None, :], -1), -1
        )
        slot_ids = jnp.where(slot_ids < 0, vocab_rows, slot_ids)
        own_ids = lax.dynamic_index_in_dim(
            lax.dynamic_index_in_dim(all_ids, my_rep, 0, False), my_shard, 0, False
        )
        own_slots = places((own_ids // vocab_rows)[None, :] == owners[:, None])
        packing = (own_slots[:, None, :] == room_iota[:, None]).astype(BF16).reshape(-1, tok_rows)

        my_slots = lax.dynamic_index_in_dim(slot_ids, my_rep, 0, False).reshape(-1)
        table_low, looked = lookup(table_master.T, my_slots, min(512, vocab_rows))

        looked, mlp_part = lax.optimization_barrier((looked, mlp_part))
        mlp_all = lax.all_gather(mlp_part, "shard", tiled=True)
        packed = lax.all_to_all(looked.reshape(n_shard, room, D), "shard", 0, 0, tiled=True)
        packed = dot(packing, packed.reshape(-1, D), ((0,), (0,)))

        def read_whole(packed, table_low):
            ids = lax.dynamic_index_in_dim(local_ids, my_rep, 0, False).reshape(-1)
            columns = jnp.arange(vocab_rows, dtype=jnp.int32)
            pick = (ids[:, None] == columns[None, :]).astype(BF16)
            rows = dot(pick, table_low, ((1,), (1,))).astype(BF16)
            rows = lax.all_to_all(rows.reshape(n_shard, tok_rows, D), "shard", 0, 0, tiled=True)
            return jnp.sum(rows.astype(F32), axis=0)

        values = lax.cond(enough, lambda packed, _: packed, read_whole, packed, table_low)
        values, gain_low = lax.optimization_barrier((values, gain_master.astype(BF16)))
        gains = links.spread(gain_low).transpose(1, 0, 2).reshape(3, D).astype(F32)

        rank_ids = jnp.concatenate(
            [lax.dynamic_index_in_dim(slot_ids, my_rep ^ r, 0, False) for r in (0, 2, 1, 3)]
        ).reshape(-1)
        quarter_rows = vocab_rows // n_rep
        quarter_start = my_rep * quarter_rows
        rank_ids = rank_ids - quarter_start
        rank_ids = jnp.where((rank_ids >= 0) & (rank_ids < quarter_rows), rank_ids, quarter_rows)
        slot_iota = jnp.arange(rank_ids.shape[0], dtype=jnp.int32)
        before = (rank_ids[None, :] < rank_ids[:, None]) | (
            (rank_ids[None, :] == rank_ids[:, None]) & (slot_iota[None, :] < slot_iota[:, None])
        )
        ranks = jnp.sum(before.astype(jnp.int32), axis=1)
        sorted_ids = jnp.sort(rank_ids)
        edges = jnp.arange(0, quarter_rows + 1, vocab_tile, dtype=jnp.int32)
        starts = jnp.sum((rank_ids[None, :] < edges[:, None]).astype(jnp.int32), axis=1)
        attn_mine, ranks, sorted_ids, starts, gains = lax.optimization_barrier(
            (attn_mine, ranks, sorted_ids, starts, gains)
        )
        attn_other = links.core(attn_mine)
        attn_in = (attn_mine[:, :in_cols], attn_other[:, :in_cols])
        attn_out = (attn_mine[:, in_cols:], attn_other[:, in_cols:])
        mlp_in = mlp_all[:, : 2 * units]
        mlp_out = mlp_all[:, 2 * units :].reshape(n_shard * unit_part, D)
        def times(value, pair):
            return dot(value, pair[0]), dot(value, pair[1])

        def times_back(mine, other, pair):
            return dot(mine, pair[0], ((1,), (1,))) + dot(other, pair[1], ((1,), (1,)))

        normed_one, norm_one_back = jax.vjp(rms_norm, values, gains[0])
        normed_one = normed_one.astype(BF16)
        mixed = in_order(*times(normed_one, attn_in))
        heads_raw = mixed[:, : QUERY + KEY].reshape(tok_rows, HEADS + KV_HEADS, HEAD_DIM)
        rotated, rope_back = jax.vjp(lambda part: rotate(part, positions), heads_raw)
        rotated = rotated.astype(BF16)
        group_size = HEADS // KV_HEADS
        queries = rotated[:, :HEADS].reshape(tok_rows, KV_HEADS, group_size, HEAD_DIM)
        queries = queries.transpose(1, 2, 0, 3).reshape(KV_HEADS, group_size * tok_rows, HEAD_DIM)
        queries = jnp.pad(queries, ((0, 0), (0, 0), (0, HEAD_DIM)))
        vals = mixed[:, QUERY + KEY :].astype(BF16).reshape(tok_rows, KV_HEADS, HEAD_DIM)
        kv = jnp.concatenate([rotated[:, HEADS:], vals], 2).transpose(1, 0, 2)
        kv = links.rep_gather(jnp.concatenate([kv[None], links.all_across(kv)]))
        kv = kv.reshape(n_rep * wide, KV_HEADS, tok_rows, 2 * HEAD_DIM)
        key_places = (
            (jnp.stack([my_rep ^ other for other in (0, 2, 1, 3)]) * wide)[:, None, None]
            + ((links.w - jnp.arange(wide, dtype=jnp.int32)) % wide)[None, :, None]
        ) * tok_rows + jnp.arange(tok_rows, dtype=jnp.int32)
        key_blocks = key_places.reshape(-1) // BLOCK
        bias = jnp.where(key_blocks <= positions[0] // BLOCK, 0.0, -1e30).astype(F32)[None]
        outputs = attend(queries, kv, bias)

        def to_rows(heads):
            return (
                heads.reshape(KV_HEADS, group_size, tok_rows, HEAD_DIM)
                .transpose(2, 0, 1, 3)
                .reshape(tok_rows, QUERY)
            )

        attended = to_rows(outputs[:, :, HEAD_DIM:].astype(BF16))
        middle = values + in_order(*times(attended, attn_out))
        normed_two, norm_two_back = jax.vjp(rms_norm, middle, gains[1])
        normed_two = normed_two.astype(BF16)
        normed_all = lax.all_gather(normed_two, "rep", tiled=True)
        gate_up = dot(normed_all, mlp_in)
        hidden, glu_back = jax.vjp(swiglu, gate_up[:, :units], gate_up[:, units:])
        hidden = hidden.astype(BF16)
        result = middle + links.rep_scatter(dot(hidden, mlp_out).reshape(n_rep, tok_rows, D))
        final, final_back = jax.vjp(rms_norm, result, gains[2])

        near = links.line_gather(final.astype(BF16))
        far = links.all_across(near).reshape(-1, D)
        near_targets, far_targets = group_targets[:line_rows], group_targets[line_rows:]
        pair_near = links.chip(near)
        pair_far = links.chip(far)
        head_tile = 1024 if vocab_rows % 1024 == 0 else 512
        near_raised, near_highs, near_stats = head_logits(
            near, near_targets, table_low, head_tile
        )
        far, near_stats = lax.optimization_barrier((far, near_stats))
        far_raised, far_highs, far_stats = head_logits(far, far_targets, table_low, head_tile)
        stats = jnp.concatenate([near_stats, far_stats])[:, :3].T
        stats = stats.reshape(3, wide, LINE, tok_rows)
        ordered = jnp.stack(
            [lax.dynamic_index_in_dim(stats, turn[step], 1, False) for step in range(wide)], 1
        )
        stats = links.spread(ordered)
        top = jnp.max(stats[:, 0], axis=0)
        log_totals = top + jnp.log(jnp.sum(stats[:, 1] * jnp.exp(stats[:, 0] - top), axis=0))
        picked = jnp.sum(stats[:, 2], axis=0)
        losses = log_totals - picked

        def turned(part):
            return jnp.stack(
                [lax.dynamic_index_in_dim(part, turn[step], 0, False) for step in range(wide)]
            ).reshape(-1)

        log_totals = turned(log_totals)
        group_loss = jnp.sum(turned(losses) * group_mask)
        pair_logs = links.chip(log_totals)

        def factors(highs, part):
            return jnp.exp(highs - log_totals[part, None]) * group_weights[part, None]

        near_rows, far_rows = slice(0, line_rows), slice(line_rows, None)
        far_grads, far_part = head_states(
            far_raised,
            factors(far_highs, far_rows),
            group_weights[far_rows],
            far_targets,
            table_low,
            head_tile,
        )
        far_sent = far_part
        near_raised, far_part = lax.optimization_barrier((near_raised, far_part))
        near_grads, near_part = head_states(
            near_raised,
            factors(near_highs, near_rows),
            group_weights[near_rows],
            near_targets,
            table_low,
            head_tile,
        )

        table_operands = (
            near.T,
            far.T,
            near_grads,
            far_grads,
            pair_near,
            pair_far,
            jnp.stack([pair_logs, pair_weights], axis=1),
            pair_targets,
            table_low,
        )
        sent = head_table(*table_operands, my_rep ^ 1, vocab_tile)
        received = links.core(sent)
        sent, near_part = lax.optimization_barrier((sent, near_part))
        grad_states = links.sum_across(near_part, far_sent)
        grad_final = links.line_sum(grad_states.reshape(LINE, tok_rows, -1))[:, :D]
        kept = head_table(*table_operands, my_rep, vocab_tile)
        kept, grad_final = lax.optimization_barrier((kept, grad_final))

        grad_output, grad_gain_three = final_back(grad_final)

        def weight_grad(value, mine, other):
            sent = dot(value, other, ((0,), (0,))).astype(BF16)
            half = dot(value, mine, ((0,), (0,))) + links.core(sent).astype(F32)
            first, second = jnp.split(half, 2, 1)
            sent = links.chip(jnp.where(second_chip, first, second).astype(BF16))
            return (jnp.where(second_chip, second, first) + sent.astype(F32)).astype(BF16)

        pad_rows = -in_rows % 16

        def pad_blocks(value):
            value = value.reshape(-1, n_shard, in_rows)
            value = jnp.pad(value, ((0, 0), (0, 0), (0, pad_rows)))
            return value.reshape(-1, n_shard * (in_rows + pad_rows))

        branch = lax.all_gather(grad_output.astype(BF16), "rep", tiled=True)
        grad_mlp_out = dot(hidden, branch, ((0,), (0,))).astype(BF16)
        grad_hidden = dot(branch, mlp_out, ((1,), (1,)))
        grad_glu = jnp.concatenate(glu_back(grad_hidden), 1).astype(BF16)
        grad_mlp_in = dot(pad_blocks(normed_all), grad_glu, ((0,), (0,))).astype(BF16)
        grad_normed_two = dot(grad_glu, mlp_in, ((1,), (1,))).reshape(n_rep, tok_rows, D)
        turns = links.in_turn(grad_normed_two)
        sent = links.core(jnp.stack(turns[2:]).astype(BF16)).astype(F32)
        passed = links.chip((turns[1] + sent[1]).astype(BF16))
        grad_normed_two = turns[0] + sent[0] + passed.astype(F32)
        middle_part, grad_gain_two = norm_two_back(grad_normed_two)
        grad_middle = grad_output + middle_part

        grad_mlp = [grad_mlp_in, grad_mlp_out.reshape(grad_mlp_in.shape[0], -1)]
        grad_mlp = lax.psum_scatter(jnp.concatenate(grad_mlp, 1), "shard", tiled=True)

        out_mine, out_other = my_half(grad_middle.astype(BF16))
        grad_attn_out = weight_grad(pad_blocks(attended), out_mine, out_other)
        grad_attended = times_back(out_mine, out_other, attn_out).astype(BF16)
        grad_heads = (
            grad_attended.reshape(tok_rows, KV_HEADS, group_size, HEAD_DIM)
            .transpose(1, 2, 0, 3)
            .reshape(KV_HEADS, group_size * tok_rows, HEAD_DIM)
        )
        grad_heads = jnp.pad(grad_heads, ((0, 0), (0, 0), (HEAD_DIM, 0)))
        grad_queries, grad_kv = attend_back(queries, kv, bias, outputs, grad_heads)
        grad_kv = grad_kv.reshape(n_rep, wide, KV_HEADS, tok_rows, 2 * HEAD_DIM)
        grad_kv = links.rep_sum(grad_kv)
        far_kv = grad_kv[1:].astype(BF16).reshape(-1, tok_rows, 2 * HEAD_DIM)
        grad_kv = links.sum_across(grad_kv[0], far_kv).transpose(1, 0, 2)
        grad_queries = grad_queries[:, :, :HEAD_DIM]
        grad_rotated = jnp.concatenate(
            [
                to_rows(grad_queries).reshape(tok_rows, HEADS, HEAD_DIM),
                grad_kv[:, :, :HEAD_DIM],
            ],
            1,
        )
        grad_raw = rope_back(grad_rotated)[0].reshape(tok_rows, QUERY + KEY)
        grad_mixed = jnp.concatenate([grad_raw, grad_kv[:, :, HEAD_DIM:].reshape(tok_rows, KEY)], 1).astype(BF16)
        mixed_mine, mixed_other = my_half(grad_mixed)
        values_part, grad_gain_one = norm_one_back(times_back(mixed_mine, mixed_other, attn_in))
        grad_values = (grad_middle + values_part).astype(BF16)
        grad_gains = jnp.stack([grad_gain_one, grad_gain_two, grad_gain_three], 1)
        grad_gains = grad_gains + links.core(grad_gains)
        grad_gains = pad_blocks((grad_gains + links.chip(grad_gains)).T).T
        wide_values = jnp.pad(grad_values, ((0, 0), (0, -D % 128)))
        packed = dot(packing, wide_values).astype(BF16).reshape(n_shard, room, -1)
        packed = lax.all_to_all(packed, "shard", 0, 0, tiled=True)
        grad_attn_in = weight_grad(pad_blocks(normed_one), mixed_mine, mixed_other)
        grad_attn = jnp.concatenate([grad_attn_out, grad_attn_in, grad_gains.astype(BF16)], 1)
        packed, grad_attn = lax.optimization_barrier((packed, grad_attn))
        packed = packed.reshape(n_shard * room, -1)
        across = links.chip(packed)
        grad_attn = grad_attn.reshape((n_shard, -1) + grad_attn.shape[1:])
        grad_attn = lax.all_to_all(grad_attn, "shard", 0, 0, tiled=True)
        across, grad_mlp = lax.optimization_barrier((across, grad_mlp))
        grad_mlp_in = grad_mlp[:in_rows, : 2 * units]
        grad_mlp_out = grad_mlp[:, 2 * units :].reshape(unit_part, D)
        mlp_in_sum = lax.all_gather(grad_mlp_in, "rep")
        rows = (packed, across, links.core(packed), links.core(across))
        rows, mlp_in_sum = lax.optimization_barrier((rows, mlp_in_sum))
        placed = place_rows(kept, received, rows, ranks, sorted_ids, starts, vocab_tile)

        def place_whole(placed, grad_values, kept, received):
            rows = lax.all_gather(lax.all_gather(grad_values, "rep"), "shard")
            ids = local_ids.transpose(1, 0, 2).reshape(-1, tok_rows) - quarter_start
            return place_slowly(kept, received, rows.reshape(-1, tok_rows, D), ids)

        table_sum, table_squares = lax.cond(
            enough, lambda placed, *_: tuple(placed), place_whole, placed, grad_values, kept, received
        )

        table_squares, grad_attn = lax.optimization_barrier((table_squares, grad_attn))
        grad_attn = jnp.sum(grad_attn.astype(F32), axis=0)[:in_rows].astype(BF16)
        gain_sum = grad_attn[:, -3:].astype(F32).T
        grad_attn = grad_attn[:, :-3]
        table_core = links.core(table_sum)
        squares = jnp.sum(table_squares) + jnp.sum(gain_sum * gain_sum) / n_rep
        for part in (grad_mlp_in, grad_mlp_out, grad_attn):
            squares = squares + jnp.sum(jnp.square(part.astype(F32)))
        totals = jnp.stack([squares, group_loss])
        totals = totals + links.core(totals)
        shared = jnp.concatenate([grad_attn, grad_mlp_out.reshape(in_rows, -1)], 1)[None]
        totals, shared = lax.optimization_barrier((totals, shared))
        totals = totals + links.chip(totals)
        mlp_in_sum = mlp_in_sum.reshape(n_rep, in_rows, 2, n_shard, unit_part)
        mlp_in_sum = mlp_in_sum.transpose(1, 2, 3, 0, 4).reshape(in_rows, 2 * FF)
        shared = jnp.concatenate([shared, links.chip(shared)])
        totals, table_sum, shared, mlp_in_sum = lax.optimization_barrier(
            (totals, table_sum, shared, mlp_in_sum)
        )
        table_chip = links.chip(table_sum)
        shared = jnp.concatenate([shared, links.core(shared)])
        shared = jnp.stack(links.in_turn(shared, True))
        loss_sum = totals[1]
        squares = links.spread(jnp.broadcast_to(totals[0], (8, 128)))
        out_cols = D // n_rep
        attn_cols = out_cols + 2 * in_cols // n_rep
        attn = jnp.stack([shared[r, :, :attn_cols] for r in (0, 2, 1, 3)], 1)
        mlp_out_sum = shared[:, :, attn_cols:].reshape(n_rep * unit_part, D)
        attn_out_sum = attn[:, :, :out_cols].reshape(in_rows, D)
        attn_in_sum = attn[:, :, out_cols:].reshape(in_rows, 2 * in_cols)
        squares, attn_in_sum, attn_out_sum, mlp_in_sum, mlp_out_sum = lax.optimization_barrier(
            (squares, attn_in_sum, attn_out_sum, mlp_in_sum, mlp_out_sum)
        )
        grad_norm = jnp.sqrt(jnp.sum(squares[:, 0, 0]))
        clip_scale = CLIP_AT / jnp.maximum(grad_norm, CLIP_AT)
        weight_sum = (attn_in_sum, attn_out_sum, mlp_in_sum, mlp_out_sum, gain_sum)
        results = [loss_sum, valid_count, grad_norm]
        masters = (
            table_master.T,
            attn_in_master,
            attn_out_master,
            mlp_in_master,
            mlp_out_master,
            gain_master,
        )
        firsts = (
            table_first.T,
            attn_in_first,
            attn_out_first,
            mlp_in_first,
            mlp_out_first,
            gain_first,
        )
        seconds = (
            table_second.T,
            attn_in_second,
            attn_out_second,
            mlp_in_second,
            mlp_out_second,
            gain_second,
        )
        rate_list = rates(seq_len)
        table = (masters[0], firsts[0], seconds[0])
        settings = (clip_scale, rate_list[0], vocab_tile)
        new = list(adam(*table, (table_sum, table_core), (my_rep, my_rep ^ 1), *settings))
        olds = [
            tuple(part.reshape(-1, part.shape[-1]) for part in member)
            for member in zip(masters[1:], firsts[1:], seconds[1:], weight_sum)
        ]
        olds[0] = (*olds[0][:3], lax.optimization_barrier((olds[0][3], new[0]))[0])
        news = list(adam_many(olds, clip_scale, rate_list[1:]))
        news[0], table_chip = lax.optimization_barrier((news[0], table_chip))
        table_both = links.core(table_chip)
        new = list(adam(*table, (table_chip,), (my_rep ^ 2,), *settings, new))
        new = adam(*table, (table_both,), (my_rep ^ 3,), *settings, new)
        results.extend(part.T for part in new)
        for index, new in enumerate(news):
            results.append(new.reshape(masters[1 + index // 4].shape))
        return tuple(results)

    return local


def solution(mesh):
    token = P(("rep", "shard"))
    weight = P(None, "shard", None)
    state = (P("shard", None), weight, weight, weight, weight, P(None, "shard"))
    outs = [P(), P(), P()]
    for spec in state:
        outs.extend([spec] * 4)
    return jax.shard_map(
        build(mesh),
        mesh=mesh,
        in_specs=(token, token, token) + state * 3,
        out_specs=tuple(outs),
        check_vma=False,
    )
```

```python
import functools

import jax
import jax.numpy as jnp
from jax import lax
from jax.experimental import pallas as pl
from jax.experimental.pallas import tpu as pltpu
from jax.sharding import PartitionSpec as P

D = 960
HEADS = 15
KV_HEADS = 5
HEAD_DIM = 64
FF = 2560
BLOCK = 256
STEP = 5
LINE = 4

EPS_NORM = 1e-05
ROPE_BASE = 100000.0
BETA_ONE = 0.5
BETA_TWO = 0.5
DECAY = 0.1
CLIP_AT = 0.01
ADAM_EPS = 1e-08

F32 = jnp.float32
BF16 = jnp.bfloat16
QUERY = HEADS * HEAD_DIM
KEY = KV_HEADS * HEAD_DIM
VMEM = 56 * 1024 * 1024


def rms_norm(values, gain):
    return values * lax.rsqrt(jnp.mean(values * values, axis=-1, keepdims=True) + EPS_NORM) * gain


def rotate(values, positions):
    half_dim = values.shape[-1] // 2
    freqs = ROPE_BASE ** (-2.0 * jnp.arange(half_dim).astype(F32) / values.shape[-1])
    angles = positions.astype(F32)[:, None] * freqs[None, :]
    cosine = jnp.cos(angles)[:, None, :]
    sine = jnp.sin(angles)[:, None, :]
    first_half = values[..., :half_dim]
    second_half = values[..., half_dim:]
    return jnp.concatenate(
        [first_half * cosine - second_half * sine, second_half * cosine + first_half * sine],
        axis=-1,
    )


def swiglu(gate, up):
    return jax.nn.silu(gate) * up


def rates(seq_len):
    out_fan = max(1, HEADS * HEAD_DIM * 16 // seq_len)
    return (
        0.8 * D ** (-0.5),
        0.5 * D ** (-0.5),
        0.5 * out_fan ** (-0.5),
        0.5 * D ** (-0.5),
        0.5 * FF ** (-0.5),
        0.2,
    )


def adam_update(master, first, second, gradient, rate):
    first_new = BETA_ONE * first + (1.0 - BETA_ONE) * gradient
    second_new = BETA_TWO * second + (1.0 - BETA_TWO) * gradient * gradient
    step_size = (
        first_new
        / (1.0 - BETA_ONE**STEP)
        / (jnp.sqrt(second_new / (1.0 - BETA_TWO**STEP)) + ADAM_EPS)
    )
    master_new = master - rate * (step_size + DECAY * master)
    return (master_new, first_new, second_new, master_new.astype(BF16))


def dot(a, b, dims=((1,), (0,))):
    return lax.dot_general(a, b, (dims, ((), ())), preferred_element_type=F32)


def params():
    return pltpu.CompilerParams(vmem_limit_bytes=VMEM)


def whole(shape):
    return pl.BlockSpec(shape, lambda *_: (0,) * len(shape), pipeline_mode=pl.Buffered(1))


def lookup_kernel(ids_ref, table_ref, low_ref, rows_ref, total):
    tile = table_ref.shape[1]
    step = pl.program_id(0)
    low = table_ref[...].astype(BF16)
    low_ref[...] = low
    columns = lax.broadcasted_iota(jnp.int32, (1, tile), 1) + step * tile
    block = min(512, rows_ref.shape[0])
    for start in range(0, rows_ref.shape[0], block):
        rows = pl.ds(start, block)
        pick = jnp.where(ids_ref[rows, :] == columns, 1.0, 0.0).astype(BF16)
        found = dot(pick, low, ((1,), (1,)))

        @pl.when(step == 0)
        def _():
            total[rows, :] = found

        @pl.when(step > 0)
        def _():
            total[rows, :] += found

    @pl.when(step == pl.num_programs(0) - 1)
    def _():
        rows_ref[...] = total[...].astype(BF16)


def lookup(table_t, local_ids, tile=512):
    width, vocab = table_t.shape
    count = local_ids.shape[0]
    return pl.pallas_call(
        lookup_kernel,
        grid=(vocab // tile,),
        in_specs=[
            whole((count, 1)),
            pl.BlockSpec((width, tile), lambda i: (0, i)),
        ],
        out_specs=[
            pl.BlockSpec((width, tile), lambda i: (0, i)),
            whole((count, width)),
        ],
        out_shape=[
            jax.ShapeDtypeStruct((width, vocab), BF16),
            jax.ShapeDtypeStruct((count, width), BF16),
        ],
        scratch_shapes=[pltpu.VMEM((count, width), F32)],
        compiler_params=params(),
        cost_estimate=pl.CostEstimate(
            flops=2 * count * width * vocab, bytes_accessed=6 * width * vocab, transcendentals=0
        ),
    )(local_ids[:, None], table_t)


def logits_kernel(
    states_ref,
    targets_ref,
    table_ref,
    raised_ref,
    highs_ref,
    stats_ref,
    high,
    total,
    picked,
    *,
    block,
):
    tile = table_ref.shape[1]
    step = pl.program_id(0)
    lanes = lax.broadcasted_iota(jnp.int32, (1, 128), 1)

    @pl.when(step == 0)
    def _():
        high[...] = jnp.full(high.shape, -jnp.inf, F32)
        total[...] = jnp.zeros(total.shape, F32)
        picked[...] = jnp.zeros(picked.shape, F32)
        highs_ref[...] = jnp.zeros(highs_ref.shape, F32)

    for start in range(0, states_ref.shape[0], block):
        rows = pl.ds(start, block)
        part = dot(states_ref[rows, :], table_ref[...])
        most = part[:, :128]
        for k in range(128, tile, 128):
            most = jnp.maximum(most, part[:, k : k + 128])
        old = high[rows, :]
        new = jnp.maximum(old, jnp.max(most, axis=-1, keepdims=True))
        high[rows, :] = new
        highs_ref[rows, :] = jnp.where(lanes == step, new, highs_ref[rows, :])
        targets = targets_ref[rows, :] - step * tile
        sums = total[rows, :] * jnp.exp(old - new)
        found = picked[rows, :]
        for k in range(0, tile, 128):
            logits = part[:, k : k + 128]
            raised = jnp.exp(logits - new)
            raised_ref[rows, k : k + 128] = raised.astype(BF16)
            sums += raised
            found += jnp.where(targets == lanes + k, logits, 0.0)
        total[rows, :] = sums
        picked[rows, :] = found

    @pl.when(step == pl.num_programs(0) - 1)
    def _():
        sums = jnp.sum(total[...], axis=-1, keepdims=True)
        found = jnp.sum(picked[...], axis=-1, keepdims=True)
        stats_ref[...] = jnp.where(lanes == 0, high[...], jnp.where(lanes == 1, sums, found))


def head_logits(states, targets, table_low, tile, block=256):
    count, width = states.shape
    vocab = table_low.shape[1]
    return pl.pallas_call(
        functools.partial(logits_kernel, block=block),
        grid=(vocab // tile,),
        in_specs=[
            whole((count, width)),
            whole((count, 1)),
            pl.BlockSpec((width, tile), lambda i: (0, i)),
        ],
        out_specs=[
            pl.BlockSpec((count, tile), lambda i: (0, i)),
            whole((count, 128)),
            whole((count, 128)),
        ],
        out_shape=[
            jax.ShapeDtypeStruct((count, vocab), BF16),
            jax.ShapeDtypeStruct((count, 128), F32),
            jax.ShapeDtypeStruct((count, 128), F32),
        ],
        scratch_shapes=[pltpu.VMEM((count, 128), F32)] * 3,
        compiler_params=params(),
        cost_estimate=pl.CostEstimate(
            flops=2 * count * width * vocab,
            bytes_accessed=2 * vocab * (width + count),
            transcendentals=count * vocab,
        ),
    )(states, targets[:, None], table_low)


def states_kernel(
    raised_ref, factors_ref, weights_ref, targets_ref, table_ref, grads_ref, out_ref, *, tile, each
):
    width, vocab = table_ref.shape
    weight = weights_ref[...]
    targets = targets_ref[...]
    total = None
    for start in range(0, vocab, tile):
        lanes = lax.broadcasted_iota(jnp.int32, (1, tile), 1) + start
        factor = factors_ref[:, start // each : start // each + 1]
        chances = raised_ref[:, start : start + tile].astype(F32) * factor
        part = (jnp.where(targets == lanes, chances - weight, chances)).astype(BF16)
        grads_ref[:, start : start + tile] = part
        found = dot(part, table_ref[:, start : start + tile], ((1,), (1,)))
        total = found if total is None else total + found
    out_ref[:, :width] = total.astype(BF16)
    out_ref[:, width:] = jnp.zeros((out_ref.shape[0], out_ref.shape[1] - width), BF16)


def head_states(raised, factors, weights, targets, table_low, each, rows=256, tile=512):
    count, vocab = raised.shape
    width = table_low.shape[0]
    padded = width + -width % 128
    return pl.pallas_call(
        functools.partial(states_kernel, tile=tile, each=each),
        grid=(count // rows,),
        in_specs=[
            pl.BlockSpec((rows, vocab), lambda i: (i, 0)),
            pl.BlockSpec((rows, 128), lambda i: (i, 0)),
            pl.BlockSpec((rows, 1), lambda i: (i, 0)),
            pl.BlockSpec((rows, 1), lambda i: (i, 0)),
            whole((width, vocab)),
        ],
        out_specs=[
            pl.BlockSpec((rows, vocab), lambda i: (i, 0)),
            pl.BlockSpec((rows, padded), lambda i: (i, 0)),
        ],
        out_shape=[
            jax.ShapeDtypeStruct((count, vocab), BF16),
            jax.ShapeDtypeStruct((count, padded), BF16),
        ],
        compiler_params=params(),
        cost_estimate=pl.CostEstimate(
            flops=2 * count * width * vocab,
            bytes_accessed=2 * vocab * (width + 2 * count),
            transcendentals=0,
        ),
    )(raised, factors, weights[:, None], targets[:, None], table_low)


def table_kernel(
    part_ref,
    near_t,
    far_t,
    near_pair_t,
    far_pair_t,
    near_grads,
    far_grads,
    near_pair,
    far_pair,
    scales,
    targets,
    table_ref,
    out_ref,
):
    tile = out_ref.shape[1]
    step = part_ref[0] * pl.num_programs(0) + pl.program_id(0)
    columns = lax.broadcasted_iota(jnp.int32, (1, tile), 1) + step * tile
    total = dot(near_t[...], near_grads[...]) + dot(far_t[...], far_grads[...])
    offset = 0
    for pair, pair_t in ((near_pair, near_pair_t), (far_pair, far_pair_t)):
        block = min(512, pair.shape[0])
        for start in range(0, pair.shape[0], block):
            rows = slice(offset + start, offset + start + block)
            weight = scales[rows, 1:2]
            logits = dot(pair[start : start + block, :], table_ref[...])
            chances = jnp.exp(logits - scales[rows, 0:1]) * weight
            grads = jnp.where(targets[rows, :] == columns, chances - weight, chances)
            total += dot(pair_t[:, start : start + block], grads.astype(BF16))
        offset += pair.shape[0]
    out_ref[...] = total.astype(BF16)


def head_table(
    near_t,
    far_t,
    near_grads,
    far_grads,
    near_pair,
    far_pair,
    scales,
    targets,
    table_low,
    part,
    tile,
):
    width, near = near_t.shape
    far = far_t.shape[1]
    both = near + far
    vocab = near_grads.shape[1] // 4
    steps = vocab // tile

    def column(i, part):
        return (0, part[0] * steps + i)

    return pl.pallas_call(
        table_kernel,
        grid_spec=pltpu.PrefetchScalarGridSpec(
            num_scalar_prefetch=1,
            grid=(steps,),
            in_specs=[
                whole((width, near)),
                whole((width, far)),
                whole((width, near)),
                whole((width, far)),
                pl.BlockSpec((near, tile), column),
                pl.BlockSpec((far, tile), column),
                whole((near, width)),
                whole((far, width)),
                whole((both, 2)),
                whole((both, 1)),
                pl.BlockSpec((width, tile), column),
            ],
            out_specs=pl.BlockSpec((width, tile), lambda i, part: (0, i)),
        ),
        out_shape=jax.ShapeDtypeStruct((width, vocab), BF16),
        compiler_params=params(),
        cost_estimate=pl.CostEstimate(
            flops=6 * both * width * vocab,
            bytes_accessed=2 * (2 * vocab + 3 * both) * width + 2 * vocab * both,
            transcendentals=both * vocab,
        ),
    )(
        jnp.reshape(part, (1,)).astype(jnp.int32),
        near_t,
        far_t,
        near_pair.T,
        far_pair.T,
        near_grads,
        far_grads,
        near_pair,
        far_pair,
        scales,
        targets[:, None],
        table_low,
    )


def attend_kernel(queries_ref, kv_ref, bias_ref, out_ref):
    queries = queries_ref[0]
    kv = kv_ref[:, 0].reshape(-1, queries.shape[1])
    scores = dot(queries, kv, ((1,), (1,))) * HEAD_DIM ** (-0.5) + bias_ref[...]
    highest = jnp.max(scores, axis=-1, keepdims=True)
    weights = jnp.exp(scores - highest)
    totals = jnp.sum(weights, axis=-1, keepdims=True)
    output = dot((weights / totals).astype(BF16), kv)
    lanes = lax.broadcasted_iota(jnp.int32, output.shape, 1)
    out_ref[0] = jnp.where(lanes < HEAD_DIM, highest + jnp.log(totals), output)


def attend_back_kernel(queries_ref, kv_ref, bias_ref, out_ref, grads_ref, grad_rows_ref, grad_kv_ref):
    queries, output, grads = queries_ref[0], out_ref[0], grads_ref[0]
    kv = kv_ref[:, 0].reshape(-1, queries.shape[1])
    scale = HEAD_DIM ** (-0.5)
    scores = dot(queries, kv, ((1,), (1,))) * scale + bias_ref[...]
    chances = jnp.exp(scores - output[:, :1])
    delta = jnp.sum(grads.astype(F32) * output, axis=-1, keepdims=True)
    grad_scores = (chances * (dot(grads, kv, ((1,), (1,))) - delta)).astype(BF16)
    grad_rows_ref[0] = dot(grad_scores, kv) * scale
    grad_kv = dot(grad_scores, queries, ((0,), (0,))) * scale
    grad_kv = grad_kv + dot(chances.astype(BF16), grads, ((0,), (0,)))
    grad_kv_ref[:, 0] = grad_kv.astype(BF16).reshape(grad_kv_ref[:, 0].shape)


def attend_specs(queries, kv):
    heads, rows, lanes = queries.shape
    blocks, _, block, _ = kv.shape
    return (
        pl.BlockSpec((1, rows, lanes), lambda h: (h, 0, 0)),
        pl.BlockSpec((blocks, 1, block, lanes), lambda h: (0, h, 0, 0)),
        whole((1, blocks * block)),
        pl.CostEstimate(
            flops=4 * heads * rows * blocks * block * lanes,
            bytes_accessed=4 * heads * blocks * block * lanes,
            transcendentals=heads * rows * blocks * block,
        ),
    )


def attend(queries, kv, bias):
    rows, pairs, one, _ = attend_specs(queries, kv)
    return pl.pallas_call(
        attend_kernel,
        grid=(queries.shape[0],),
        in_specs=[rows, pairs, one],
        out_specs=rows,
        out_shape=jax.ShapeDtypeStruct(queries.shape, F32),
        compiler_params=params(),
        cost_estimate=pl.CostEstimate(flops=0, bytes_accessed=0, transcendentals=0),
    )(queries, kv, bias)


def attend_back(queries, kv, bias, output, grads):
    rows, pairs, one, cost = attend_specs(queries, kv)
    return pl.pallas_call(
        attend_back_kernel,
        grid=(queries.shape[0],),
        in_specs=[rows, pairs, one, rows, rows],
        out_specs=[rows, pairs],
        out_shape=[
            jax.ShapeDtypeStruct(queries.shape, F32),
            jax.ShapeDtypeStruct(kv.shape, BF16),
        ],
        compiler_params=params(),
        cost_estimate=cost,
    )(queries, kv, bias, output, grads)


def place_kernel(
    starts_ref,
    ranks_ref,
    ids_ref,
    *refs,
    chunk,
    block,
):
    rows_refs = refs[:-6]
    kept_ref, received_ref, out_ref, square_ref, sorted_rows, total = refs[-6:]
    step = pl.program_id(0)
    tile = out_ref.shape[1]
    lanes = rows_refs[0].shape[0]

    @pl.when(step == 0)
    def _():
        def sort(k, carry):
            columns = pl.ds(pl.multiple_of(k * block, block), block)
            wanted = lax.broadcasted_iota(jnp.int32, (1, block), 1) + k * block
            found = None
            for source, rows_ref in enumerate(rows_refs):
                pick = ranks_ref[source * lanes : (source + 1) * lanes, :] == wanted
                pick = jnp.where(pick, 1.0, 0.0).astype(BF16)
                part = dot(rows_ref[...], pick, ((0,), (0,)))[: sorted_rows.shape[0]]
                found = part if found is None else found + part
            sorted_rows[:, columns] = found.astype(BF16)
            return carry

        lax.fori_loop(0, (starts_ref[pl.num_programs(0)] + block - 1) // block, sort, 0)

    first = starts_ref[step]
    last = starts_ref[step + 1]
    total[...] = kept_ref[...].astype(F32) + received_ref[...].astype(F32)
    columns = lax.broadcasted_iota(jnp.int32, (1, tile), 1) + step * tile

    def add(k, carry):
        rows = pl.ds(pl.multiple_of(k * chunk, chunk), chunk)
        place = lax.broadcasted_iota(jnp.int32, (chunk, 1), 0) + k * chunk
        ids = ids_ref[rows, :]
        inside = jnp.logical_and(place >= first, place < last)
        pick = jnp.where(jnp.logical_and(ids == columns, inside), 1.0, 0.0).astype(BF16)
        total[...] += dot(sorted_rows[:, rows], pick)
        return carry

    lax.fori_loop(first // chunk, (last + chunk - 1) // chunk, add, 0)
    low = total[...].astype(BF16)
    out_ref[...] = low
    value = low.astype(F32)
    squares = jnp.sum(value * value, axis=0, keepdims=True)
    part = jnp.zeros((1, 128), F32)
    for start in range(0, tile, 128):
        part += squares[:, start : start + 128]

    @pl.when(step == 0)
    def _():
        square_ref[...] = part

    @pl.when(step > 0)
    def _():
        square_ref[...] += part


def place_rows(kept, received, rows, ranks, ids, starts, tile, chunk=128, block=256):
    width, columns = kept.shape
    lanes, padded = rows[0].shape
    total = len(rows) * lanes
    block = min(block, total)
    spec = pl.BlockSpec((width, tile), lambda i, starts: (0, i))
    return pl.pallas_call(
        functools.partial(place_kernel, chunk=chunk, block=block),
        grid_spec=pltpu.PrefetchScalarGridSpec(
            num_scalar_prefetch=1,
            grid=(columns // tile,),
            in_specs=[whole((total, 1)), whole((total, 1))]
            + [whole((lanes, padded))] * len(rows)
            + [spec] * 2,
            out_specs=[spec, whole((1, 128))],
            scratch_shapes=[pltpu.VMEM((width, total), BF16), pltpu.VMEM((width, tile), F32)],
        ),
        out_shape=[
            jax.ShapeDtypeStruct((width, columns), BF16),
            jax.ShapeDtypeStruct((1, 128), F32),
        ],
        compiler_params=params(),
        cost_estimate=pl.CostEstimate(
            flops=2 * 4 * chunk * tile * width,
            bytes_accessed=6 * width * columns + 2 * total * width,
            transcendentals=0,
        ),
    )(starts, ranks[:, None], ids[:, None], *rows, kept, received)


def adam_kernel(quarters_ref, scale_ref, w_ref, m_ref, v_ref, *refs, rate, count):
    grads, outs = refs[:count], refs[-4:]
    part = pl.program_id(0) // (pl.num_programs(0) // count)
    for index, ref in enumerate(grads):

        @pl.when(part == index)
        def _(ref=ref):
            gradient = ref[...].astype(F32) * scale_ref[0]
            new = adam_update(w_ref[...], m_ref[...], v_ref[...], gradient, rate)
            for out, value in zip(outs, new):
                out[...] = value


def adam(master, first, second, grads, quarters, scale, rate, tile, before=()):
    rows, columns = master.shape
    count = len(grads)
    steps = grads[0].shape[1] // tile

    def column(i, quarters):
        return (0, quarters[i // steps] * steps + i % steps)

    def own(index):
        return lambda i, quarters: (0, jnp.clip(i - index * steps, 0, steps - 1))

    spec = pl.BlockSpec((rows, tile), column)
    shape = jax.ShapeDtypeStruct((rows, columns), F32)
    return pl.pallas_call(
        functools.partial(adam_kernel, rate=rate, count=count),
        grid_spec=pltpu.PrefetchScalarGridSpec(
            num_scalar_prefetch=1,
            grid=(count * steps,),
            in_specs=[pl.BlockSpec(memory_space=pltpu.SMEM)]
            + [spec] * 3
            + [pl.BlockSpec((rows, tile), own(index)) for index in range(count)]
            + [pl.BlockSpec(memory_space=pl.ANY)] * len(before),
            out_specs=[spec] * 4,
        ),
        out_shape=[shape] * 3 + [jax.ShapeDtypeStruct((rows, columns), BF16)],
        input_output_aliases={5 + count + k: k for k in range(len(before))},
        compiler_params=params(),
        cost_estimate=pl.CostEstimate(flops=0, bytes_accessed=0, transcendentals=0),
    )(
        jnp.stack(quarters).astype(jnp.int32),
        jnp.reshape(scale, (1,)),
        master,
        first,
        second,
        *grads,
        *before,
    )


def adam_many_kernel(scale_ref, *refs, rates):
    count = len(rates)
    inputs, outputs = refs[: 4 * count], refs[4 * count :]
    scale = scale_ref[0]
    for member, rate in enumerate(rates):
        olds = inputs[4 * member : 4 * member + 4]
        news = outputs[4 * member : 4 * member + 4]
        rows = olds[0].shape[0]
        block = 8 if rows % 8 == 0 else rows

        def update(k, carry, olds=olds, news=news, block=block, rate=rate):
            place = pl.ds(pl.multiple_of(k * block, block), block)
            w, m, v, g = (ref[place, :] for ref in olds)
            for ref, value in zip(news, adam_update(w, m, v, g.astype(F32) * scale, rate)):
                ref[place, :] = value
            return carry

        lax.fori_loop(0, rows // block, update, 0)


def adam_many(olds, scale, rates, steps=5):
    if any(master.shape[0] % (8 * steps) for master, *_ in olds[:-1]):
        steps = 1
    shapes, specs = [], []
    for index, (master, *_) in enumerate(olds):
        rows, columns = master.shape
        shapes += [jax.ShapeDtypeStruct(master.shape, F32)] * 3
        shapes += [jax.ShapeDtypeStruct(master.shape, BF16)]
        if index < len(olds) - 1:
            specs += [pl.BlockSpec((rows // steps, columns), lambda i: (i, 0))] * 4
        else:
            specs += [pl.BlockSpec((rows, columns), lambda i: (0, 0))] * 4
    return pl.pallas_call(
        functools.partial(adam_many_kernel, rates=rates),
        grid=(steps,),
        in_specs=[pl.BlockSpec(memory_space=pltpu.SMEM)] + specs,
        out_specs=specs,
        out_shape=shapes,
        compiler_params=params(),
        cost_estimate=pl.CostEstimate(flops=0, bytes_accessed=0, transcendentals=0),
    )(jnp.reshape(scale, (1,)), *[part for member in olds for part in member])


def place_slowly(kept, received, rows, ids):
    columns = jnp.arange(kept.shape[1], dtype=jnp.int32)

    def add(total, operands):
        part, part_ids = operands
        pick = (part_ids[:, None] == columns[None, :]).astype(BF16)
        return total + dot(part, pick, ((0,), (0,))), None

    total, _ = lax.scan(add, kept.astype(F32) + received.astype(F32), (rows, ids))
    total = total.astype(BF16)
    squares = jnp.sum(jnp.square(total.astype(F32)))
    return total, jnp.full((1, 128), squares / 128)


class Links:
    def __init__(self, n_shard, n_rep):
        self.n = n_shard
        self.wide = n_shard // LINE
        self.n_rep = n_rep
        me = lax.axis_index("shard")
        self.z = me // self.wide
        self.w = me % self.wide
        self.lines = [[z * self.wide + w for z in range(LINE)] for w in range(self.wide)]

    def across(self, value, step):
        pairs = [
            (z * self.wide + w, z * self.wide + (w + step) % self.wide)
            for z in range(LINE)
            for w in range(self.wide)
        ]
        return lax.ppermute(value, "shard", pairs)

    def all_across(self, value):
        return jnp.stack([self.across(value, step) for step in range(1, self.wide)])

    def sum_across(self, near, far):
        rows = near.shape[0]
        total = near.astype(F32)
        for step in range(1, self.wide):
            part = far[(step - 1) * rows : step * rows] if self.wide > 2 else far
            total = total + self.across(part, -step).astype(F32)
        return total

    def line_gather(self, value):
        return lax.all_gather(value, "shard", axis_index_groups=self.lines, tiled=True)

    def line_sum(self, value):
        parts = lax.all_to_all(
            value.astype(BF16), "shard", 0, 0, axis_index_groups=self.lines, tiled=True
        )
        return jnp.sum(parts.astype(F32), axis=0)

    def scatter(self, value):
        value = value.reshape((self.n, -1) + value.shape[1:])
        parts = lax.all_to_all(value, "shard", 0, 0, tiled=True)
        return jnp.sum(parts.astype(F32), axis=0)

    def spread(self, value):
        many = jnp.broadcast_to(value[None], (self.n,) + value.shape)
        return lax.all_to_all(many, "shard", 0, 0, tiled=True)

    def core(self, value):
        return lax.ppermute(value, "rep", [(r, r ^ 1) for r in range(self.n_rep)])

    def rep_gather(self, value):
        value = value[None]
        value = jnp.concatenate([value, self.chip(value)])
        return jnp.concatenate([value, self.core(value)])

    def in_turn(self, value, back=False):
        rep = lax.axis_index("rep")
        places = [rep ^ k for k in (0, 2, 1, 3)]
        if back:
            places = [(rep ^ k) % 2 * 2 + (rep ^ k) // 2 for k in range(4)]
        return [lax.dynamic_index_in_dim(value, place, 0, False) for place in places]

    def rep_scatter(self, value):
        parts = lax.all_to_all(value.astype(BF16), "rep", 0, 0, tiled=True)
        return jnp.sum(parts.astype(F32), axis=0)

    def rep_sum(self, value):
        value = value.astype(BF16)
        mine = value[:2].astype(F32) + self.core(value[2:]).astype(F32)
        return mine[0] + self.chip(mine[1].astype(BF16)).astype(F32)

    def chip(self, value):
        return lax.ppermute(value, "rep", [(r, r ^ 2) for r in range(self.n_rep)])


def build(mesh):
    n_shard = mesh.shape["shard"]
    n_rep = mesh.shape["rep"]

    def local(
        token_ids,
        target_ids,
        loss_mask,
        table_master,
        attn_in_master,
        attn_out_master,
        mlp_in_master,
        mlp_out_master,
        gain_master,
        table_first,
        attn_in_first,
        attn_out_first,
        mlp_in_first,
        mlp_out_first,
        gain_first,
        table_second,
        attn_in_second,
        attn_out_second,
        mlp_in_second,
        mlp_out_second,
        gain_second,
    ):
        links = Links(n_shard, n_rep)
        my_rep = lax.axis_index("rep")
        my_shard = lax.axis_index("shard")
        second_core = (my_rep % 2) == 1
        second_chip = (my_rep // 2) == 1
        tok_rows = token_ids.shape[0]
        seq_len = n_shard * tok_rows
        vocab_rows = table_master.shape[0]
        vocab_start = my_shard * vocab_rows
        wide = n_shard // LINE
        line_rows = LINE * tok_rows

        def in_order(mine, other, axis=-1):
            return jnp.where(
                second_core,
                jnp.concatenate([other, mine], axis),
                jnp.concatenate([mine, other], axis),
            )

        def my_half(value, axis=-1):
            first, second = jnp.split(value, 2, axis)
            return jnp.where(second_core, second, first), jnp.where(second_core, first, second)

        def halves(master):
            return my_half(master[0].astype(BF16))[0]

        in_rows = D // n_shard
        in_cols = attn_in_master.shape[2] // 2
        attn_part = jnp.concatenate([halves(attn_in_master), halves(attn_out_master)], 1)

        packed = jnp.stack([token_ids, target_ids, loss_mask])
        packed, attn_part = lax.optimization_barrier((packed, attn_part))
        everyone = links.spread(lax.all_gather(packed, "rep")).transpose(1, 0, 2, 3)
        everyone = everyone.reshape(LINE, n_rep, wide, 3, tok_rows).transpose(1, 0, 2, 3, 4)
        valid_count = jnp.sum(everyone[:, :, :, 2].astype(F32))
        turn = [(links.w - step) % wide for step in range(wide)]

        def group_of(rep):
            group = lax.dynamic_index_in_dim(everyone, rep, 0, False)
            group = jnp.stack(
                [lax.dynamic_index_in_dim(group, turn[step], 1, False) for step in range(wide)]
            )
            targets = group[:, :, 1].reshape(-1) - vocab_start
            return targets, group[:, :, 2].reshape(-1).astype(F32)

        group_targets, group_mask = group_of(my_rep)
        pair_targets, pair_mask = group_of(my_rep ^ 2)
        group_weights = group_mask / valid_count
        pair_weights = pair_mask / valid_count
        place_block = my_rep * wide + links.w
        positions = place_block * tok_rows + jnp.arange(tok_rows, dtype=jnp.int32)

        unit_rows = FF // n_shard
        unit_part = unit_rows // n_rep
        units = n_shard * unit_part
        mlp_in_part = mlp_in_master[0].astype(BF16)
        mlp_in_part = mlp_in_part.reshape(-1, 2, n_shard, n_rep, unit_part)
        mlp_in_part = lax.dynamic_index_in_dim(mlp_in_part, my_rep, 3, False).reshape(-1, 2 * units)
        mlp_out_part = mlp_out_master[0].astype(BF16).reshape(n_rep, unit_part, D)
        mlp_out_part = lax.dynamic_index_in_dim(mlp_out_part, my_rep, 0, False)
        mlp_part = jnp.concatenate([mlp_in_part, mlp_out_part.reshape(in_rows, -1)], 1)
        attn_mine = lax.all_gather(attn_part, "shard", tiled=True)

        room = min(64, tok_rows)
        vocab_tile = min(512, vocab_rows // 4)
        all_ids = everyone[:, :, :, 0].reshape(n_rep, n_shard, tok_rows)
        earlier = jnp.tril(jnp.ones((tok_rows, tok_rows), BF16), -1)

        def places(inside):
            found = jnp.einsum(
                "...j,ij->...i", inside.astype(BF16), earlier, preferred_element_type=F32
            )
            return jnp.where(inside, found.astype(jnp.int32), -1)

        owners = jnp.arange(n_shard, dtype=jnp.int32)
        owned = (all_ids // vocab_rows)[:, :, None, :] == owners[:, None]
        enough = jnp.max(jnp.sum(owned.astype(jnp.int32), -1)) <= room
        local_ids = all_ids - vocab_start
        inside = (local_ids >= 0) & (local_ids < vocab_rows)
        room_iota = jnp.arange(room, dtype=jnp.int32)
        slots = places(inside)
        slot_ids = jnp.max(
            jnp.where(slots[:, :, None, :] == room_iota[:, None], local_ids[:, :, None, :], -1), -1
        )
        slot_ids = jnp.where(slot_ids < 0, vocab_rows, slot_ids)
        own_ids = lax.dynamic_index_in_dim(
            lax.dynamic_index_in_dim(all_ids, my_rep, 0, False), my_shard, 0, False
        )
        own_slots = places((own_ids // vocab_rows)[None, :] == owners[:, None])
        packing = (own_slots[:, None, :] == room_iota[:, None]).astype(BF16).reshape(-1, tok_rows)

        my_slots = lax.dynamic_index_in_dim(slot_ids, my_rep, 0, False).reshape(-1)
        table_low, looked = lookup(table_master.T, my_slots, min(512, vocab_rows))

        looked, mlp_part = lax.optimization_barrier((looked, mlp_part))
        mlp_all = lax.all_gather(mlp_part, "shard", tiled=True)
        packed = lax.all_to_all(looked.reshape(n_shard, room, D), "shard", 0, 0, tiled=True)
        packed = dot(packing, packed.reshape(-1, D), ((0,), (0,)))

        def read_whole(packed, table_low):
            ids = lax.dynamic_index_in_dim(local_ids, my_rep, 0, False).reshape(-1)
            columns = jnp.arange(vocab_rows, dtype=jnp.int32)
            pick = (ids[:, None] == columns[None, :]).astype(BF16)
            rows = dot(pick, table_low, ((1,), (1,))).astype(BF16)
            rows = lax.all_to_all(rows.reshape(n_shard, tok_rows, D), "shard", 0, 0, tiled=True)
            return jnp.sum(rows.astype(F32), axis=0)

        values = lax.cond(enough, lambda packed, _: packed, read_whole, packed, table_low)
        values, gain_low = lax.optimization_barrier((values, gain_master.astype(BF16)))
        gains = links.spread(gain_low).transpose(1, 0, 2).reshape(3, D).astype(F32)

        rank_ids = jnp.concatenate(
            [lax.dynamic_index_in_dim(slot_ids, my_rep ^ r, 0, False) for r in (0, 2, 1, 3)]
        ).reshape(-1)
        quarter_rows = vocab_rows // n_rep
        quarter_start = my_rep * quarter_rows
        rank_ids = rank_ids - quarter_start
        rank_ids = jnp.where((rank_ids >= 0) & (rank_ids < quarter_rows), rank_ids, quarter_rows)
        slot_iota = jnp.arange(rank_ids.shape[0], dtype=jnp.int32)
        before = (rank_ids[None, :] < rank_ids[:, None]) | (
            (rank_ids[None, :] == rank_ids[:, None]) & (slot_iota[None, :] < slot_iota[:, None])
        )
        ranks = jnp.sum(before.astype(jnp.int32), axis=1)
        sorted_ids = jnp.sort(rank_ids)
        edges = jnp.arange(0, quarter_rows + 1, vocab_tile, dtype=jnp.int32)
        starts = jnp.sum((rank_ids[None, :] < edges[:, None]).astype(jnp.int32), axis=1)
        attn_mine, ranks, sorted_ids, starts, gains = lax.optimization_barrier(
            (attn_mine, ranks, sorted_ids, starts, gains)
        )
        attn_other = links.core(attn_mine)
        attn_in = (attn_mine[:, :in_cols], attn_other[:, :in_cols])
        attn_out = (attn_mine[:, in_cols:], attn_other[:, in_cols:])
        def times(value, pair):
            return dot(value, pair[0]), dot(value, pair[1])

        def times_back(mine, other, pair):
            return dot(mine, pair[0], ((1,), (1,))) + dot(other, pair[1], ((1,), (1,)))

        normed_one, norm_one_back = jax.vjp(rms_norm, values, gains[0])
        normed_one = normed_one.astype(BF16)
        mixed = in_order(*times(normed_one, attn_in))
        heads_raw = mixed[:, : QUERY + KEY].reshape(tok_rows, HEADS + KV_HEADS, HEAD_DIM)
        rotated, rope_back = jax.vjp(lambda part: rotate(part, positions), heads_raw)
        rotated = rotated.astype(BF16)
        group_size = HEADS // KV_HEADS
        queries = rotated[:, :HEADS].reshape(tok_rows, KV_HEADS, group_size, HEAD_DIM)
        queries = queries.transpose(1, 2, 0, 3).reshape(KV_HEADS, group_size * tok_rows, HEAD_DIM)
        queries = jnp.pad(queries, ((0, 0), (0, 0), (0, HEAD_DIM)))
        vals = mixed[:, QUERY + KEY :].astype(BF16).reshape(tok_rows, KV_HEADS, HEAD_DIM)
        kv = jnp.concatenate([rotated[:, HEADS:], vals], 2).transpose(1, 0, 2)
        kv = links.rep_gather(jnp.concatenate([kv[None], links.all_across(kv)]))
        kv = kv.reshape(n_rep * wide, KV_HEADS, tok_rows, 2 * HEAD_DIM)
        key_places = (
            (jnp.stack([my_rep ^ other for other in (0, 2, 1, 3)]) * wide)[:, None, None]
            + ((links.w - jnp.arange(wide, dtype=jnp.int32)) % wide)[None, :, None]
        ) * tok_rows + jnp.arange(tok_rows, dtype=jnp.int32)
        key_blocks = key_places.reshape(-1) // BLOCK
        bias = jnp.where(key_blocks <= positions[0] // BLOCK, 0.0, -1e30).astype(F32)[None]
        outputs = attend(queries, kv, bias)
        outputs, mlp_all = lax.optimization_barrier((outputs, mlp_all))
        mlp_in = mlp_all[:, : 2 * units]
        mlp_out = mlp_all[:, 2 * units :].reshape(n_shard * unit_part, D)

        def to_rows(heads):
            return (
                heads.reshape(KV_HEADS, group_size, tok_rows, HEAD_DIM)
                .transpose(2, 0, 1, 3)
                .reshape(tok_rows, QUERY)
            )

        attended = to_rows(outputs[:, :, HEAD_DIM:].astype(BF16))
        middle = values + in_order(*times(attended, attn_out))
        normed_two, norm_two_back = jax.vjp(rms_norm, middle, gains[1])
        normed_two = normed_two.astype(BF16)
        normed_all = lax.all_gather(normed_two, "rep", tiled=True)
        gate_up = dot(normed_all, mlp_in)
        hidden, glu_back = jax.vjp(swiglu, gate_up[:, :units], gate_up[:, units:])
        hidden = hidden.astype(BF16)
        result = middle + links.rep_scatter(dot(hidden, mlp_out).reshape(n_rep, tok_rows, D))
        final, final_back = jax.vjp(rms_norm, result, gains[2])

        near = links.line_gather(final.astype(BF16))
        far = links.all_across(near).reshape(-1, D)
        near_targets, far_targets = group_targets[:line_rows], group_targets[line_rows:]
        pair_near = links.chip(near)
        pair_far = links.chip(far)
        head_tile = 1024 if vocab_rows % 1024 == 0 else 512
        near_raised, near_highs, near_stats = head_logits(
            near, near_targets, table_low, head_tile
        )
        far, near_stats = lax.optimization_barrier((far, near_stats))
        far_raised, far_highs, far_stats = head_logits(far, far_targets, table_low, head_tile)
        stats = jnp.concatenate([near_stats, far_stats])[:, :3].T
        stats = stats.reshape(3, wide, LINE, tok_rows)
        ordered = jnp.stack(
            [lax.dynamic_index_in_dim(stats, turn[step], 1, False) for step in range(wide)], 1
        )
        stats = links.spread(ordered)
        top = jnp.max(stats[:, 0], axis=0)
        log_totals = top + jnp.log(jnp.sum(stats[:, 1] * jnp.exp(stats[:, 0] - top), axis=0))
        picked = jnp.sum(stats[:, 2], axis=0)
        losses = log_totals - picked

        def turned(part):
            return jnp.stack(
                [lax.dynamic_index_in_dim(part, turn[step], 0, False) for step in range(wide)]
            ).reshape(-1)

        log_totals = turned(log_totals)
        group_loss = jnp.sum(turned(losses) * group_mask)
        pair_logs = links.chip(log_totals)

        def factors(highs, part):
            return jnp.exp(highs - log_totals[part, None]) * group_weights[part, None]

        near_rows, far_rows = slice(0, line_rows), slice(line_rows, None)
        far_grads, far_part = head_states(
            far_raised,
            factors(far_highs, far_rows),
            group_weights[far_rows],
            far_targets,
            table_low,
            head_tile,
        )
        far_sent = far_part
        near_raised, far_part = lax.optimization_barrier((near_raised, far_part))
        near_grads, near_part = head_states(
            near_raised,
            factors(near_highs, near_rows),
            group_weights[near_rows],
            near_targets,
            table_low,
            head_tile,
        )

        table_operands = (
            near.T,
            far.T,
            near_grads,
            far_grads,
            pair_near,
            pair_far,
            jnp.stack([pair_logs, pair_weights], axis=1),
            pair_targets,
            table_low,
        )
        sent = head_table(*table_operands, my_rep ^ 1, vocab_tile)
        received = links.core(sent)
        sent, near_part = lax.optimization_barrier((sent, near_part))
        grad_states = links.sum_across(near_part, far_sent)
        grad_final = links.line_sum(grad_states.reshape(LINE, tok_rows, -1))[:, :D]
        kept = head_table(*table_operands, my_rep, vocab_tile)
        kept, grad_final = lax.optimization_barrier((kept, grad_final))

        grad_output, grad_gain_three = final_back(grad_final)

        def weight_grad(value, mine, other):
            sent = dot(value, other, ((0,), (0,))).astype(BF16)
            half = dot(value, mine, ((0,), (0,))) + links.core(sent).astype(F32)
            first, second = jnp.split(half, 2, 1)
            sent = links.chip(jnp.where(second_chip, first, second).astype(BF16))
            return (jnp.where(second_chip, second, first) + sent.astype(F32)).astype(BF16)

        pad_rows = -in_rows % 16

        def pad_blocks(value):
            value = value.reshape(-1, n_shard, in_rows)
            value = jnp.pad(value, ((0, 0), (0, 0), (0, pad_rows)))
            return value.reshape(-1, n_shard * (in_rows + pad_rows))

        branch = lax.all_gather(grad_output.astype(BF16), "rep", tiled=True)
        grad_mlp_out = dot(hidden, branch, ((0,), (0,))).astype(BF16)
        grad_hidden = dot(branch, mlp_out, ((1,), (1,)))
        grad_glu = jnp.concatenate(glu_back(grad_hidden), 1).astype(BF16)
        grad_mlp_in = dot(pad_blocks(normed_all), grad_glu, ((0,), (0,))).astype(BF16)
        grad_normed_two = dot(grad_glu, mlp_in, ((1,), (1,))).reshape(n_rep, tok_rows, D)
        turns = links.in_turn(grad_normed_two)
        sent = links.core(jnp.stack(turns[2:]).astype(BF16)).astype(F32)
        passed = links.chip((turns[1] + sent[1]).astype(BF16))
        grad_normed_two = turns[0] + sent[0] + passed.astype(F32)
        middle_part, grad_gain_two = norm_two_back(grad_normed_two)
        grad_middle = grad_output + middle_part

        grad_mlp = [grad_mlp_in, grad_mlp_out.reshape(grad_mlp_in.shape[0], -1)]
        grad_mlp = lax.psum_scatter(jnp.concatenate(grad_mlp, 1), "shard", tiled=True)

        out_mine, out_other = my_half(grad_middle.astype(BF16))
        grad_attn_out = weight_grad(pad_blocks(attended), out_mine, out_other)
        grad_attended = times_back(out_mine, out_other, attn_out).astype(BF16)
        grad_heads = (
            grad_attended.reshape(tok_rows, KV_HEADS, group_size, HEAD_DIM)
            .transpose(1, 2, 0, 3)
            .reshape(KV_HEADS, group_size * tok_rows, HEAD_DIM)
        )
        grad_heads = jnp.pad(grad_heads, ((0, 0), (0, 0), (HEAD_DIM, 0)))
        grad_queries, grad_kv = attend_back(queries, kv, bias, outputs, grad_heads)
        grad_kv = grad_kv.reshape(n_rep, wide, KV_HEADS, tok_rows, 2 * HEAD_DIM)
        grad_kv = links.rep_sum(grad_kv)
        far_kv = grad_kv[1:].astype(BF16).reshape(-1, tok_rows, 2 * HEAD_DIM)
        grad_kv = links.sum_across(grad_kv[0], far_kv).transpose(1, 0, 2)
        grad_queries = grad_queries[:, :, :HEAD_DIM]
        grad_rotated = jnp.concatenate(
            [
                to_rows(grad_queries).reshape(tok_rows, HEADS, HEAD_DIM),
                grad_kv[:, :, :HEAD_DIM],
            ],
            1,
        )
        grad_raw = rope_back(grad_rotated)[0].reshape(tok_rows, QUERY + KEY)
        grad_mixed = jnp.concatenate([grad_raw, grad_kv[:, :, HEAD_DIM:].reshape(tok_rows, KEY)], 1).astype(BF16)
        mixed_mine, mixed_other = my_half(grad_mixed)
        values_part, grad_gain_one = norm_one_back(times_back(mixed_mine, mixed_other, attn_in))
        grad_values = (grad_middle + values_part).astype(BF16)
        grad_gains = jnp.stack([grad_gain_one, grad_gain_two, grad_gain_three], 1)
        grad_gains = grad_gains + links.core(grad_gains)
        grad_gains = pad_blocks((grad_gains + links.chip(grad_gains)).T).T
        wide_values = jnp.pad(grad_values, ((0, 0), (0, -D % 128)))
        packed = dot(packing, wide_values).astype(BF16).reshape(n_shard, room, -1)
        packed = lax.all_to_all(packed, "shard", 0, 0, tiled=True)
        grad_attn_in = weight_grad(pad_blocks(normed_one), mixed_mine, mixed_other)
        grad_attn = jnp.concatenate([grad_attn_out, grad_attn_in, grad_gains.astype(BF16)], 1)
        packed, grad_attn = lax.optimization_barrier((packed, grad_attn))
        packed = packed.reshape(n_shard * room, -1)
        across = links.chip(packed)
        grad_attn = grad_attn.reshape((n_shard, -1) + grad_attn.shape[1:])
        grad_attn = lax.all_to_all(grad_attn, "shard", 0, 0, tiled=True)
        across, grad_mlp = lax.optimization_barrier((across, grad_mlp))
        grad_mlp_in = grad_mlp[:in_rows, : 2 * units]
        grad_mlp_out = grad_mlp[:, 2 * units :].reshape(unit_part, D)
        mlp_in_sum = lax.all_gather(grad_mlp_in, "rep")
        rows = (packed, across, links.core(packed), links.core(across))
        rows, mlp_in_sum = lax.optimization_barrier((rows, mlp_in_sum))
        placed = place_rows(kept, received, rows, ranks, sorted_ids, starts, vocab_tile)

        def place_whole(placed, grad_values, kept, received):
            rows = lax.all_gather(lax.all_gather(grad_values, "rep"), "shard")
            ids = local_ids.transpose(1, 0, 2).reshape(-1, tok_rows) - quarter_start
            return place_slowly(kept, received, rows.reshape(-1, tok_rows, D), ids)

        table_sum, table_squares = lax.cond(
            enough, lambda placed, *_: tuple(placed), place_whole, placed, grad_values, kept, received
        )

        table_squares, grad_attn = lax.optimization_barrier((table_squares, grad_attn))
        grad_attn = jnp.sum(grad_attn.astype(F32), axis=0)[:in_rows].astype(BF16)
        gain_sum = grad_attn[:, -3:].astype(F32).T
        grad_attn = grad_attn[:, :-3]
        table_core = links.core(table_sum)
        squares = jnp.sum(table_squares) + jnp.sum(gain_sum * gain_sum) / n_rep
        for part in (grad_mlp_in, grad_mlp_out, grad_attn):
            squares = squares + jnp.sum(jnp.square(part.astype(F32)))
        totals = jnp.stack([squares, group_loss])
        totals = totals + links.core(totals)
        shared = jnp.concatenate([grad_attn, grad_mlp_out.reshape(in_rows, -1)], 1)[None]
        totals, shared = lax.optimization_barrier((totals, shared))
        totals = totals + links.chip(totals)
        mlp_in_sum = mlp_in_sum.reshape(n_rep, in_rows, 2, n_shard, unit_part)
        mlp_in_sum = mlp_in_sum.transpose(1, 2, 3, 0, 4).reshape(in_rows, 2 * FF)
        shared = jnp.concatenate([shared, links.chip(shared)])
        totals, table_sum, shared, mlp_in_sum = lax.optimization_barrier(
            (totals, table_sum, shared, mlp_in_sum)
        )
        table_chip = links.chip(table_sum)
        shared = jnp.concatenate([shared, links.core(shared)])
        shared = jnp.stack(links.in_turn(shared, True))
        loss_sum = totals[1]
        squares = links.spread(jnp.broadcast_to(totals[0], (8, 128)))
        out_cols = D // n_rep
        attn_cols = out_cols + 2 * in_cols // n_rep
        attn = jnp.stack([shared[r, :, :attn_cols] for r in (0, 2, 1, 3)], 1)
        mlp_out_sum = shared[:, :, attn_cols:].reshape(n_rep * unit_part, D)
        attn_out_sum = attn[:, :, :out_cols].reshape(in_rows, D)
        attn_in_sum = attn[:, :, out_cols:].reshape(in_rows, 2 * in_cols)
        squares, attn_in_sum, attn_out_sum, mlp_in_sum, mlp_out_sum = lax.optimization_barrier(
            (squares, attn_in_sum, attn_out_sum, mlp_in_sum, mlp_out_sum)
        )
        grad_norm = jnp.sqrt(jnp.sum(squares[:, 0, 0]))
        clip_scale = CLIP_AT / jnp.maximum(grad_norm, CLIP_AT)
        weight_sum = (attn_in_sum, attn_out_sum, mlp_in_sum, mlp_out_sum, gain_sum)
        results = [loss_sum, valid_count, grad_norm]
        masters = (
            table_master.T,
            attn_in_master,
            attn_out_master,
            mlp_in_master,
            mlp_out_master,
            gain_master,
        )
        firsts = (
            table_first.T,
            attn_in_first,
            attn_out_first,
            mlp_in_first,
            mlp_out_first,
            gain_first,
        )
        seconds = (
            table_second.T,
            attn_in_second,
            attn_out_second,
            mlp_in_second,
            mlp_out_second,
            gain_second,
        )
        rate_list = rates(seq_len)
        table = (masters[0], firsts[0], seconds[0])
        settings = (clip_scale, rate_list[0], vocab_tile)
        new = list(adam(*table, (table_sum, table_core), (my_rep, my_rep ^ 1), *settings))
        olds = [
            tuple(part.reshape(-1, part.shape[-1]) for part in member)
            for member in zip(masters[1:], firsts[1:], seconds[1:], weight_sum)
        ]
        olds[0] = (*olds[0][:3], lax.optimization_barrier((olds[0][3], new[0]))[0])
        news = list(adam_many(olds, clip_scale, rate_list[1:]))
        news[0], table_chip = lax.optimization_barrier((news[0], table_chip))
        table_both = links.core(table_chip)
        new = list(adam(*table, (table_chip,), (my_rep ^ 2,), *settings, new))
        new = adam(*table, (table_both,), (my_rep ^ 3,), *settings, new)
        results.extend(part.T for part in new)
        for index, new in enumerate(news):
            results.append(new.reshape(masters[1 + index // 4].shape))
        return tuple(results)

    return local


def solution(mesh):
    token = P(("rep", "shard"))
    weight = P(None, "shard", None)
    state = (P("shard", None), weight, weight, weight, weight, P(None, "shard"))
    outs = [P(), P(), P()]
    for spec in state:
        outs.extend([spec] * 4)
    return jax.shard_map(
        build(mesh),
        mesh=mesh,
        in_specs=(token, token, token) + state * 3,
        out_specs=tuple(outs),
        check_vma=False,
    )
```
